32 devices in a mesh: batch: 8 (over z, y), chan: 4 (over x, core).
Axes of the slice: x: 2, y: 2, z: 4, core: 2. Of those that a mesh axis runs over, the one named last changes fastest.
Arguments:
- features: bfloat16 [16, 48, 48, 512], P('batch', None, None, 'chan'), may hold values from -54 to 54
- tile_split: int32 [16, 2], P('batch'), may hold values from 2 to 22
- out_grad: bfloat16 [16, 24, 24, 1024], P('batch', None, None, 'chan'), may hold values from -18 to 18
- w_down: bfloat16 [3, 3, 512, 1024], P(None, None, None, 'chan'), may hold values from -0.09375 to 0.09375
- gain_down: float32 [1024], P('chan'), may hold values from 0.1 to 1.9
- shift_down: float32 [1024], P('chan'), may hold values from -3 to 3
- w_split: bfloat16 [2, 1024, 512], P(None, None, 'chan'), may hold values from -0.1875 to 0.1875
- gain_split: float32 [2, 512], P(None, 'chan'), may hold values from 0.1 to 1.9
- shift_split: float32 [2, 512], P(None, 'chan'), may hold values from -3 to 3
- w_first: bfloat16 [2, 512, 512], P(None, None, 'chan'), may hold values from -0.25 to 0.25
- w_second: bfloat16 [2, 3, 3, 512, 512], P(None, None, None, None, 'chan'), may hold values from -0.09375 to 0.09375
- gain_block: float32 [2, 2, 512], P(None, None, 'chan'), may hold values from 0.1 to 1.9
- shift_block: float32 [2, 2, 512], P(None, None, 'chan'), may hold values from -3 to 3
- w_trans: bfloat16 [512, 512], P(None, 'chan'), may hold values from -0.25 to 0.25
- gain_trans: float32 [512], P('chan'), may hold values from 0.1 to 1.9
- shift_trans: float32 [512], P('chan'), may hold values from -3 to 3
- w_merge: bfloat16 [1024, 1024], P(None, 'chan'), may hold values from -0.1875 to 0.1875
- gain_merge: float32 [1024], P('chan'), may hold values from 0.1 to 1.9
- shift_merge: float32 [1024], P('chan'), may hold values from -3 to 3
Outputs:
- mixed: bfloat16 [16, 24, 24, 1024], P('batch', None, None, 'chan')
- features_grad: float32 [16, 48, 48, 512], P('batch', None, None, 'chan')
- w_down_grad: float32 [3, 3, 512, 1024], P(None, None, None, 'chan')
- gain_down_grad: float32 [1024], P('chan')
- shift_down_grad: float32 [1024], P('chan')
- w_split_grad: float32 [2, 1024, 512], P(None, None, 'chan')
- gain_split_grad: float32 [2, 512], P(None, 'chan')
- shift_split_grad: float32 [2, 512], P(None, 'chan')
- w_first_grad: float32 [2, 512, 512], P(None, None, 'chan')
- w_second_grad: float32 [2, 3, 3, 512, 512], P(None, None, None, None, 'chan')
- gain_block_grad: float32 [2, 2, 512], P(None, None, 'chan')
- shift_block_grad: float32 [2, 2, 512], P(None, None, 'chan')
- w_trans_grad: float32 [512, 512], P(None, 'chan')
- gain_trans_grad: float32 [512], P('chan')
- shift_trans_grad: float32 [512], P('chan')
- w_merge_grad: float32 [1024, 1024], P(None, 'chan')
- gain_merge_grad: float32 [1024], P('chan')
- shift_merge_grad: float32 [1024], P('chan')
The draws below stay inside these ranges and needn't reach their ends.
All inputs are finite; a program needn't handle non-finite values.
Results may differ from the reference program's by a relative error of at most 0.03.
Values may be sent and summed in bfloat16 or wider, within the bound.
A program may use at most 320 MiB of HBM per device.

```python
import math
from functools import partial
import jax
import jax.numpy as jnp
from jax import lax

C_IN = 512
WIDTH = 1024
HALF = 512
BLOCKS = 2
SIDE = 24
SAMPLES = 16


def sample_scales(number, lowest, factor):
    steps = jnp.arange(number, dtype=jnp.float32) / (number - 1)
    return lowest * factor ** steps


def scaled_field(key, shape, channels, chan_low, chan_high, row_low, row_factor):
    first_key, second_key = jax.random.split(key, 2)
    chan_scale = jnp.exp(jax.random.uniform(second_key, (channels,), minval=math.log(chan_low), maxval=math.log(chan_high)))
    base = jax.random.truncated_normal(first_key, -6.0, 6.0, shape)
    row_scale = sample_scales(shape[0], row_low, row_factor)
    return base * row_scale[:, None, None, None] * chan_scale


def draw_features(key, part):
    key = jax.random.fold_in(key, 11)
    field = scaled_field(key, (SAMPLES, 2 * SIDE, 2 * SIDE, C_IN), C_IN, 0.3, 3.0, 0.3, 10.0)
    return field.astype(jnp.bfloat16)


def draw_out_grad(key, part):
    key = jax.random.fold_in(key, 12)
    field = scaled_field(key, (SAMPLES, SIDE, SIDE, WIDTH), WIDTH, 0.5, 2.0, 0.4, 3.0)
    return field.astype(jnp.bfloat16)


def set_ends(entries, stream_key, least, high):
    shape = entries.shape
    index_at = [jax.random.randint(jax.random.fold_in(stream_key, axis), (), 0, shape[axis]) for axis in range(len(shape))]
    entries = entries.at[tuple(index_at)].set(least)
    longest = shape.index(max(shape))
    index_at[longest] = (index_at[longest] + 1) % shape[longest]
    return entries.at[tuple(index_at)].set(high)


def block_levels(stream_key, dims, cuts, low, high):
    loudness = 1.0
    for dim, parts in cuts:
        steps = jax.random.uniform(jax.random.fold_in(jax.random.fold_in(stream_key, 6), dim), (parts,), jnp.float32, low / len(cuts), high / len(cuts))
        loudness = loudness * jnp.repeat(jnp.exp(steps), dims[dim] // parts).reshape((-1,) + (1,) * (len(dims) - 1 - dim))
    return loudness


def centred(rng, extent, scale, limit, cuts=(), held_as=jnp.bfloat16):
    values = jax.random.normal(rng, extent, jnp.float32) * scale
    if len(cuts) > 0:
        values = block_levels(rng, extent, cuts, -0.22, 0.18) * values
    return jnp.clip(values, min=-limit, max=limit).astype(held_as)


def setup_inputs(seed: int = 0) -> dict:
    seeds = jax.random.split(jax.random.key(seed), 20)
    features = draw_features(jax.random.fold_in(seeds[19], 71), 0)
    tile_split = set_ends(jax.random.randint(seeds[1], (SAMPLES, 2), 2, SIDE - 1), jax.random.fold_in(seeds[1], 1), 2, (SIDE - 1) - 1).astype(jnp.int32)
    out_grad = draw_out_grad(jax.random.fold_in(seeds[19], 71), 0)
    w_down = centred(seeds[3], (3, 3, C_IN, WIDTH), (9 * C_IN) ** -0.5, 0.09375, ((3, 4),))
    gain_down = jnp.clip(1.0 + 0.18 * jax.random.normal(seeds[4], (WIDTH,), jnp.float32), 0.1, 1.9)
    shift_down = centred(seeds[5], (WIDTH,), 0.5, 3.0, ((0, 4),), jnp.float32)
    w_split = centred(seeds[6], (2, WIDTH, HALF), WIDTH ** -0.5, 0.1875, ((2, 4),))
    gain_split = jnp.clip(1.0 + 0.18 * jax.random.normal(seeds[7], (2, HALF), jnp.float32), 0.1, 1.9)
    shift_split = centred(seeds[8], (2, HALF), 0.5, 3.0, ((1, 4),), jnp.float32)
    w_first = centred(seeds[9], (BLOCKS, HALF, HALF), HALF ** -0.5, 0.25, ((2, 4),))
    w_second = centred(seeds[10], (BLOCKS, 3, 3, HALF, HALF), (9 * HALF) ** -0.5, 0.09375, ((4, 4),))
    gain_block = jnp.clip(1.0 + 0.18 * jax.random.normal(seeds[11], (BLOCKS, 2, HALF), jnp.float32), 0.1, 1.9)
    shift_block = centred(seeds[12], (BLOCKS, 2, HALF), 0.5, 3.0, ((2, 4),), jnp.float32)
    w_trans = centred(seeds[13], (HALF, HALF), HALF ** -0.5, 0.25, ((1, 4),))
    gain_trans = jnp.clip(1.0 + 0.18 * jax.random.normal(seeds[14], (HALF,), jnp.float32), 0.1, 1.9)
    shift_trans = centred(seeds[15], (HALF,), 0.5, 3.0, ((0, 4),), jnp.float32)
    w_merge = centred(seeds[16], (WIDTH, WIDTH), WIDTH ** -0.5, 0.1875, ((1, 4),))
    gain_merge = jnp.clip(1.0 + 0.18 * jax.random.normal(seeds[17], (WIDTH,), jnp.float32), 0.1, 1.9)
    shift_merge = centred(seeds[18], (WIDTH,), 0.5, 3.0, ((0, 4),), jnp.float32)
    return dict(features=features, tile_split=tile_split, out_grad=out_grad, w_down=w_down, gain_down=gain_down, shift_down=shift_down, w_split=w_split, gain_split=gain_split, shift_split=shift_split, w_first=w_first, w_second=w_second, gain_block=gain_block, shift_block=shift_block, w_trans=w_trans, gain_trans=gain_trans, shift_trans=shift_trans, w_merge=w_merge, gain_merge=gain_merge, shift_merge=shift_merge)


epsilon = 1e-05

@jax.custom_vjp
def low(v):
    return lax.optimization_barrier(v.astype(jnp.bfloat16)).astype(jnp.float32)

@jax.custom_vjp
def low_back(v):
    return v

def low_keep(v):
    return (low(v), None)

def low_pass(kept, grad):
    return (grad,)

def back_keep(v):
    return (v, None)

def back_low(kept, grad):
    return (low(grad),)
low.defvjp(low_keep, low_pass)
low_back.defvjp(back_keep, back_low)

def mish_act(values):
    return values * jnp.tanh(jax.nn.softplus(values))

def tap_masks(splits, side_len, stride):
    places = jnp.arange(side_len, dtype=jnp.int32)
    offset = jnp.arange(3, dtype=jnp.int32) - 1
    source = stride * places[:, None] + offset[None, :]
    inside = (source >= 0) & (source < stride * side_len)

    def along_axis(cut_at):
        cut_at = cut_at[:, None, None]
        same_tile = (source[None] < stride * cut_at) == (places[None, :, None] < cut_at)
        return (inside[None] & same_tile).astype(jnp.float32)
    return (along_axis(splits[:, 0]), along_axis(splits[:, 1]))

def tap_sum(tensor, weight, mask_pair, stride):
    rows_ok, cols_ok = mask_pair
    number, height, breadth, channels = tensor.shape
    out_h = height // stride
    out_w = breadth // stride
    padded = jnp.pad(tensor, ((0, 0), (1, 1), (1, 1), (0, 0)))
    summed = jnp.zeros((number, out_h, out_w, weight.shape[3]), jnp.float32)
    for row_tap in range(3):
        for col_tap in range(3):
            window = lax.slice(padded, (0, row_tap, col_tap, 0), (number, row_tap + stride * (out_h - 1) + 1, col_tap + stride * (out_w - 1) + 1, channels), (1, stride, stride, 1))
            kept_mask = rows_ok[:, :, row_tap][:, :, None, None] * cols_ok[:, :, col_tap][:, None, :, None]
            summed = summed + jnp.einsum('nhwc,cd->nhwd', window * kept_mask, weight[row_tap, col_tap], precision=lax.Precision.HIGHEST)
    return summed

def conv_three(tensor, weight, mask_pair, stride):
    return jax.checkpoint(partial(tap_sum, stride=stride))(tensor, weight, mask_pair)

def conv_one(tensor, weight):
    return jnp.einsum('nhwc,cd->nhwd', tensor, weight, precision=lax.Precision.HIGHEST)

def norm_act(conv_out, gain_vec, shift_vec):
    conv_out = low_back(conv_out)
    mean_val = lax.optimization_barrier(jnp.mean(conv_out, axis=(0, 1, 2)))
    centered = conv_out - mean_val
    variance = lax.optimization_barrier(jnp.mean(centered * centered, axis=(0, 1, 2)))
    return mish_act(centered * lax.rsqrt(variance + epsilon) * gain_vec + shift_vec)

def reference(features, tile_split, out_grad, w_down, gain_down, shift_down, w_split, gain_split, shift_split, w_first, w_second, gain_block, shift_block, w_trans, gain_trans, shift_trans, w_merge, gain_merge, shift_merge):
    mask_down = tap_masks(tile_split, SIDE, 2)
    mask_one = tap_masks(tile_split, SIDE, 1)

    def forward(params):
        tensor, down_w, down_g, down_s, split_w, split_g, split_s, first_w, second_w, block_g, block_s, trans_w, trans_g, trans_s, merge_w, merge_g, merge_s = params
        down_act = norm_act(conv_three(tensor, down_w, mask_down, 2), down_g, down_s)
        down_low = low(down_act)
        branch = norm_act(conv_one(down_low, split_w[0]), split_g[0], split_s[0])
        bypass = norm_act(conv_one(down_low, split_w[1]), split_g[1], split_s[1])
        for layer in range(BLOCKS):
            inner = norm_act(conv_one(low(branch), first_w[layer]), block_g[layer, 0], block_s[layer, 0])
            branch = branch + norm_act(conv_three(low(inner), second_w[layer], mask_one, 1), block_g[layer, 1], block_s[layer, 1])
        top_act = norm_act(conv_one(low(branch), trans_w), trans_g, trans_s)
        joined = jnp.concatenate([low(top_act), low(bypass)], axis=-1)
        return norm_act(conv_one(joined, merge_w), merge_g, merge_s)
    params = (features.astype(jnp.float32), w_down.astype(jnp.float32), gain_down.astype(jnp.float32), shift_down.astype(jnp.float32), w_split.astype(jnp.float32), gain_split.astype(jnp.float32), shift_split.astype(jnp.float32), w_first.astype(jnp.float32), w_second.astype(jnp.float32), gain_block.astype(jnp.float32), shift_block.astype(jnp.float32), w_trans.astype(jnp.float32), gain_trans.astype(jnp.float32), shift_trans.astype(jnp.float32), w_merge.astype(jnp.float32), gain_merge.astype(jnp.float32), shift_merge.astype(jnp.float32))
    mixed, pullback = jax.vjp(forward, params)
    grads, = pullback(out_grad.astype(jnp.float32))
    g_feat, g_wd, g_gd, g_sd, g_ws, g_gs, g_ss, g_wf, g_wsec, g_gb, g_sb, g_wt, g_gt, g_st, g_wu, g_gu, g_su = grads
    return (mixed.astype(jnp.bfloat16), g_feat, g_wd, g_gd, g_sd, g_ws, g_gs, g_ss, g_wf, g_wsec, g_gb, g_sb, g_wt, g_gt, g_st, g_wu, g_gu, g_su)
```

```python
import functools

import jax
import jax.numpy as jnp
from jax import lax
from jax.experimental import pallas as pl
from jax.experimental.pallas import tpu as pltpu
from jax.sharding import PartitionSpec as P

epsilon = 1e-05
F32 = jnp.float32
BF16 = jnp.bfloat16
MESH = pl.DeviceIdType.MESH
LANES = 128
VMEM_LIMIT = 60 * 1024 * 1024


def tap_masks(splits, side_len, stride):
    places = jnp.arange(side_len, dtype=jnp.int32)
    offset = jnp.arange(3, dtype=jnp.int32) - 1
    source = stride * places[:, None] + offset[None, :]
    inside = (source >= 0) & (source < stride * side_len)

    def along_axis(cut_at):
        cut_at = cut_at[:, None, None]
        same_tile = (source[None] < stride * cut_at) == (places[None, :, None] < cut_at)
        return (inside[None] & same_tile).astype(jnp.float32)

    return (along_axis(splits[:, 0]), along_axis(splits[:, 1]))


def mask_columns(tile_split, side_len):
    number = tile_split.shape[0]
    rows_two, cols_two = tap_masks(tile_split, side_len, 2)
    rows_one, cols_one = tap_masks(tile_split, side_len, 1)

    def by_row(flags):
        return jnp.broadcast_to(flags[:, :, None], (number, side_len, side_len)).reshape(-1)

    def by_col(flags):
        return jnp.broadcast_to(flags[:, None, :], (number, side_len, side_len)).reshape(-1)

    stacked = jnp.stack(
        [
            by_row(rows_two[:, :, 0]),
            by_col(cols_two[:, :, 0]),
            by_row(rows_one[:, :, 0]),
            by_row(rows_one[:, :, 2]),
            by_col(cols_one[:, :, 0]),
            by_col(cols_one[:, :, 2]),
        ],
        axis=1,
    )
    return jnp.pad(stacked, ((side_len, side_len), (0, 2)))


class Places:
    def __init__(self, batch_count):
        self.count = batch_count
        self.chan = lax.axis_index("chan")
        self.batch = lax.axis_index("batch")
        self.mate = self.chan + 1 - 2 * lax.rem(self.chan, 2)
        self.cross = lax.rem(self.chan + 2, 4)
        self.far = lax.rem(self.mate + 2, 4)
        self.pair = self.chan // 2

    def greet(self):
        barrier = pltpu.get_barrier_semaphore()
        for partner in (self.mate, self.cross):
            pl.semaphore_signal(
                barrier, inc=1, device_id={"chan": partner}, device_id_type=MESH
            )

        def hail(step, carry):
            peer = lax.rem(self.batch + step, self.count)
            pl.semaphore_signal(barrier, inc=1, device_id={"batch": peer}, device_id_type=MESH)
            return carry

        lax.fori_loop(1, self.count, hail, 0)
        pl.semaphore_wait(barrier, 2 + self.count - 1)


class Gather:
    def __init__(self, places, view, chunks, send, recv, base):
        self.at, self.view, self.chunks = places, view, chunks
        self.send, self.recv, self.base = send, recv, base

    def copy(self, owner, chunk, kind, partner):
        ref = self.view(owner, chunk)
        slot = self.base + 3 * chunk + kind
        return pltpu.make_async_remote_copy(
            src_ref=ref,
            dst_ref=ref,
            send_sem=self.send.at[slot],
            recv_sem=self.recv.at[slot],
            device_id={"chan": partner},
            device_id_type=MESH,
        )

    def start(self, chunk):
        self.copy(self.at.chan, chunk, 1, self.at.cross).start()
        self.copy(self.at.chan, chunk, 0, self.at.mate).start()

    def wait_mate(self, chunk):
        self.copy(self.at.mate, chunk, 0, self.at.mate).wait_recv()

    def forward(self, chunk):
        self.copy(self.at.cross, chunk, 1, self.at.cross).wait_recv()
        self.copy(self.at.cross, chunk, 2, self.at.mate).start()

    def wait_far(self, chunk):
        self.copy(self.at.far, chunk, 2, self.at.mate).wait_recv()

    def drain(self):
        for chunk in range(self.chunks):
            self.copy(self.at.chan, chunk, 0, self.at.mate).wait_send()
            self.copy(self.at.chan, chunk, 1, self.at.cross).wait_send()
            self.copy(self.at.cross, chunk, 2, self.at.mate).wait_send()


class Exchange:
    def __init__(self, places, slots, send, recv):
        self.at, self.slots, self.send, self.recv = places, slots, send, recv

    def copy(self, step, owner, peer):
        ref = self.slots.at[owner]
        return pltpu.make_async_remote_copy(
            src_ref=ref,
            dst_ref=ref,
            send_sem=self.send.at[step],
            recv_sem=self.recv.at[step],
            device_id={"batch": peer},
            device_id_type=MESH,
        )

    def run(self, block):
        at = self.at
        self.slots[at.batch] = block

        def push(step, carry):
            self.copy(step, at.batch, lax.rem(at.batch + step, at.count)).start()
            return carry

        def take(step, carry):
            owner = lax.rem(at.batch + at.count - step, at.count)
            self.copy(step, owner, owner).wait_recv()
            return carry

        lax.fori_loop(1, at.count, push, 0)
        lax.fori_loop(1, at.count, take, 0)

    def drain(self):
        at = self.at

        def sent(step, carry):
            self.copy(step, at.batch, lax.rem(at.batch + step, at.count)).wait_send()
            return carry

        lax.fori_loop(1, at.count, sent, 0)


def two_rows(first, second):
    return jnp.where(
        lax.broadcasted_iota(jnp.int32, (8, first.shape[1]), 0) == 0, first, second
    )


def fold(values):
    return jnp.sum(values.reshape(values.shape[0] // 8, 8, values.shape[1]), axis=0)


def tiles(total, size, body):
    def step(index, carry):
        body(pl.multiple_of(index * size, size))
        return carry

    lax.fori_loop(0, total // size, step, 0)


def mish_parts(before):
    grown = jnp.exp(jnp.minimum(before, 20.0))
    top = grown * (grown + 2.0)
    return grown, top


def join(halves):
    return jnp.concatenate(halves, axis=1)


class Norms:
    def __init__(self, exchange, rows, pixels):
        self.exchange, self.rows, self.pixels = exchange, rows, pixels

    def statistics(self, z_ref):
        rows, width = self.rows, z_ref.shape[1]
        size = 96

        def add_up(index, total):
            return total + fold(z_ref[pl.ds(pl.multiple_of(index * size, size), size), :])

        zero = jnp.zeros((8, width), F32)
        total = lax.fori_loop(0, rows // size, add_up, zero)
        mean = jnp.sum(total, axis=0, keepdims=True) / rows

        def spread(index, total):
            away = z_ref[pl.ds(pl.multiple_of(index * size, size), size), :] - mean
            return total + fold(away * away)

        total = lax.fori_loop(0, rows // size, spread, zero)
        square = jnp.sum(total, axis=0, keepdims=True)
        self.exchange.run(two_rows(mean, square))
        slots, count = self.exchange.slots, self.exchange.at.count

        def means(index, total):
            return total + slots[index]

        whole = lax.fori_loop(0, count, means, zero)[0:1] / count

        def squares(index, total):
            block = slots[index]
            away = block[0:1] - whole
            return total + block[1:2] + rows * (away * away)

        variance = lax.fori_loop(0, count, squares, jnp.zeros((1, width), F32)) / self.pixels
        return whole, lax.rsqrt(variance + epsilon)


def forward_kernel(
    batch_count,
    side,
    feat,
    flags,
    wd_in,
    ws_in,
    wf_in,
    w2_in,
    wt_in,
    wm_in,
    gain_d,
    shift_d,
    gain_s,
    shift_s,
    gain_b,
    shift_b,
    gain_t,
    shift_t,
    gain_m,
    shift_m,
    mixed,
    feat_out,
    down_out,
    half_out,
    join_out,
    wide_out,
    slim_out,
    inv_wide,
    inv_slim,
    wd,
    ws,
    wf,
    w2,
    wt,
    wm,
    raw,
    fbuf,
    dbuf,
    hbuf,
    jbuf,
    hat_wide,
    hat_slim,
    acc_wide,
    acc_slim,
    z_wide,
    z_slim,
    branch,
    slots_wide,
    slots_slim,
    wide_sem,
    slim_sem,
    wide_rsem,
    slim_rsem,
    send,
    recv,
    wsem,
    osem,
):
    at = Places(batch_count)
    me = at.chan
    rows = z_wide.shape[0]
    half_rows = rows // 2
    pixels = rows * batch_count
    area = side * side

    weight_copies = {}

    def bring(name, pairs):
        copies = []
        for source, target in pairs:
            slot = sum(len(done) for done in weight_copies.values()) + len(copies)
            copies.append(pltpu.make_async_copy(source, target, wsem.at[slot]))
        weight_copies[name] = copies
        for copy in copies:
            copy.start()

    def have(name):
        for copy in weight_copies[name]:
            copy.wait()

    bring("down", [(wd_in.at[tap], wd.at[tap]) for tap in range(9)])
    bring("split", [(ws_in.at[part], ws.at[:, pl.ds(LANES * part, LANES)]) for part in range(2)])
    for layer in range(2):
        bring(f"first{layer}", [(wf_in.at[layer], wf.at[layer])])
        bring(
            f"second{layer}",
            [
                (w2_in.at[layer, tap], w2.at[layer, :, pl.ds(LANES * tap, LANES)])
                for tap in range(9)
            ],
        )
    bring("trans", [(wt_in, wt)])
    bring("merge", [(wm_in, wm)])

    saved = []

    def save(source, target):
        copy = pltpu.make_async_copy(source, target, osem.at[len(saved)])
        copy.start()
        saved.append(copy)

    base = [0]

    def gather(view, chunks):
        made = Gather(at, view, chunks, send, recv, base[0])
        base[0] += 3 * chunks
        return made

    def by_half(ref):
        return lambda owner, chunk: ref.at[owner, pl.ds(chunk * half_rows, half_rows)]

    feat_go = gather(lambda owner, phase: fbuf.at[owner, phase], 4)
    down_go = gather(by_half(dbuf), 2)
    half_go = [gather(by_half(hbuf.at[index]), 2) for index in range(5)]
    side_go = gather(by_half(jbuf.at[1]), 2)
    top_go = gather(by_half(jbuf.at[0]), 2)
    wide_ex = [
        Exchange(at, slots_wide.at[index], wide_sem.at[index], wide_rsem.at[index])
        for index in range(3)
    ]
    slim_ex = [
        Exchange(at, slots_slim.at[index], slim_sem.at[index], slim_rsem.at[index])
        for index in range(5)
    ]

    at.greet()

    for phase in range(4):
        row_par, col_par = phase // 2, phase % 2

        if col_par == 0:

            def widen(index, carry):
                raw[index] = feat[2 * index + row_par].astype(F32)
                return carry

            lax.fori_loop(0, feat.shape[0] // 2, widen, 0)

        def pick(start):
            both = [
                raw[2 * (start // (2 * side)) + step, pl.ds(col_par, side, stride=2), :]
                for step in range(2)
            ]
            fbuf[me, phase, pl.ds(start, 2 * side), :] = jnp.concatenate(both, axis=0).astype(BF16)

        tiles(rows, 2 * side, pick)
        feat_go.start(phase)

    acc_wide[...] = jnp.zeros_like(acc_wide)
    have("down")

    def down_pair(phase, pair):
        row_par, col_par = phase // 2, phase % 2
        row_taps = (0, 2) if row_par else (1,)
        col_taps = (0, 2) if col_par else (1,)
        size = 192

        def body(start):
            block = join(
                [fbuf[2 * pair + step, phase, pl.ds(start, size), :] for step in range(2)]
            )
            for row_tap in row_taps:
                for col_tap in col_taps:
                    part = jnp.dot(
                        block,
                        wd[3 * row_tap + col_tap, pl.ds(pl.multiple_of(pair * 256, 256), 256), :],
                        preferred_element_type=F32,
                    )
                    place = pl.ds(start + (2 * side if row_tap == 0 else side), size)
                    if row_tap == 0:
                        part = part * flags[place, 0:1]
                    kind = 1 if col_tap == 0 else 0
                    acc_wide[kind, place, :] += part

        tiles(rows, size, body)

    for phase in range(4):
        feat_go.wait_mate(phase)
        down_pair(phase, at.pair)
        feat_go.forward(phase)
    for phase in range(4):
        feat_go.wait_far(phase)
        down_pair(phase, 1 - at.pair)
    save(fbuf, feat_out)

    vsize = 4 * side

    def settle_down(start):
        place = pl.ds(start + side, vsize)
        z_wide[pl.ds(start, vsize), :] = acc_wide[0, place, :] + flags[place, 1:2] * pltpu.roll(
            acc_wide[1, place, :], 1, 0
        )

    tiles(rows, vsize, settle_down)

    def activate(exchange, z_ref, hat_ref, gain, shift, inv_ref, give, begin):
        mean, inverse = Norms(exchange, rows, pixels).statistics(z_ref)
        inv_ref[...] = jnp.broadcast_to(inverse, inv_ref.shape)

        def body(start):
            place = pl.ds(start, vsize)
            normed = (z_ref[place, :] - mean) * inverse
            hat_ref[place, :] = normed
            before = normed * gain + shift
            _, top = mish_parts(before)
            give(place, before * (top / (top + 2.0)))

        for chunk in range(2):

            def inner(start):
                body(start + chunk * half_rows)

            tiles(half_rows, vsize, inner)
            begin(chunk)

    def keep_down(place, value):
        dbuf[me, place, :] = value.astype(BF16)

    activate(
        wide_ex[0], z_wide, hat_wide.at[0], gain_d[...], shift_d[...], inv_wide.at[0], keep_down,
        down_go.start,
    )
    save(hat_wide.at[0], wide_out.at[0])
    have("split")

    msize = 192

    def split_block(owner, chunk, first):
        def body(start):
            place = pl.ds(start + chunk * half_rows, msize)
            part = jnp.dot(
                dbuf[owner, place, :],
                ws[pl.ds(pl.multiple_of(owner * 256, 256), 256), :],
                preferred_element_type=F32,
            )
            if first:
                z_wide[place, :] = part
            else:
                z_wide[place, :] += part

        tiles(half_rows, msize, body)

    for chunk in range(2):
        split_block(me, chunk, True)
    for chunk in range(2):
        down_go.wait_mate(chunk)
        split_block(at.mate, chunk, False)
    for chunk in range(2):
        down_go.forward(chunk)
        split_block(at.cross, chunk, False)
    for chunk in range(2):
        down_go.wait_far(chunk)
        split_block(at.far, chunk, False)
    save(dbuf, down_out)

    def keep_split(place, value):
        branch[place, :] = value[:, :LANES]
        hbuf[0, me, place, :] = value[:, :LANES].astype(BF16)
        jbuf[1, me, place, :] = value[:, LANES:].astype(BF16)

    activate(
        wide_ex[1],
        z_wide,
        hat_wide.at[1],
        join([gain_s[0:1, :], gain_s[1:2, :]]),
        join([shift_s[0:1, :], shift_s[1:2, :]]),
        inv_wide.at[1],
        keep_split,
        half_go[0].start,
    )
    save(hat_wide.at[1], wide_out.at[1])
    for chunk in range(2):
        side_go.start(chunk)

    def two_of(ref, pair, place):
        return join([ref[2 * pair + step, place, :] for step in range(2)])

    def thin_pair(source, weight, pair, chunk, first):
        def body(start):
            place = pl.ds(start + chunk * half_rows, msize)
            part = jnp.dot(
                two_of(source, pair, place),
                weight[pl.ds(pl.multiple_of(pair * 256, 256), 256), :],
                preferred_element_type=F32,
            )
            if first:
                z_slim[place, :] = part
            else:
                z_slim[place, :] += part

        tiles(half_rows, msize, body)

    def thin_conv(index, weight):
        source, go = hbuf.at[index], half_go[index]
        for chunk in range(2):
            go.wait_mate(chunk)
            thin_pair(source, weight, at.pair, chunk, True)
        for chunk in range(2):
            go.forward(chunk)
        for chunk in range(2):
            go.wait_far(chunk)
            thin_pair(source, weight, 1 - at.pair, chunk, False)
        save(source, half_out.at[index])

    def tap_pair(source, weight, pair, chunk):
        def body(start):
            begin = start + chunk * half_rows
            part = jnp.dot(
                two_of(source, pair, pl.ds(begin, msize)),
                weight[pl.ds(pl.multiple_of(pair * 256, 256), 256), :],
                preferred_element_type=F32,
            )
            for col_tap in range(3):
                for row_tap in range(3):
                    tap = 3 * row_tap + col_tap
                    piece = part[:, LANES * tap : LANES * (tap + 1)]
                    place = pl.ds(begin + side - side * (row_tap - 1), msize)
                    if row_tap != 1:
                        column = 2 if row_tap == 0 else 3
                        piece = piece * flags[place, column : column + 1]
                    acc_slim[col_tap, place, :] += piece

        tiles(half_rows, msize, body)

    def tap_conv(index, weight):
        source, go = hbuf.at[index], half_go[index]
        acc_slim[...] = jnp.zeros_like(acc_slim)
        for chunk in range(2):
            go.wait_mate(chunk)
            tap_pair(source, weight, at.pair, chunk)
        for chunk in range(2):
            go.forward(chunk)
        for chunk in range(2):
            go.wait_far(chunk)
            tap_pair(source, weight, 1 - at.pair, chunk)
        save(source, half_out.at[index])

        def settle(start):
            place = pl.ds(start + side, vsize)
            z_slim[pl.ds(start, vsize), :] = (
                acc_slim[1, place, :]
                + flags[place, 4:5] * pltpu.roll(acc_slim[0, place, :], 1, 0)
                + flags[place, 5:6] * pltpu.roll(acc_slim[2, place, :], vsize - 1, 0)
            )

        tiles(rows, vsize, settle)

    def slim_act(index, gain, shift, give, begin):
        activate(
            slim_ex[index], z_slim, hat_slim.at[index], gain, shift, inv_slim.at[index], give, begin
        )
        save(hat_slim.at[index], slim_out.at[index])

    for layer in range(2):
        have(f"first{layer}")
        thin_conv(2 * layer, wf.at[layer])

        def keep_inner(place, value):
            hbuf[2 * layer + 1, me, place, :] = value.astype(BF16)

        slim_act(
            2 * layer,
            gain_b[2 * layer : 2 * layer + 1, :],
            shift_b[2 * layer : 2 * layer + 1, :],
            keep_inner,
            half_go[2 * layer + 1].start,
        )
        have(f"second{layer}")
        tap_conv(2 * layer + 1, w2.at[layer])

        def keep_branch(place, value):
            total = branch[place, :] + value
            branch[place, :] = total
            hbuf[2 * layer + 2, me, place, :] = total.astype(BF16)

        slim_act(
            2 * layer + 1,
            gain_b[2 * layer + 1 : 2 * layer + 2, :],
            shift_b[2 * layer + 1 : 2 * layer + 2, :],
            keep_branch,
            half_go[2 * layer + 2].start,
        )
        if layer == 0:
            for chunk in range(2):
                side_go.forward(chunk)
    have("trans")
    thin_conv(4, wt)

    def keep_top(place, value):
        jbuf[0, me, place, :] = value.astype(BF16)

    slim_act(4, gain_t[...], shift_t[...], keep_top, top_go.start)
    have("merge")

    def merge_pair(part_index, pair, chunk, first):
        def body(start):
            place = pl.ds(start + chunk * half_rows, msize)
            part = jnp.dot(
                two_of(jbuf.at[part_index], pair, place),
                wm[pl.ds(pl.multiple_of(part_index * 512 + pair * 256, 256), 256), :],
                preferred_element_type=F32,
            )
            if first:
                z_wide[place, :] = part
            else:
                z_wide[place, :] += part

        tiles(half_rows, msize, body)

    for chunk in range(2):
        side_go.wait_mate(chunk)
        merge_pair(1, at.pair, chunk, True)
    for chunk in range(2):
        side_go.wait_far(chunk)
        merge_pair(1, 1 - at.pair, chunk, False)
    for chunk in range(2):
        top_go.wait_mate(chunk)
        merge_pair(0, at.pair, chunk, False)
    for chunk in range(2):
        top_go.forward(chunk)
    for chunk in range(2):
        top_go.wait_far(chunk)
        merge_pair(0, 1 - at.pair, chunk, False)
    save(jbuf, join_out)

    def keep_mixed(place, value):
        mixed[place, :] = value.astype(BF16)

    activate(
        wide_ex[2], z_wide, hat_wide.at[2], gain_m[...], shift_m[...], inv_wide.at[2], keep_mixed,
        lambda chunk: None,
    )
    save(hat_wide.at[2], wide_out.at[2])

    for made in (feat_go, down_go, *half_go, side_go, top_go):
        made.drain()
    for made in (*wide_ex, *slim_ex):
        made.drain()
    for copy in saved:
        copy.wait()


def forward_call(batch_count, side, feat, flags, weights, vectors):
    rows = feat.shape[0] * feat.shape[1] // 4 // 1 * 1 if feat.ndim == 2 else None
    rows = feat.shape[0] * side // 2
    wide = 2 * LANES
    hbm = pl.BlockSpec(memory_space=pl.ANY)
    vmem = pl.BlockSpec(memory_space=pltpu.VMEM)
    dma = pltpu.SemaphoreType.DMA
    shape = jax.ShapeDtypeStruct
    kept = [
        shape((4, 4, rows, LANES), BF16),
        shape((4, rows, wide), BF16),
        shape((5, 4, rows, LANES), BF16),
        shape((2, 4, rows, LANES), BF16),
        shape((3, rows, wide), F32),
        shape((5, rows, LANES), F32),
    ]
    taps_width = 9 * LANES
    scratch = [
        pltpu.VMEM((9, 512, wide), BF16),
        pltpu.VMEM((1024, wide), BF16),
        pltpu.VMEM((2, 512, LANES), BF16),
        pltpu.VMEM((2, 512, taps_width), BF16),
        pltpu.VMEM((512, LANES), BF16),
        pltpu.VMEM((1024, wide), BF16),
        pltpu.VMEM((feat.shape[0] // 2, feat.shape[1], LANES), F32),
        *[pltpu.VMEM(one.shape, one.dtype) for one in kept],
        pltpu.VMEM((2, rows + 2 * side, wide), F32),
        pltpu.VMEM((3, rows + 2 * side, LANES), F32),
        pltpu.VMEM((rows, wide), F32),
        pltpu.VMEM((rows, LANES), F32),
        pltpu.VMEM((rows, LANES), F32),
        pltpu.VMEM((3, batch_count, 8, wide), F32),
        pltpu.VMEM((5, batch_count, 8, LANES), F32),
        dma((3, batch_count)),
        dma((5, batch_count)),
        dma((3, batch_count)),
        dma((5, batch_count)),
        dma((60,)),
        dma((60,)),
        dma((40,)),
        dma((20,)),
    ]
    return pl.pallas_call(
        functools.partial(forward_kernel, batch_count, side),
        out_shape=[
            shape((rows, wide), BF16),
            *kept,
            shape((3, 8, wide), F32),
            shape((5, 8, LANES), F32),
        ],
        in_specs=[vmem, vmem] + [hbm] * 6 + [vmem] * 10,
        out_specs=[vmem] + [hbm] * 6 + [vmem, vmem],
        scratch_shapes=scratch,
        compiler_params=pltpu.CompilerParams(
            collective_id=0, has_side_effects=True, vmem_limit_bytes=VMEM_LIMIT
        ),
    )(feat, flags, *weights, *vectors)


def make_taps(tensor, mask_pair, stride):
    rows_ok, cols_ok = mask_pair
    number, height, breadth, channels = tensor.shape
    out_h = height // stride
    out_w = breadth // stride
    padded = jnp.pad(tensor, ((0, 0), (1, 1), (1, 1), (0, 0)))
    tap_list = []
    for row_tap in range(3):
        for col_tap in range(3):
            window = lax.slice(
                padded,
                (0, row_tap, col_tap, 0),
                (
                    number,
                    row_tap + stride * (out_h - 1) + 1,
                    col_tap + stride * (out_w - 1) + 1,
                    channels,
                ),
                (1, stride, stride, 1),
            )
            kept_mask = (
                rows_ok[:, :, row_tap][:, :, None, None] * cols_ok[:, :, col_tap][:, None, :, None]
            ).astype(tensor.dtype)
            tap_list.append((window * kept_mask).reshape(-1, channels))
    return tap_list


def conv_part(portion, weight_part, mask_pair, stride):
    if weight_part.shape[0] == 1:
        return jnp.dot(
            portion.reshape(-1, portion.shape[3]),
            weight_part[0],
            preferred_element_type=jnp.float32,
        )
    tap_list = make_taps(portion, mask_pair, stride)
    summed = jnp.dot(tap_list[0], weight_part[0], preferred_element_type=jnp.float32)
    for tap_index in range(1, 9):
        summed = summed + jnp.dot(
            tap_list[tap_index], weight_part[tap_index], preferred_element_type=jnp.float32
        )
    return summed


def weight_rows(portion, gradient, mask_pair, stride, tap_count):
    dims = (((0,), (0,)), ((), ()))
    if tap_count == 1:
        flat_rows = portion.reshape(-1, portion.shape[3])
        return lax.dot_general(flat_rows, gradient, dims, preferred_element_type=jnp.float32)[None]
    tap_list = make_taps(portion, mask_pair, stride)
    return jnp.stack(
        [
            lax.dot_general(tap_rows, gradient, dims, preferred_element_type=jnp.float32)
            for tap_rows in tap_list
        ]
    )


def input_partial(gradient, weight, mask_pair, stride, shape):
    number, height, breadth, channels = shape
    dims = (((1,), (1,)), ((), ()))
    if weight.shape[0] == 1:
        return lax.dot_general(
            gradient, weight[0], dims, preferred_element_type=jnp.float32
        ).reshape(shape)
    rows_ok, cols_ok = mask_pair
    out_h = height // stride
    out_w = breadth // stride
    summed = jnp.zeros((number, height + 2, breadth + 2, channels), jnp.float32)
    for row_tap in range(3):
        for col_tap in range(3):
            tap_index = 3 * row_tap + col_tap
            window = lax.dot_general(
                gradient, weight[tap_index], dims, preferred_element_type=jnp.float32
            )
            window = window.reshape(number, out_h, out_w, channels)
            kept_mask = (
                rows_ok[:, :, row_tap][:, :, None, None] * cols_ok[:, :, col_tap][:, None, :, None]
            )
            summed = summed + lax.pad(
                window * kept_mask,
                jnp.float32(0),
                (
                    (0, 0, 0),
                    (row_tap, height + 2 - row_tap - stride * (out_h - 1) - 1, stride - 1),
                    (col_tap, breadth + 2 - col_tap - stride * (out_w - 1) - 1, stride - 1),
                    (0, 0, 0),
                ),
            )
    return summed[:, 1 : height + 1, 1 : breadth + 1, :]


def conv_forward(local_map, weight, mask_pair, stride):
    gathered = lax.all_gather(local_map, "chan", axis=3, tiled=True)
    return (conv_part(gathered, weight, mask_pair, stride), gathered)


def conv_backward(gradient, weight, kept_map, mask_pair, stride):
    number, height, breadth = kept_map.shape[:3]
    tap_count, channels, width_out = weight.shape
    weight_grad = weight_rows(kept_map, gradient, mask_pair, stride, tap_count)
    partial_grad = input_partial(
        gradient, weight, mask_pair, stride, (number, height, breadth, channels)
    )
    return (
        weight_grad,
        lax.psum_scatter(
            partial_grad.astype(jnp.bfloat16), "chan", scatter_dimension=3, tiled=True
        ).astype(jnp.float32),
    )


def norm_backward(upstream, saved, gain_vec, pixels):
    normed, inverse, before = saved
    softer = jnp.tanh(jax.nn.softplus(before))
    slopes = softer + before * (1.0 - softer * softer) * jax.nn.sigmoid(before)
    d_before = upstream * slopes
    shift_grad, gain_grad = lax.psum(
        (jnp.sum(d_before, axis=0), jnp.sum(d_before * normed, axis=0)), "batch"
    )
    d_conv = gain_vec * inverse * (d_before - shift_grad / pixels - normed * gain_grad / pixels)
    return (d_conv.astype(jnp.bfloat16), gain_grad, shift_grad)


def local(
    features,
    tile_split,
    out_grad,
    w_down,
    gain_down,
    shift_down,
    w_split,
    gain_split,
    shift_split,
    w_first,
    w_second,
    gain_block,
    shift_block,
    w_trans,
    gain_trans,
    shift_trans,
    w_merge,
    gain_merge,
    shift_merge,
):
    number = features.shape[0]
    side_len = out_grad.shape[1]
    chan_count = lax.axis_size("chan")
    pixels = float(number * side_len * side_len * lax.axis_size("batch"))
    mask_down = tap_masks(tile_split, side_len, 2)
    mask_one = tap_masks(tile_split, side_len, 1)
    in_chans = w_down.shape[2]
    half_full = w_first.shape[1]
    half_local = w_first.shape[2]
    wide_full = w_split.shape[1]
    merge_local = w_merge.shape[1]
    down_rows = w_down.reshape(9, in_chans, w_down.shape[3])
    split_rows = jnp.transpose(w_split, (1, 0, 2)).reshape(1, wide_full, 2 * half_local)
    merge_rows = jnp.transpose(
        w_merge.reshape(2, chan_count, half_local, merge_local), (1, 0, 2, 3)
    ).reshape(1, wide_full, merge_local)
    trans_rows = w_trans[None]

    def shaped(flat_rows):
        return flat_rows.reshape(number, side_len, side_len, flat_rows.shape[1])

    flags = mask_columns(tile_split, side_len)
    row = lambda vec: vec.reshape(1, -1)
    mixed_rows, _, dbuf, hbuf, jbuf, hat_wide, hat_slim, inv_wide, inv_slim = forward_call(
        lax.axis_size("batch"),
        side_len,
        features.reshape(-1, features.shape[2], features.shape[3]),
        flags,
        (
            down_rows,
            w_split,
            w_first,
            w_second.reshape(2, 9, half_full, half_local),
            w_trans,
            w_merge,
        ),
        (
            row(gain_down),
            row(shift_down),
            gain_split,
            shift_split,
            gain_block.reshape(4, -1),
            shift_block.reshape(4, -1),
            row(gain_trans),
            row(shift_trans),
            row(gain_merge),
            row(shift_merge),
        ),
    )
    mixed = shaped(mixed_rows)

    def kept_norm(hat, inv, gain, shift):
        return (hat, inv, hat * gain + shift)

    def whole(buf):
        return shaped(jnp.transpose(buf, (1, 0, 2)).reshape(buf.shape[1], -1))

    down_kept = lax.all_gather(features, "chan", axis=3, tiled=True)
    down_saved = kept_norm(hat_wide[0], inv_wide[0, 0], gain_down, shift_down)
    split_kept = whole(dbuf)
    split_saved = kept_norm(
        hat_wide[1], inv_wide[1, 0], gain_split.reshape(-1), shift_split.reshape(-1)
    )
    records = []
    for layer in range(2):
        records.append(
            (
                w_first[layer][None],
                w_second[layer].reshape(9, half_full, half_local),
                whole(hbuf[2 * layer]),
                whole(hbuf[2 * layer + 1]),
                kept_norm(
                    hat_slim[2 * layer],
                    inv_slim[2 * layer, 0],
                    gain_block[layer, 0],
                    shift_block[layer, 0],
                ),
                kept_norm(
                    hat_slim[2 * layer + 1],
                    inv_slim[2 * layer + 1, 0],
                    gain_block[layer, 1],
                    shift_block[layer, 1],
                ),
            )
        )
    trans_kept = whole(hbuf[4])
    trans_saved = kept_norm(hat_slim[4], inv_slim[4, 0], gain_trans, shift_trans)
    merge_kept = whole(
        jnp.transpose(jbuf, (1, 2, 0, 3)).reshape(4, jbuf.shape[2], 2 * half_local)
    )
    merge_saved = kept_norm(hat_wide[2], inv_wide[2, 0], gain_merge, shift_merge)
    upstream = out_grad.astype(jnp.float32).reshape(-1, out_grad.shape[3])
    merge_dz, merge_gain_grad, merge_shift_grad = norm_backward(
        upstream, merge_saved, gain_merge, pixels
    )
    merge_wgrad, joined_grad = conv_backward(merge_dz, merge_rows, merge_kept, None, 1)
    joined_grad = joined_grad.reshape(-1, 2 * half_local)
    trans_dz, trans_gain_grad, trans_shift_grad = norm_backward(
        joined_grad[:, :half_local], trans_saved, gain_trans, pixels
    )
    trans_wgrad, branch_grad = conv_backward(trans_dz, trans_rows, trans_kept, None, 1)
    branch_grad = branch_grad.reshape(-1, half_local)
    first_list = []
    second_list = []
    gain_list = []
    shift_list = []
    for layer in reversed(range(len(records))):
        first_rows, second_rows, first_kept, second_kept, first_saved, second_saved = records[layer]
        second_dz, second_gain, second_shift = norm_backward(
            branch_grad, second_saved, gain_block[layer, 1], pixels
        )
        second_wgrad, inner_grad = conv_backward(second_dz, second_rows, second_kept, mask_one, 1)
        first_dz, first_gain, first_shift = norm_backward(
            inner_grad.reshape(-1, half_local), first_saved, gain_block[layer, 0], pixels
        )
        first_wgrad, extra_grad = conv_backward(first_dz, first_rows, first_kept, None, 1)
        branch_grad = branch_grad + extra_grad.reshape(-1, half_local)
        first_list.insert(0, first_wgrad[0])
        second_list.insert(0, second_wgrad.reshape(3, 3, half_full, half_local))
        gain_list.insert(0, jnp.stack([first_gain, second_gain]))
        shift_list.insert(0, jnp.stack([first_shift, second_shift]))
    first_all = jnp.stack(first_list)
    second_all = jnp.stack(second_list)
    block_gain_grad = jnp.stack(gain_list)
    block_shift_grad = jnp.stack(shift_list)
    merge_plain = jnp.transpose(
        merge_wgrad[0].reshape(chan_count, 2, half_local, merge_local), (1, 0, 2, 3)
    ).reshape(wide_full, merge_local)
    trans_plain = trans_wgrad[0]
    split_dz, split_gain, split_shift = norm_backward(
        jnp.concatenate([branch_grad, joined_grad[:, half_local:]], axis=1),
        split_saved,
        gain_split.reshape(-1),
        pixels,
    )
    split_wgrad, down_grad = conv_backward(split_dz, split_rows, split_kept, None, 1)
    down_dz, down_gain, down_shift = norm_backward(
        down_grad.reshape(-1, down_grad.shape[3]), down_saved, gain_down, pixels
    )
    down_wgrad, features_grad = conv_backward(down_dz, down_rows, down_kept, mask_down, 2)
    split_plain = jnp.transpose(split_wgrad[0].reshape(wide_full, 2, half_local), (1, 0, 2))
    down_plain = down_wgrad.reshape(3, 3, in_chans, down_wgrad.shape[2])
    down_plain, split_plain, first_all, second_all, trans_plain, merge_plain = lax.psum(
        (down_plain, split_plain, first_all, second_all, trans_plain, merge_plain), "batch"
    )
    return (
        mixed,
        features_grad,
        down_plain,
        down_gain,
        down_shift,
        split_plain,
        split_gain.reshape(2, half_local),
        split_shift.reshape(2, half_local),
        first_all,
        second_all,
        block_gain_grad,
        block_shift_grad,
        trans_plain,
        trans_gain_grad,
        trans_shift_grad,
        merge_plain,
        merge_gain_grad,
        merge_shift_grad,
    )


def solution(mesh):
    placed = (
        P("batch", None, None, "chan"),
        P("batch", None),
        P("batch", None, None, "chan"),
        P(None, None, None, "chan"),
        P("chan"),
        P("chan"),
        P(None, None, "chan"),
        P(None, "chan"),
        P(None, "chan"),
        P(None, None, "chan"),
        P(None, None, None, None, "chan"),
        P(None, None, "chan"),
        P(None, None, "chan"),
        P(None, "chan"),
        P("chan"),
        P("chan"),
        P(None, "chan"),
        P("chan"),
        P("chan"),
    )
    return jax.shard_map(
        local,
        mesh=mesh,
        in_specs=placed,
        out_specs=(
            P("batch", None, None, "chan"),
            P("batch", None, None, "chan"),
            P(None, None, None, "chan"),
            P("chan"),
            P("chan"),
            P(None, None, "chan"),
            P(None, "chan"),
            P(None, "chan"),
            P(None, None, "chan"),
            P(None, None, None, None, "chan"),
            P(None, None, "chan"),
            P(None, None, "chan"),
            P(None, "chan"),
            P("chan"),
            P("chan"),
            P(None, "chan"),
            P("chan"),
            P("chan"),
        ),
        check_vma=False,
    )
```

```python
import functools

import jax
import jax.numpy as jnp
from jax import lax
from jax.experimental import pallas as pl
from jax.experimental.pallas import tpu as pltpu
from jax.sharding import PartitionSpec as P

epsilon = 1e-05
F32 = jnp.float32
BF16 = jnp.bfloat16
MESH = pl.DeviceIdType.MESH
LANES = 128
VMEM_LIMIT = 60 * 1024 * 1024


def tap_masks(splits, side_len, stride):
    places = jnp.arange(side_len, dtype=jnp.int32)
    offset = jnp.arange(3, dtype=jnp.int32) - 1
    source = stride * places[:, None] + offset[None, :]
    inside = (source >= 0) & (source < stride * side_len)

    def along_axis(cut_at):
        cut_at = cut_at[:, None, None]
        same_tile = (source[None] < stride * cut_at) == (places[None, :, None] < cut_at)
        return (inside[None] & same_tile).astype(jnp.float32)

    return (along_axis(splits[:, 0]), along_axis(splits[:, 1]))


def mask_columns(tile_split, side_len):
    number = tile_split.shape[0]
    rows_two, cols_two = tap_masks(tile_split, side_len, 2)
    rows_one, cols_one = tap_masks(tile_split, side_len, 1)

    def by_row(flags):
        return jnp.broadcast_to(flags[:, :, None], (number, side_len, side_len)).reshape(-1)

    def by_col(flags):
        return jnp.broadcast_to(flags[:, None, :], (number, side_len, side_len)).reshape(-1)

    stacked = jnp.stack(
        [
            by_row(rows_two[:, :, 0]),
            by_col(cols_two[:, :, 0]),
            by_row(rows_one[:, :, 0]),
            by_row(rows_one[:, :, 2]),
            by_col(cols_one[:, :, 0]),
            by_col(cols_one[:, :, 2]),
        ],
        axis=1,
    )
    return jnp.pad(stacked, ((side_len, side_len), (0, 2)))


class Places:
    def __init__(self, batch_count):
        self.count = batch_count
        self.chan = lax.axis_index("chan")
        self.batch = lax.axis_index("batch")
        self.mate = self.chan + 1 - 2 * lax.rem(self.chan, 2)
        self.cross = lax.rem(self.chan + 2, 4)
        self.far = lax.rem(self.mate + 2, 4)
        self.pair = self.chan // 2

    def greet(self):
        barrier = pltpu.get_barrier_semaphore()
        for partner in (self.mate, self.cross):
            pl.semaphore_signal(
                barrier, inc=1, device_id={"chan": partner}, device_id_type=MESH
            )

        def hail(step, carry):
            peer = lax.rem(self.batch + step, self.count)
            pl.semaphore_signal(barrier, inc=1, device_id={"batch": peer}, device_id_type=MESH)
            return carry

        lax.fori_loop(1, self.count, hail, 0)
        pl.semaphore_wait(barrier, 2 + self.count - 1)


class Gather:
    def __init__(self, places, view, chunks, send, recv, base):
        self.at, self.view, self.chunks = places, view, chunks
        self.send, self.recv, self.base = send, recv, base

    def copy(self, owner, chunk, kind, partner):
        ref = self.view(owner, chunk)
        slot = self.base + 3 * chunk + kind
        return pltpu.make_async_remote_copy(
            src_ref=ref,
            dst_ref=ref,
            send_sem=self.send.at[slot],
            recv_sem=self.recv.at[slot],
            device_id={"chan": partner},
            device_id_type=MESH,
        )

    def start(self, chunk):
        self.copy(self.at.chan, chunk, 1, self.at.cross).start()
        self.copy(self.at.chan, chunk, 0, self.at.mate).start()

    def wait_mate(self, chunk):
        self.copy(self.at.mate, chunk, 0, self.at.mate).wait_recv()

    def forward(self, chunk):
        self.copy(self.at.cross, chunk, 1, self.at.cross).wait_recv()
        self.copy(self.at.cross, chunk, 2, self.at.mate).start()

    def wait_far(self, chunk):
        self.copy(self.at.far, chunk, 2, self.at.mate).wait_recv()

    def drain(self):
        for chunk in range(self.chunks):
            self.copy(self.at.chan, chunk, 0, self.at.mate).wait_send()
            self.copy(self.at.chan, chunk, 1, self.at.cross).wait_send()
            self.copy(self.at.cross, chunk, 2, self.at.mate).wait_send()


class Exchange:
    def __init__(self, places, slots, send, recv):
        self.at, self.slots, self.send, self.recv = places, slots, send, recv

    def copy(self, step, owner, peer):
        ref = self.slots.at[owner]
        return pltpu.make_async_remote_copy(
            src_ref=ref,
            dst_ref=ref,
            send_sem=self.send.at[step],
            recv_sem=self.recv.at[step],
            device_id={"batch": peer},
            device_id_type=MESH,
        )

    def push(self, block):
        at = self.at
        self.slots[at.batch] = block

        def start(step, carry):
            self.copy(step, at.batch, lax.rem(at.batch + step, at.count)).start()
            return carry

        lax.fori_loop(1, at.count, start, 0)

    def take(self):
        at = self.at

        def arrive(step, carry):
            owner = lax.rem(at.batch + at.count - step, at.count)
            self.copy(step, owner, owner).wait_recv()
            return carry

        lax.fori_loop(1, at.count, arrive, 0)

    def drain(self):
        at = self.at

        def sent(step, carry):
            self.copy(step, at.batch, lax.rem(at.batch + step, at.count)).wait_send()
            return carry

        lax.fori_loop(1, at.count, sent, 0)


def two_rows(first, second):
    return jnp.where(
        lax.broadcasted_iota(jnp.int32, (8, first.shape[1]), 0) == 0, first, second
    )


def fold(values):
    return jnp.sum(values.reshape(values.shape[0] // 8, 8, values.shape[1]), axis=0)


def tiles(total, size, body):
    def step(index, carry):
        body(pl.multiple_of(index * size, size))
        return carry

    lax.fori_loop(0, total // size, step, 0)


def mish_parts(before):
    grown = jnp.exp(jnp.minimum(before, 20.0))
    top = grown * (grown + 2.0)
    return grown, top


def join(halves):
    return jnp.concatenate(halves, axis=1)


class Norms:
    def __init__(self, exchange, rows, pixels):
        self.exchange, self.rows, self.pixels = exchange, rows, pixels

    def statistics(self, z_ref):
        rows, width = self.rows, z_ref.shape[1]
        size = 96

        def add_up(index, total):
            return total + fold(z_ref[pl.ds(pl.multiple_of(index * size, size), size), :])

        zero = jnp.zeros((8, width), F32)
        total = lax.fori_loop(0, rows // size, add_up, zero)
        mean = jnp.sum(total, axis=0, keepdims=True) / rows

        def spread(index, total):
            away = z_ref[pl.ds(pl.multiple_of(index * size, size), size), :] - mean
            return total + fold(away * away)

        total = lax.fori_loop(0, rows // size, spread, zero)
        square = jnp.sum(total, axis=0, keepdims=True)
        self.exchange.push(two_rows(mean, square))
        self.exchange.take()
        slots, count = self.exchange.slots, self.exchange.at.count

        def means(index, total):
            return total + slots[index]

        whole = lax.fori_loop(0, count, means, zero)[0:1] / count

        def squares(index, total):
            block = slots[index]
            away = block[0:1] - whole
            return total + block[1:2] + rows * (away * away)

        variance = lax.fori_loop(0, count, squares, jnp.zeros((1, width), F32)) / self.pixels
        return whole, lax.rsqrt(variance + epsilon)


def forward_kernel(
    batch_count,
    side,
    feat,
    flags,
    wd_in,
    ws_in,
    wf_in,
    w2_in,
    wt_in,
    wm_in,
    gain_d,
    shift_d,
    gain_s,
    shift_s,
    gain_b,
    shift_b,
    gain_t,
    shift_t,
    gain_m,
    shift_m,
    mixed,
    feat_out,
    down_out,
    half_out,
    join_out,
    wide_out,
    slim_out,
    inv_wide,
    inv_slim,
    wd,
    ws,
    wf,
    w2,
    wt,
    wm,
    raw,
    fbuf,
    dbuf,
    hbuf,
    jbuf,
    hat_wide,
    hat_slim,
    acc_wide,
    acc_slim,
    z_wide,
    z_slim,
    branch,
    slots_wide,
    slots_slim,
    wide_sem,
    slim_sem,
    wide_rsem,
    slim_rsem,
    send,
    recv,
    wsem,
    osem,
):
    at = Places(batch_count)
    me = at.chan
    rows = z_wide.shape[0]
    half_rows = rows // 2
    pixels = rows * batch_count
    area = side * side

    weight_copies = {}

    def bring(name, pairs):
        copies = []
        for source, target in pairs:
            slot = sum(len(done) for done in weight_copies.values()) + len(copies)
            copies.append(pltpu.make_async_copy(source, target, wsem.at[slot]))
        weight_copies[name] = copies
        for copy in copies:
            copy.start()

    def have(name):
        for copy in weight_copies[name]:
            copy.wait()

    bring("down", [(wd_in.at[tap], wd.at[tap]) for tap in range(9)])
    bring("split", [(ws_in.at[part], ws.at[:, pl.ds(LANES * part, LANES)]) for part in range(2)])
    for layer in range(2):
        bring(f"first{layer}", [(wf_in.at[layer], wf.at[layer])])
        bring(
            f"second{layer}",
            [
                (w2_in.at[layer, tap], w2.at[layer, :, pl.ds(LANES * tap, LANES)])
                for tap in range(9)
            ],
        )
    bring("trans", [(wt_in, wt)])
    bring("merge", [(wm_in, wm)])

    saved = []

    def save(source, target):
        copy = pltpu.make_async_copy(source, target, osem.at[len(saved)])
        copy.start()
        saved.append(copy)

    base = [0]

    def gather(view, chunks):
        made = Gather(at, view, chunks, send, recv, base[0])
        base[0] += 3 * chunks
        return made

    def by_half(ref):
        return lambda owner, chunk: ref.at[owner, pl.ds(chunk * half_rows, half_rows)]

    feat_go = gather(lambda owner, phase: fbuf.at[owner, phase], 4)
    down_go = gather(by_half(dbuf), 2)
    half_go = [gather(by_half(hbuf.at[index]), 2) for index in range(5)]
    side_go = gather(by_half(jbuf.at[1]), 2)
    top_go = gather(by_half(jbuf.at[0]), 2)
    wide_ex = [
        Exchange(at, slots_wide.at[index], wide_sem.at[index], wide_rsem.at[index])
        for index in range(3)
    ]
    slim_ex = [
        Exchange(at, slots_slim.at[index], slim_sem.at[index], slim_rsem.at[index])
        for index in range(5)
    ]

    at.greet()

    for phase in range(4):
        row_par, col_par = phase // 2, phase % 2

        if col_par == 0:

            def widen(index, carry):
                raw[index] = feat[2 * index + row_par].astype(F32)
                return carry

            lax.fori_loop(0, feat.shape[0] // 2, widen, 0)

        def pick(start):
            both = [
                raw[2 * (start // (2 * side)) + step, pl.ds(col_par, side, stride=2), :]
                for step in range(2)
            ]
            fbuf[me, phase, pl.ds(start, 2 * side), :] = jnp.concatenate(both, axis=0).astype(BF16)

        tiles(rows, 2 * side, pick)
        feat_go.start(phase)

    acc_wide[...] = jnp.zeros_like(acc_wide)
    have("down")

    def down_pair(phase, pair):
        row_par, col_par = phase // 2, phase % 2
        row_taps = (0, 2) if row_par else (1,)
        col_taps = (0, 2) if col_par else (1,)
        size = 192

        def body(start):
            block = join(
                [fbuf[2 * pair + step, phase, pl.ds(start, size), :] for step in range(2)]
            )
            for row_tap in row_taps:
                for col_tap in col_taps:
                    part = jnp.dot(
                        block,
                        wd[3 * row_tap + col_tap, pl.ds(pl.multiple_of(pair * 256, 256), 256), :],
                        preferred_element_type=F32,
                    )
                    place = pl.ds(start + (2 * side if row_tap == 0 else side), size)
                    if row_tap == 0:
                        part = part * flags[place, 0:1]
                    kind = 1 if col_tap == 0 else 0
                    acc_wide[kind, place, :] += part

        tiles(rows, size, body)

    for phase in range(4):
        feat_go.wait_mate(phase)
        down_pair(phase, at.pair)
        feat_go.forward(phase)
    for phase in range(4):
        feat_go.wait_far(phase)
        down_pair(phase, 1 - at.pair)
    save(fbuf, feat_out)

    vsize = 4 * side

    def settle_down(start):
        place = pl.ds(start + side, vsize)
        z_wide[pl.ds(start, vsize), :] = acc_wide[0, place, :] + flags[place, 1:2] * pltpu.roll(
            acc_wide[1, place, :], 1, 0
        )

    tiles(rows, vsize, settle_down)

    def activate(exchange, z_ref, hat_ref, gain, shift, inv_ref, give, begin):
        mean, inverse = Norms(exchange, rows, pixels).statistics(z_ref)
        inv_ref[...] = jnp.broadcast_to(inverse, inv_ref.shape)

        def body(start):
            place = pl.ds(start, vsize)
            normed = (z_ref[place, :] - mean) * inverse
            hat_ref[place, :] = normed
            before = normed * gain + shift
            _, top = mish_parts(before)
            give(place, before * (top / (top + 2.0)))

        for chunk in range(2):

            def inner(start):
                body(start + chunk * half_rows)

            tiles(half_rows, vsize, inner)
            begin(chunk)

    def keep_down(place, value):
        dbuf[me, place, :] = value.astype(BF16)

    activate(
        wide_ex[0], z_wide, hat_wide.at[0], gain_d[...], shift_d[...], inv_wide.at[0], keep_down,
        down_go.start,
    )
    save(hat_wide.at[0], wide_out.at[0])
    have("split")

    msize = 192

    def split_block(owner, chunk, first):
        def body(start):
            place = pl.ds(start + chunk * half_rows, msize)
            part = jnp.dot(
                dbuf[owner, place, :],
                ws[pl.ds(pl.multiple_of(owner * 256, 256), 256), :],
                preferred_element_type=F32,
            )
            if first:
                z_wide[place, :] = part
            else:
                z_wide[place, :] += part

        tiles(half_rows, msize, body)

    for chunk in range(2):
        split_block(me, chunk, True)
    for chunk in range(2):
        down_go.wait_mate(chunk)
        split_block(at.mate, chunk, False)
    for chunk in range(2):
        down_go.forward(chunk)
        split_block(at.cross, chunk, False)
    for chunk in range(2):
        down_go.wait_far(chunk)
        split_block(at.far, chunk, False)
    save(dbuf, down_out)

    def keep_split(place, value):
        branch[place, :] = value[:, :LANES]
        hbuf[0, me, place, :] = value[:, :LANES].astype(BF16)
        jbuf[1, me, place, :] = value[:, LANES:].astype(BF16)

    activate(
        wide_ex[1],
        z_wide,
        hat_wide.at[1],
        join([gain_s[0:1, :], gain_s[1:2, :]]),
        join([shift_s[0:1, :], shift_s[1:2, :]]),
        inv_wide.at[1],
        keep_split,
        half_go[0].start,
    )
    save(hat_wide.at[1], wide_out.at[1])
    for chunk in range(2):
        side_go.start(chunk)

    def two_of(ref, pair, place):
        return join([ref[2 * pair + step, place, :] for step in range(2)])

    def thin_pair(source, weight, pair, chunk, first):
        def body(start):
            place = pl.ds(start + chunk * half_rows, msize)
            part = jnp.dot(
                two_of(source, pair, place),
                weight[pl.ds(pl.multiple_of(pair * 256, 256), 256), :],
                preferred_element_type=F32,
            )
            if first:
                z_slim[place, :] = part
            else:
                z_slim[place, :] += part

        tiles(half_rows, msize, body)

    def thin_conv(index, weight):
        source, go = hbuf.at[index], half_go[index]
        for chunk in range(2):
            go.wait_mate(chunk)
            thin_pair(source, weight, at.pair, chunk, True)
        for chunk in range(2):
            go.forward(chunk)
        for chunk in range(2):
            go.wait_far(chunk)
            thin_pair(source, weight, 1 - at.pair, chunk, False)
        save(source, half_out.at[index])

    def tap_pair(source, weight, pair, chunk):
        def body(start):
            begin = start + chunk * half_rows
            part = jnp.dot(
                two_of(source, pair, pl.ds(begin, msize)),
                weight[pl.ds(pl.multiple_of(pair * 256, 256), 256), :],
                preferred_element_type=F32,
            )
            for col_tap in range(3):
                for row_tap in range(3):
                    tap = 3 * row_tap + col_tap
                    piece = part[:, LANES * tap : LANES * (tap + 1)]
                    place = pl.ds(begin + side - side * (row_tap - 1), msize)
                    if row_tap != 1:
                        column = 2 if row_tap == 0 else 3
                        piece = piece * flags[place, column : column + 1]
                    acc_slim[col_tap, place, :] += piece

        tiles(half_rows, msize, body)

    def tap_conv(index, weight):
        source, go = hbuf.at[index], half_go[index]
        acc_slim[...] = jnp.zeros_like(acc_slim)
        for chunk in range(2):
            go.wait_mate(chunk)
            tap_pair(source, weight, at.pair, chunk)
        for chunk in range(2):
            go.forward(chunk)
        for chunk in range(2):
            go.wait_far(chunk)
            tap_pair(source, weight, 1 - at.pair, chunk)
        save(source, half_out.at[index])

        def settle(start):
            place = pl.ds(start + side, vsize)
            z_slim[pl.ds(start, vsize), :] = (
                acc_slim[1, place, :]
                + flags[place, 4:5] * pltpu.roll(acc_slim[0, place, :], 1, 0)
                + flags[place, 5:6] * pltpu.roll(acc_slim[2, place, :], vsize - 1, 0)
            )

        tiles(rows, vsize, settle)

    def slim_act(index, gain, shift, give, begin):
        activate(
            slim_ex[index], z_slim, hat_slim.at[index], gain, shift, inv_slim.at[index], give, begin
        )
        save(hat_slim.at[index], slim_out.at[index])

    for layer in range(2):
        have(f"first{layer}")
        thin_conv(2 * layer, wf.at[layer])

        def keep_inner(place, value):
            hbuf[2 * layer + 1, me, place, :] = value.astype(BF16)

        slim_act(
            2 * layer,
            gain_b[2 * layer : 2 * layer + 1, :],
            shift_b[2 * layer : 2 * layer + 1, :],
            keep_inner,
            half_go[2 * layer + 1].start,
        )
        have(f"second{layer}")
        tap_conv(2 * layer + 1, w2.at[layer])

        def keep_branch(place, value):
            total = branch[place, :] + value
            branch[place, :] = total
            hbuf[2 * layer + 2, me, place, :] = total.astype(BF16)

        slim_act(
            2 * layer + 1,
            gain_b[2 * layer + 1 : 2 * layer + 2, :],
            shift_b[2 * layer + 1 : 2 * layer + 2, :],
            keep_branch,
            half_go[2 * layer + 2].start,
        )
        if layer == 0:
            for chunk in range(2):
                side_go.forward(chunk)
    have("trans")
    thin_conv(4, wt)

    def keep_top(place, value):
        jbuf[0, me, place, :] = value.astype(BF16)

    slim_act(4, gain_t[...], shift_t[...], keep_top, top_go.start)
    have("merge")

    def merge_pair(part_index, pair, chunk, first):
        def body(start):
            place = pl.ds(start + chunk * half_rows, msize)
            part = jnp.dot(
                two_of(jbuf.at[part_index], pair, place),
                wm[pl.ds(pl.multiple_of(part_index * 512 + pair * 256, 256), 256), :],
                preferred_element_type=F32,
            )
            if first:
                z_wide[place, :] = part
            else:
                z_wide[place, :] += part

        tiles(half_rows, msize, body)

    for chunk in range(2):
        side_go.wait_mate(chunk)
        merge_pair(1, at.pair, chunk, True)
    for chunk in range(2):
        side_go.wait_far(chunk)
        merge_pair(1, 1 - at.pair, chunk, False)
    for chunk in range(2):
        top_go.wait_mate(chunk)
        merge_pair(0, at.pair, chunk, False)
    for chunk in range(2):
        top_go.forward(chunk)
    for chunk in range(2):
        top_go.wait_far(chunk)
        merge_pair(0, 1 - at.pair, chunk, False)
    save(jbuf, join_out)

    def keep_mixed(place, value):
        mixed[place, :] = value.astype(BF16)

    activate(
        wide_ex[2], z_wide, hat_wide.at[2], gain_m[...], shift_m[...], inv_wide.at[2], keep_mixed,
        lambda chunk: None,
    )
    save(hat_wide.at[2], wide_out.at[2])

    for made in (feat_go, down_go, *half_go, side_go, top_go):
        made.drain()
    for made in (*wide_ex, *slim_ex):
        made.drain()
    for copy in saved:
        copy.wait()


def forward_call(batch_count, side, feat, flags, weights, vectors):
    rows = feat.shape[0] * side // 2
    wide = 2 * LANES
    hbm = pl.BlockSpec(memory_space=pl.ANY)
    vmem = pl.BlockSpec(memory_space=pltpu.VMEM)
    dma = pltpu.SemaphoreType.DMA
    shape = jax.ShapeDtypeStruct
    kept = [
        shape((4, 4, rows, LANES), BF16),
        shape((4, rows, wide), BF16),
        shape((5, 4, rows, LANES), BF16),
        shape((2, 4, rows, LANES), BF16),
        shape((3, rows, wide), F32),
        shape((5, rows, LANES), F32),
    ]
    taps_width = 9 * LANES
    scratch = [
        pltpu.VMEM((9, 512, wide), BF16),
        pltpu.VMEM((1024, wide), BF16),
        pltpu.VMEM((2, 512, LANES), BF16),
        pltpu.VMEM((2, 512, taps_width), BF16),
        pltpu.VMEM((512, LANES), BF16),
        pltpu.VMEM((1024, wide), BF16),
        pltpu.VMEM((feat.shape[0] // 2, feat.shape[1], LANES), F32),
        *[pltpu.VMEM(one.shape, one.dtype) for one in kept],
        pltpu.VMEM((2, rows + 2 * side, wide), F32),
        pltpu.VMEM((3, rows + 2 * side, LANES), F32),
        pltpu.VMEM((rows, wide), F32),
        pltpu.VMEM((rows, LANES), F32),
        pltpu.VMEM((rows, LANES), F32),
        pltpu.VMEM((3, batch_count, 8, wide), F32),
        pltpu.VMEM((5, batch_count, 8, LANES), F32),
        dma((3, batch_count)),
        dma((5, batch_count)),
        dma((3, batch_count)),
        dma((5, batch_count)),
        dma((60,)),
        dma((60,)),
        dma((40,)),
        dma((20,)),
    ]
    return pl.pallas_call(
        functools.partial(forward_kernel, batch_count, side),
        out_shape=[
            shape((rows, wide), BF16),
            *kept,
            shape((3, 8, wide), F32),
            shape((5, 8, LANES), F32),
        ],
        in_specs=[vmem, vmem] + [hbm] * 6 + [vmem] * 10,
        out_specs=[vmem] + [hbm] * 6 + [vmem, vmem],
        scratch_shapes=scratch,
        compiler_params=pltpu.CompilerParams(
            collective_id=0, has_side_effects=True, vmem_limit_bytes=VMEM_LIMIT
        ),
    )(feat, flags, *weights, *vectors)


class Scatter:
    def __init__(self, places, views, send, recv, base):
        self.at = places
        self.term, self.from_mate, self.from_cross, self.across = views
        self.send, self.recv, self.base = send, recv, base
        self.used = []

    def copy(self, source, target, chunk, kind, partner):
        slot = self.base + 3 * chunk + kind
        return pltpu.make_async_remote_copy(
            src_ref=source,
            dst_ref=target,
            send_sem=self.send.at[slot],
            recv_sem=self.recv.at[slot],
            device_id={"chan": partner},
            device_id_type=MESH,
        )

    def far_copy(self, chunk):
        return self.copy(
            self.term(self.at.far, chunk), self.from_mate(0, chunk), chunk, 0, self.at.mate
        )

    def mate_copy(self, chunk):
        return self.copy(
            self.term(self.at.mate, chunk), self.from_mate(1, chunk), chunk, 1, self.at.mate
        )

    def cross_copy(self, chunk):
        return self.copy(self.across(chunk), self.from_cross(chunk), chunk, 2, self.at.cross)

    def relay(self, chunk, size):
        self.far_copy(chunk).wait_recv()
        mine, theirs, both = (
            self.term(self.at.cross, chunk),
            self.from_mate(0, chunk),
            self.across(chunk),
        )

        def add(start):
            place = pl.ds(start, size)
            both[place, :] = (mine[place, :].astype(F32) + theirs[place, :].astype(F32)).astype(
                BF16
            )

        tiles(mine.shape[0], size, add)
        self.cross_copy(chunk).start()

    def finish(self, chunk, size, give):
        self.mate_copy(chunk).wait_recv()
        self.cross_copy(chunk).wait_recv()
        parts = (self.term(self.at.chan, chunk), self.from_mate(1, chunk), self.from_cross(chunk))

        def add(start):
            place = pl.ds(start, size)
            first, second, third = [part[place, :].astype(F32) for part in parts]
            give(start, first + second + third)

        tiles(parts[0].shape[0], size, add)
        self.used.append(chunk)

    def drain(self):
        for chunk in self.used:
            self.far_copy(chunk).wait_send()
            self.mate_copy(chunk).wait_send()
            self.cross_copy(chunk).wait_send()


def tile_of(rows):
    return max(size for size in range(8, 321, 8) if rows % size == 0)


class Reducer:
    def __init__(self, places, buf, landing, out, order, sems, base, own_sem):
        self.at, self.buf, self.landing, self.out = places, buf, landing, out
        self.order, (self.send, self.recv), self.base = order, sems, base
        self.own_sem = own_sem
        self.low, self.size, self.taken, self.step = 0, buf.shape[0], 0, 0

    def partner(self, bit):
        side = lax.rem(self.at.batch // (1 << bit), 2)
        return side, self.at.batch + (1 - 2 * side) * (1 << bit)

    def copy(self, source, target, partner):
        return pltpu.make_async_remote_copy(
            src_ref=source,
            dst_ref=target,
            send_sem=self.send.at[self.base + self.step],
            recv_sem=self.recv.at[self.base + self.step],
            device_id={"batch": partner},
            device_id_type=MESH,
        )

    def rows(self, low, size):
        return pl.ds(pl.multiple_of(low, 8), size)

    def launch(self):
        steps = len(self.order)
        if self.step < steps:
            side, partner = self.partner(self.order[self.step])
            half = self.size // 2
            gone = self.low + (1 - side) * half
            self.flying = self.copy(
                self.buf.at[self.rows(gone, half)],
                self.landing.at[pl.ds(self.taken, half)],
                partner,
            )
            self.kept = self.low + side * half
            self.flying.start()
            return
        side, partner = self.partner(self.order[2 * steps - 1 - self.step])
        target = self.out.at[self.rows(self.low, self.size)]
        source = target
        if self.step == steps:
            source = self.buf.at[self.rows(self.low, self.size)]
            self.own = pltpu.make_async_copy(source, target, self.own_sem)
            self.own.start()
        self.flying = self.copy(source, target, partner)
        self.flying.start()
        other = self.out.at[self.rows(self.low + (1 - 2 * side) * self.size, self.size)]
        self.coming = self.copy(other, other, partner)
        self.next_low = self.low - side * self.size

    def advance(self):
        steps = len(self.order)
        if self.step < steps:
            self.flying.wait()
            half = self.size // 2
            size = tile_of(half)
            taken, kept = self.taken, self.kept

            def add(start):
                place = self.rows(kept + start, size)
                self.buf[place, :] = (
                    self.buf[place, :].astype(F32)
                    + self.landing[pl.ds(taken + start, size), :].astype(F32)
                ).astype(BF16)

            tiles(half, size, add)
            self.low, self.size, self.taken = kept, half, taken + half
        else:
            self.coming.wait_recv()
            self.flying.wait_send()
            if self.step == steps:
                self.own.wait()
            self.low, self.size = self.next_low, 2 * self.size
        self.step += 1
        if self.step == 2 * steps:
            return True
        self.launch()
        return False


def landing_rows(rows, batch_count):
    return rows - rows // batch_count


def backward_kernel(
    batch_count,
    side,
    orders,
    grad_in,
    flags,
    wd_in,
    ws_in,
    wf_in,
    w2_in,
    wt_in,
    wm_in,
    feat_in,
    down_in,
    half_in,
    join_in,
    wide_in,
    slim_in,
    inv_wide,
    inv_slim,
    gain_d,
    shift_d,
    gain_s,
    shift_s,
    gain_b,
    shift_b,
    gain_t,
    shift_t,
    gain_m,
    shift_m,
    feat_grad,
    vec_wide,
    vec_slim,
    merge_out,
    late_out,
    early_out,
    split_out,
    down_out,
    grad,
    wd,
    ws,
    wf,
    w2,
    wt,
    wm,
    fbuf,
    dbuf,
    hbuf,
    jbuf,
    hat_wide,
    hat_slim,
    up_wide,
    up_slim,
    branch,
    bypass,
    shifted,
    spread,
    dz_wide,
    dz_slim,
    pbuf,
    rmate,
    rcross,
    across,
    rcross_d,
    across_d,
    sum_merge,
    sum_late,
    sum_early,
    sum_split,
    sum_down,
    land_merge,
    land_late,
    land_early,
    land_split,
    slots_wide,
    slots_slim,
    wide_sem,
    slim_sem,
    wide_rsem,
    slim_rsem,
    send,
    recv,
    bsend,
    brecv,
    wsem,
    osem,
):
    at = Places(batch_count)
    rows = up_wide.shape[0]
    half_rows = rows // 2
    pixels = rows * batch_count
    vsize = 4 * side
    msize = 192

    fetched = {}
    count = [0]

    def bring(name, *pairs):
        copies = []
        for source, target in pairs:
            copies.append(pltpu.make_async_copy(source, target, wsem.at[count[0]]))
            count[0] += 1
        fetched[name] = copies
        for copy in copies:
            copy.start()

    def have(name):
        for copy in fetched[name]:
            copy.wait()

    bring("grad", (grad_in, grad), (wide_in.at[2], hat_wide.at[2]))
    bring("merge", (wm_in, wm))
    bring("joined", (join_in, jbuf))
    bring("hat4", (slim_in.at[4], hat_slim.at[4]))
    bring("trans", (wt_in, wt))
    bring("half4", (half_in.at[4], hbuf.at[4]))
    for layer in (1, 0):
        index = 2 * layer + 1
        bring(f"hat{index}", (slim_in.at[index], hat_slim.at[index]))
        bring(
            f"second{layer}",
            *[
                (w2_in.at[layer, tap], w2.at[layer, :, pl.ds(LANES * tap, LANES)])
                for tap in range(9)
            ],
        )
        bring(f"half{index}", (half_in.at[index], hbuf.at[index]))
        index = 2 * layer
        bring(f"hat{index}", (slim_in.at[index], hat_slim.at[index]))
        bring(f"first{layer}", (wf_in.at[layer], wf.at[layer]))
        bring(f"half{index}", (half_in.at[index], hbuf.at[index]))
    bring("hat_split", (wide_in.at[1], hat_wide.at[1]))
    bring("split", *[(ws_in.at[part], ws.at[:, pl.ds(LANES * part, LANES)]) for part in range(2)])
    bring("down_low", (down_in, dbuf))
    bring("hat_down", (wide_in.at[0], hat_wide.at[0]))
    bring("features", (feat_in, fbuf))
    bring("down", *[(wd_in.at[tap], wd.at[tap]) for tap in range(9)])

    wide_ex = [
        Exchange(at, slots_wide.at[index], wide_sem.at[index], wide_rsem.at[index])
        for index in range(3)
    ]
    slim_ex = [
        Exchange(at, slots_slim.at[index], slim_sem.at[index], slim_rsem.at[index])
        for index in range(5)
    ]

    base = [0]

    def scatter(stage, parts):
        kit = stage % 2

        def cut(ref):
            return lambda *where: ref.at[(*where[:-1], pl.ds(where[-1] * half_rows, half_rows))]

        def term(owner, chunk):
            return cut(pbuf)(chunk // 2, owner, chunk % 2)

        def from_mate(block, chunk):
            return cut(rmate)(kit, chunk // 2, block, chunk % 2)

        def from_cross(chunk):
            return cut(rcross)(kit, chunk // 2, chunk % 2)

        def over(chunk):
            return cut(across)(chunk // 2, chunk % 2)

        made = Scatter(at, (term, from_mate, from_cross, over), send, recv, base[0])
        base[0] += 6 * parts
        return made

    steps = 2 * len(orders[0])
    bbase = [0]

    queue = []

    def begin(buf, landing, order, out):
        made = Reducer(
            at,
            buf,
            landing,
            out,
            orders[order],
            (bsend, brecv),
            bbase[0],
            osem.at[bbase[0] // steps],
        )
        bbase[0] += steps
        made.launch()
        queue.append(made)

    def tick(most=1):
        for made in list(queue)[:most]:
            if made.advance():
                queue.remove(made)

    at.greet()

    for ref in (shifted,):
        ref[...] = jnp.zeros_like(ref)

    def norm_back(exchange, load, back, hat, gain, shift, inverse, vec_ref, give, meanwhile):
        width = back.shape[1]

        def first(index, carry):
            place = pl.ds(pl.multiple_of(index * vsize, vsize), vsize)
            normed = hat[place, :]
            before = normed * gain + shift
            grown, top = mish_parts(before)
            share = 1.0 / (top + 2.0)
            slope = top * share + before * (4.0 * grown * (1.0 + grown) * share * share)
            value = load(place) * slope
            back[place, :] = value
            return (carry[0] + fold(value), carry[1] + fold(value * normed))

        zero = jnp.zeros((8, width), F32)
        one, two = lax.fori_loop(0, rows // vsize, first, (zero, zero))
        exchange.push(
            two_rows(jnp.sum(one, axis=0, keepdims=True), jnp.sum(two, axis=0, keepdims=True))
        )
        meanwhile()
        exchange.take()
        slots = exchange.slots

        def gather_up(index, total):
            return total + slots[index]

        total = lax.fori_loop(0, batch_count, gather_up, zero)
        vec_ref[...] = total
        scale = gain * inverse
        shift_part, gain_part = total[0:1] / pixels, total[1:2] / pixels

        def second(start):
            place = pl.ds(start, vsize)
            give(start, scale * (back[place, :] - shift_part - hat[place, :] * gain_part))

        tiles(rows, vsize, second)

    across_dims = (((1,), (1,)), ((), ()))
    along_dims = (((0,), (0,)), ((), ()))

    def back_pair(left, weight, pair, chunk, part):
        def body(start):
            begin_at = start + chunk * half_rows
            terms = lax.dot_general(
                left(pl.ds(begin_at, msize)), weight, across_dims, preferred_element_type=F32
            ).astype(BF16)
            for step in range(2):
                pbuf[part, 2 * pair + step, pl.ds(begin_at, msize), :] = terms[
                    :, LANES * step : LANES * (step + 1)
                ]

        tiles(half_rows, msize, body)

    def pair_rows(pair, offset=0):
        return pl.ds(pl.multiple_of(offset + pair * 256, 256), 256)

    def spread_out(go, left, weight_at, parts):
        chunks = 2 * parts
        for chunk in range(chunks):
            back_pair(left, weight_at(chunk // 2, 1 - at.pair), 1 - at.pair, chunk % 2, chunk // 2)
            go.far_copy(chunk).start()
        for chunk in range(chunks):
            go.relay(chunk, vsize)
        for chunk in range(chunks):
            back_pair(left, weight_at(chunk // 2, at.pair), at.pair, chunk % 2, chunk // 2)
            go.mate_copy(chunk).start()

    def two_of(ref, pair):
        return join([ref[2 * pair + step] for step in range(2)])

    have("grad")
    merge_go = scatter(0, 2)

    def keep_wide(start, value):
        dz_wide[pl.ds(start, vsize), :] = value.astype(BF16)

    norm_back(
        wide_ex[2],
        lambda place: grad[place, :].astype(F32),
        up_wide,
        hat_wide.at[2],
        gain_m[...],
        shift_m[...],
        inv_wide[2, 0:1, :],
        vec_wide.at[2],
        keep_wide,
        lambda: None,
    )
    have("merge")
    spread_out(
        merge_go,
        lambda place: dz_wide[place, :],
        lambda part, pair: wm[pair_rows(pair, 512 * part), :],
        2,
    )
    have("joined")
    for part in range(2):
        for pair in range(2):
            sum_merge[pl.ds(512 * part + 256 * pair, 256), :] = lax.dot_general(
                two_of(jbuf.at[part], pair), dz_wide[...], along_dims, preferred_element_type=F32
            ).astype(BF16)
    begin(sum_merge, land_merge, 0, merge_out)

    def top_up(chunk):
        def give(start, value):
            up_slim[pl.ds(start + chunk * half_rows, vsize), :] = value

        return give

    for chunk in range(2):
        merge_go.finish(chunk, vsize, top_up(chunk))

    def keep_slim(start, value):
        dz_slim[pl.ds(start, vsize), :] = value.astype(BF16)

    def slim_back(index, load, gain, shift, give):
        have(f"hat{index}")
        norm_back(
            slim_ex[index],
            load,
            up_slim,
            hat_slim.at[index],
            gain,
            shift,
            inv_slim[index, 0:1, :],
            vec_slim.at[index],
            give,
            tick,
        )

    def thin_back(stage, index, weight, name, target, offset, settle, extra=None):
        go = scatter(stage, 1)
        have(name)
        spread_out(
            go,
            lambda place: dz_slim[place, :],
            lambda part, pair: weight[pair_rows(pair), :],
            1,
        )
        have(f"half{index}")
        for pair in range(2):
            target[pl.ds(offset + 256 * pair, 256), :] = lax.dot_general(
                two_of(hbuf.at[index], pair), dz_slim[...], along_dims, preferred_element_type=F32
            ).astype(BF16)
        if extra is not None:
            extra()
        tick()
        for chunk in range(2):
            go.finish(chunk, vsize, settle(chunk))
        return go

    slim_back(4, lambda place: up_slim[place, :], gain_t[...], shift_t[...], keep_slim)

    def branch_new(chunk):
        def give(start, value):
            branch[pl.ds(start + chunk * half_rows, vsize), :] = value

        return give

    def branch_more(chunk):
        def give(start, value):
            branch[pl.ds(start + chunk * half_rows, vsize), :] += value

        return give

    def bypass_up(chunk):
        def give(start, value):
            bypass[pl.ds(start + chunk * half_rows, vsize), :] = value

        return give

    def finish_bypass():
        for chunk in range(2):
            merge_go.finish(2 + chunk, vsize, bypass_up(chunk))
        merge_go.drain()

    finish_bypass()
    thin_back(1, 4, wt, "trans", sum_late, 4608, branch_new).drain()

    def nine(start, value):
        place = pl.ds(start + side, vsize)
        value = value.astype(BF16).astype(F32)
        shifted[1, place, :] = value
        shifted[0, place, :] = pltpu.roll(value * flags[place, 4:5], vsize - 1, 0)
        shifted[2, place, :] = pltpu.roll(value * flags[place, 5:6], 1, 0)

    def nine_rows(start):
        for row_tap in range(3):
            source = pl.ds(start + side - side * (row_tap - 1), vsize)
            for col_tap in range(3):
                tap = 3 * row_tap + col_tap
                value = shifted[col_tap, source, :]
                if row_tap != 1:
                    column = 2 if row_tap == 0 else 3
                    value = value * flags[source, column : column + 1]
                spread[pl.ds(start, vsize), LANES * tap : LANES * (tap + 1)] = value.astype(BF16)

    def tap_back(stage, layer, target, settle, extra):
        index = 2 * layer + 1
        go = scatter(stage, 1)
        tiles(rows, vsize, nine_rows)
        have(f"second{layer}")
        spread_out(
            go,
            lambda place: spread[place, :],
            lambda part, pair: w2[layer, pair_rows(pair), :],
            1,
        )
        have(f"half{index}")
        for pair in range(2):
            left = two_of(hbuf.at[index], pair)
            for row_tap in range(3):
                three = lax.dot_general(
                    left,
                    spread[:, 3 * LANES * row_tap : 3 * LANES * (row_tap + 1)],
                    along_dims,
                    preferred_element_type=F32,
                ).astype(BF16)
                for col_tap in range(3):
                    target[pl.ds(512 * (3 * row_tap + col_tap) + 256 * pair, 256), :] = three[
                        :, LANES * col_tap : LANES * (col_tap + 1)
                    ]
        extra()
        tick()
        for chunk in range(2):
            go.finish(chunk, vsize, settle(chunk))
        go.drain()

    for layer in (1, 0):
        stage = 2 if layer == 1 else 4
        target = sum_late if layer == 1 else sum_early
        slim_back(
            2 * layer + 1,
            lambda place: branch[place, :],
            gain_b[2 * layer + 1 : 2 * layer + 2, :],
            shift_b[2 * layer + 1 : 2 * layer + 2, :],
            nine,
        )
        if layer == 1:
            extra = lambda: begin(sum_late, land_late, 1, late_out)
        else:
            extra = lambda: begin(sum_early, land_early, 1, early_out)
        tap_back(stage, layer, target, top_up, extra)
        slim_back(
            2 * layer,
            lambda place: up_slim[place, :],
            gain_b[2 * layer : 2 * layer + 1, :],
            shift_b[2 * layer : 2 * layer + 1, :],
            keep_slim,
        )
        thin_back(
            stage + 1,
            2 * layer,
            wf.at[layer],
            f"first{layer}",
            sum_early if layer == 1 else sum_split,
            4608 if layer == 1 else 2048,
            branch_more,
        ).drain()

    have("hat_split")
    norm_back(
        wide_ex[1],
        lambda place: join([branch[place, :], bypass[place, :]]),
        up_wide,
        hat_wide.at[1],
        join([gain_s[0:1, :], gain_s[1:2, :]]),
        join([shift_s[0:1, :], shift_s[1:2, :]]),
        inv_wide[1, 0:1, :],
        vec_wide.at[1],
        keep_wide,
        tick,
    )
    have("split")
    split_go = scatter(6, 2)

    def split_terms(owner, chunk):
        def body(start):
            place = pl.ds(start + chunk * half_rows, msize)
            terms = lax.dot_general(
                dz_wide[place, :],
                ws[pl.ds(pl.multiple_of(owner * 256, 256), 256), :],
                across_dims,
                preferred_element_type=F32,
            ).astype(BF16)
            for part in range(2):
                pbuf[part, owner, place, :] = terms[:, LANES * part : LANES * (part + 1)]

        tiles(half_rows, msize, body)

    for chunk in range(2):
        split_terms(at.far, chunk)
        for part in range(2):
            split_go.far_copy(2 * part + chunk).start()
    for chunk in range(2):
        split_terms(at.cross, chunk)
        for part in range(2):
            split_go.relay(2 * part + chunk, vsize)
    for chunk in range(2):
        split_terms(at.mate, chunk)
        for part in range(2):
            split_go.mate_copy(2 * part + chunk).start()
    for chunk in range(2):
        split_terms(at.chan, chunk)
    have("down_low")
    for owner in range(4):
        result = lax.dot_general(
            dbuf[rows * owner : rows * (owner + 1), :], dz_wide[...], along_dims, preferred_element_type=F32
        ).astype(BF16)
        for part in range(2):
            sum_split[pl.ds(1024 * part + 256 * owner, 256), :] = result[
                :, LANES * part : LANES * (part + 1)
            ]
    begin(sum_split, land_split, 0, split_out)
    tick()

    def wide_up(part, chunk):
        def give(start, value):
            up_wide[
                pl.ds(start + chunk * half_rows, vsize), LANES * part : LANES * (part + 1)
            ] = value

        return give

    for chunk in range(2):
        for part in range(2):
            split_go.finish(2 * part + chunk, vsize, wide_up(part, chunk))
    split_go.drain()

    def keep_down(start, value):
        place = pl.ds(start + side, vsize)
        value = value.astype(BF16).astype(F32)
        moved = pltpu.roll(value * flags[place, 1:2], vsize - 1, 0)
        for half in range(2):
            lanes = slice(LANES * half, LANES * (half + 1))
            shifted[half, place, :] = value[:, lanes]
            shifted[2 + half, place, :] = moved[:, lanes]

    have("hat_down")
    norm_back(
        wide_ex[0],
        lambda place: up_wide[place, :],
        up_wide,
        hat_wide.at[0],
        gain_d[...],
        shift_d[...],
        inv_wide[0, 0:1, :],
        vec_wide.at[0],
        keep_down,
        tick,
    )

    def four_rows(start):
        place = pl.ds(start, vsize)
        here, below = pl.ds(start + side, vsize), pl.ds(start + 2 * side, vsize)
        keep = flags[below, 0:1]
        for kind in range(2):
            for half in range(2):
                lane = 256 * kind + LANES * half
                spread[place, lane : lane + LANES] = shifted[2 * kind + half, here, :].astype(BF16)
                spread[place, 512 + lane : 512 + lane + LANES] = (
                    shifted[2 * kind + half, below, :] * keep
                ).astype(BF16)

    tiles(rows, vsize, four_rows)
    have("features")

    def version(row_tap, col_tap):
        return 256 * (2 * (row_tap == 0) + (col_tap == 0))

    def phase_of(row_tap, col_tap):
        return 2 * (row_tap != 1) + (col_tap != 1)

    for row_tap in range(3):
        for col_tap in range(3):
            tap = 3 * row_tap + col_tap
            lane = version(row_tap, col_tap)
            for pair in range(2):
                phase = phase_of(row_tap, col_tap)
                left = join([fbuf[2 * pair + step, phase] for step in range(2)])
                sum_down[pl.ds(512 * tap + 256 * pair, 256), :] = lax.dot_general(
                    left, spread[:, lane : lane + 256], along_dims, preferred_element_type=F32
                ).astype(BF16)
        piece = pl.ds(1536 * row_tap, 1536)
        room = landing_rows(1536, batch_count)
        flat = dbuf.at[pl.ds(room * row_tap, room)]
        begin(sum_down.at[piece], flat, 1 if row_tap == 1 else 0, down_out.at[piece])
    have("down")

    down_go = Scatter(
        at,
        (
            lambda owner, phase: hbuf.at[phase, owner],
            lambda block, phase: jbuf.at[block, phase],
            lambda phase: rcross_d.at[phase],
            lambda phase: across_d.at[phase],
        ),
        send,
        recv,
        base[0],
    )
    order = (3, 2, 1, 0)

    def feature_terms(phase, pair):
        row_taps = (0, 2) if phase // 2 else (1,)
        col_taps = (0, 2) if phase % 2 else (1,)

        def body(start):
            place = pl.ds(start, msize)
            total = None
            for row_tap in row_taps:
                for col_tap in col_taps:
                    lane = version(row_tap, col_tap)
                    one = lax.dot_general(
                        spread[place, lane : lane + 256],
                        wd[3 * row_tap + col_tap, pair_rows(pair), :],
                        across_dims,
                        preferred_element_type=F32,
                    )
                    total = one if total is None else total + one
            terms = total.astype(BF16)
            for step in range(2):
                hbuf[phase, 2 * pair + step, place, :] = terms[:, LANES * step : LANES * (step + 1)]

        tiles(rows, msize, body)

    for phase in order:
        feature_terms(phase, 1 - at.pair)
        down_go.far_copy(phase).start()
    for phase in order:
        down_go.relay(phase, vsize)
        feature_terms(phase, at.pair)
        down_go.mate_copy(phase).start()
        tick(3)

    def place_back(phase):
        row_par, col_par = phase // 2, phase % 2

        def give(start, value):
            line = start // side
            for step in range(vsize // side):
                feat_grad[2 * (line + step) + row_par, pl.ds(col_par, side, stride=2), :] = value[
                    side * step : side * (step + 1), :
                ]

        return give

    for phase in order:
        down_go.finish(phase, vsize, place_back(phase))
        tick(3)
    down_go.drain()
    while queue:
        tick(len(queue))
    for made in (*wide_ex, *slim_ex):
        made.drain()


def backward_call(batch_count, side, grad_in, flags, weights, kept, inverses, vectors):
    rows = grad_in.shape[0]
    wide = 2 * LANES
    hbm = pl.BlockSpec(memory_space=pl.ANY)
    vmem = pl.BlockSpec(memory_space=pltpu.VMEM)
    dma = pltpu.SemaphoreType.DMA
    shape = jax.ShapeDtypeStruct
    bits = batch_count.bit_length() - 1
    near = list(range(bits))
    turned = [1, 0, *near[2:]] if bits > 1 else near
    feat_rows = 2 * rows // side * 1
    sums = [
        shape((1024, wide), BF16),
        shape((5120, LANES), BF16),
        shape((5120, LANES), BF16),
        shape((2560, LANES), BF16),
        shape((4608, wide), BF16),
    ]
    scratch = [
        pltpu.VMEM((rows, wide), BF16),
        pltpu.VMEM((9, 512, wide), BF16),
        pltpu.VMEM((1024, wide), BF16),
        pltpu.VMEM((2, 512, LANES), BF16),
        pltpu.VMEM((2, 512, 9 * LANES), BF16),
        pltpu.VMEM((512, LANES), BF16),
        pltpu.VMEM((1024, wide), BF16),
        pltpu.VMEM((4, 4, rows, LANES), BF16),
        pltpu.VMEM((4 * rows, wide), BF16),
        pltpu.VMEM((5, 4, rows, LANES), BF16),
        pltpu.VMEM((2, 4, rows, LANES), BF16),
        pltpu.VMEM((3, rows, wide), F32),
        pltpu.VMEM((5, rows, LANES), F32),
        pltpu.VMEM((rows, wide), F32),
        pltpu.VMEM((rows, LANES), F32),
        pltpu.VMEM((rows, LANES), F32),
        pltpu.VMEM((rows, LANES), F32),
        pltpu.VMEM((4, rows + 2 * side, LANES), F32),
        pltpu.VMEM((rows, 9 * LANES), BF16),
        pltpu.VMEM((rows, wide), BF16),
        pltpu.VMEM((rows, LANES), BF16),
        pltpu.VMEM((2, 4, rows, LANES), BF16),
        pltpu.VMEM((2, 2, 2, rows, LANES), BF16),
        pltpu.VMEM((2, 2, rows, LANES), BF16),
        pltpu.VMEM((2, rows, LANES), BF16),
        pltpu.VMEM((4, rows, LANES), BF16),
        pltpu.VMEM((4, rows, LANES), BF16),
        *[pltpu.VMEM(one.shape, one.dtype) for one in sums],
        *[
            pltpu.VMEM((landing_rows(one.shape[0], batch_count), one.shape[1]), one.dtype)
            for one in sums[:4]
        ],
        pltpu.VMEM((3, batch_count, 8, wide), F32),
        pltpu.VMEM((5, batch_count, 8, LANES), F32),
        dma((3, batch_count)),
        dma((5, batch_count)),
        dma((3, batch_count)),
        dma((5, batch_count)),
        dma((72,)),
        dma((72,)),
        dma((8 * 2 * bits,)),
        dma((8 * 2 * bits,)),
        dma((60,)),
        dma((12,)),
    ]
    return pl.pallas_call(
        functools.partial(backward_kernel, batch_count, side, (near, turned)),
        out_shape=[
            shape((feat_rows, 2 * side, LANES), F32),
            shape((3, 8, wide), F32),
            shape((5, 8, LANES), F32),
            *sums,
        ],
        in_specs=[hbm, vmem] + [hbm] * 6 + [hbm] * 6 + [vmem] * 2 + [vmem] * 10,
        out_specs=[vmem] * 3 + [hbm] * 5,
        scratch_shapes=scratch,
        compiler_params=pltpu.CompilerParams(
            collective_id=1, has_side_effects=True, vmem_limit_bytes=VMEM_LIMIT
        ),
    )(grad_in, flags, *weights, *kept, *inverses, *vectors)


def local(
    features,
    tile_split,
    out_grad,
    w_down,
    gain_down,
    shift_down,
    w_split,
    gain_split,
    shift_split,
    w_first,
    w_second,
    gain_block,
    shift_block,
    w_trans,
    gain_trans,
    shift_trans,
    w_merge,
    gain_merge,
    shift_merge,
):
    side = out_grad.shape[1]
    count = lax.axis_size("batch")
    flags = mask_columns(tile_split, side)

    def row(vec):
        return vec.reshape(1, -1)

    weights = (
        w_down.reshape(9, w_down.shape[2], w_down.shape[3]),
        w_split,
        w_first,
        w_second.reshape(2, 9, w_second.shape[3], w_second.shape[4]),
        w_trans,
        w_merge,
    )
    vectors = (
        row(gain_down),
        row(shift_down),
        gain_split,
        shift_split,
        gain_block.reshape(4, -1),
        shift_block.reshape(4, -1),
        row(gain_trans),
        row(shift_trans),
        row(gain_merge),
        row(shift_merge),
    )
    mixed, *kept = forward_call(
        count,
        side,
        features.reshape(-1, features.shape[2], features.shape[3]),
        flags,
        weights,
        vectors,
    )
    kept[1] = kept[1].reshape(-1, kept[1].shape[2])
    grad_rows = out_grad.reshape(-1, out_grad.shape[3])
    feat_grad, vec_wide, vec_slim, merge, late, early, split, down = backward_call(
        count, side, grad_rows, flags, weights, kept[:6], kept[6:], vectors
    )
    taps = w_second.shape[1:]
    nine = late.shape[0] - w_trans.shape[0]
    two = split.shape[0] - w_first.shape[1]
    second_grad = jnp.stack([early[:nine].reshape(taps), late[:nine].reshape(taps)])
    first_grad = jnp.stack([split[two:], early[nine:]])
    return (
        mixed.reshape(out_grad.shape),
        feat_grad.reshape(features.shape),
        down.reshape(w_down.shape).astype(F32),
        vec_wide[0, 1],
        vec_wide[0, 0],
        split[:two].reshape(w_split.shape).astype(F32),
        vec_wide[1, 1].reshape(gain_split.shape),
        vec_wide[1, 0].reshape(shift_split.shape),
        first_grad.astype(F32),
        second_grad.astype(F32),
        vec_slim[:4, 1].reshape(gain_block.shape),
        vec_slim[:4, 0].reshape(shift_block.shape),
        late[nine:].astype(F32),
        vec_slim[4, 1],
        vec_slim[4, 0],
        merge.astype(F32),
        vec_wide[2, 1],
        vec_wide[2, 0],
    )


def solution(mesh):
    placed = (
        P("batch", None, None, "chan"),
        P("batch", None),
        P("batch", None, None, "chan"),
        P(None, None, None, "chan"),
        P("chan"),
        P("chan"),
        P(None, None, "chan"),
        P(None, "chan"),
        P(None, "chan"),
        P(None, None, "chan"),
        P(None, None, None, None, "chan"),
        P(None, None, "chan"),
        P(None, None, "chan"),
        P(None, "chan"),
        P("chan"),
        P("chan"),
        P(None, "chan"),
        P("chan"),
        P("chan"),
    )
    return jax.shard_map(
        local,
        mesh=mesh,
        in_specs=placed,
        out_specs=(
            P("batch", None, None, "chan"),
            P("batch", None, None, "chan"),
            P(None, None, None, "chan"),
            P("chan"),
            P("chan"),
            P(None, None, "chan"),
            P(None, "chan"),
            P(None, "chan"),
            P(None, None, "chan"),
            P(None, None, None, None, "chan"),
            P(None, None, "chan"),
            P(None, None, "chan"),
            P(None, "chan"),
            P("chan"),
            P("chan"),
            P(None, "chan"),
            P("chan"),
            P("chan"),
        ),
        check_vma=False,
    )
```

```python
import functools

import jax
import jax.numpy as jnp
from jax import lax
from jax.experimental import pallas as pl
from jax.experimental.pallas import tpu as pltpu
from jax.sharding import PartitionSpec as P

epsilon = 1e-05
F32 = jnp.float32
BF16 = jnp.bfloat16
MESH = pl.DeviceIdType.MESH
LANES = 128
VMEM_LIMIT = 60 * 1024 * 1024


def tap_masks(splits, side_len, stride):
    places = jnp.arange(side_len, dtype=jnp.int32)
    offset = jnp.arange(3, dtype=jnp.int32) - 1
    source = stride * places[:, None] + offset[None, :]
    inside = (source >= 0) & (source < stride * side_len)

    def along_axis(cut_at):
        cut_at = cut_at[:, None, None]
        same_tile = (source[None] < stride * cut_at) == (places[None, :, None] < cut_at)
        return (inside[None] & same_tile).astype(jnp.float32)

    return (along_axis(splits[:, 0]), along_axis(splits[:, 1]))


def mask_columns(tile_split, side_len):
    number = tile_split.shape[0]
    rows_two, cols_two = tap_masks(tile_split, side_len, 2)
    rows_one, cols_one = tap_masks(tile_split, side_len, 1)

    def by_row(flags):
        return jnp.broadcast_to(flags[:, :, None], (number, side_len, side_len)).reshape(-1)

    def by_col(flags):
        return jnp.broadcast_to(flags[:, None, :], (number, side_len, side_len)).reshape(-1)

    stacked = jnp.stack(
        [
            by_row(rows_two[:, :, 0]),
            by_col(cols_two[:, :, 0]),
            by_row(rows_one[:, :, 0]),
            by_row(rows_one[:, :, 2]),
            by_col(cols_one[:, :, 0]),
            by_col(cols_one[:, :, 2]),
        ],
        axis=1,
    )
    return jnp.pad(stacked, ((side_len, side_len), (0, 2)))


class Places:
    def __init__(self, batch_count):
        self.count = batch_count
        self.chan = lax.axis_index("chan")
        self.batch = lax.axis_index("batch")
        self.mate = self.chan + 1 - 2 * lax.rem(self.chan, 2)
        self.cross = lax.rem(self.chan + 2, 4)
        self.far = lax.rem(self.mate + 2, 4)
        self.pair = self.chan // 2

    def greet(self):
        barrier = pltpu.get_barrier_semaphore()
        for partner in (self.mate, self.cross):
            pl.semaphore_signal(
                barrier, inc=1, device_id={"chan": partner}, device_id_type=MESH
            )

        def hail(step, carry):
            peer = lax.rem(self.batch + step, self.count)
            pl.semaphore_signal(barrier, inc=1, device_id={"batch": peer}, device_id_type=MESH)
            return carry

        lax.fori_loop(1, self.count, hail, 0)
        pl.semaphore_wait(barrier, 2 + self.count - 1)


class Gather:
    def __init__(self, places, view, chunks, send, recv, base):
        self.at, self.view, self.chunks = places, view, chunks
        self.send, self.recv, self.base = send, recv, base

    def copy(self, owner, chunk, kind, partner):
        ref = self.view(owner, chunk)
        slot = self.base + 3 * chunk + kind
        return pltpu.make_async_remote_copy(
            src_ref=ref,
            dst_ref=ref,
            send_sem=self.send.at[slot],
            recv_sem=self.recv.at[slot],
            device_id={"chan": partner},
            device_id_type=MESH,
        )

    def start(self, chunk):
        self.copy(self.at.chan, chunk, 1, self.at.cross).start()
        self.copy(self.at.chan, chunk, 0, self.at.mate).start()

    def wait_mate(self, chunk):
        self.copy(self.at.mate, chunk, 0, self.at.mate).wait_recv()

    def forward(self, chunk):
        self.copy(self.at.cross, chunk, 1, self.at.cross).wait_recv()
        self.copy(self.at.cross, chunk, 2, self.at.mate).start()

    def wait_far(self, chunk):
        self.copy(self.at.far, chunk, 2, self.at.mate).wait_recv()

    def drain(self):
        for chunk in range(self.chunks):
            self.copy(self.at.chan, chunk, 0, self.at.mate).wait_send()
            self.copy(self.at.chan, chunk, 1, self.at.cross).wait_send()
            self.copy(self.at.cross, chunk, 2, self.at.mate).wait_send()


class Exchange:
    def __init__(self, places, slots, send, recv):
        self.at, self.slots, self.send, self.recv = places, slots, send, recv

    def copy(self, step, owner, peer):
        ref = self.slots.at[owner]
        return pltpu.make_async_remote_copy(
            src_ref=ref,
            dst_ref=ref,
            send_sem=self.send.at[step],
            recv_sem=self.recv.at[step],
            device_id={"batch": peer},
            device_id_type=MESH,
        )

    def push(self, block):
        at = self.at
        self.slots[at.batch] = block

        def start(step, carry):
            self.copy(step, at.batch, lax.rem(at.batch + step, at.count)).start()
            return carry

        lax.fori_loop(1, at.count, start, 0)

    def take(self):
        at = self.at

        def arrive(step, carry):
            owner = lax.rem(at.batch + at.count - step, at.count)
            self.copy(step, owner, owner).wait_recv()
            return carry

        lax.fori_loop(1, at.count, arrive, 0)

    def drain(self):
        at = self.at

        def sent(step, carry):
            self.copy(step, at.batch, lax.rem(at.batch + step, at.count)).wait_send()
            return carry

        lax.fori_loop(1, at.count, sent, 0)


def two_rows(first, second):
    return jnp.where(
        lax.broadcasted_iota(jnp.int32, (8, first.shape[1]), 0) == 0, first, second
    )


def fold(values):
    return jnp.sum(values.reshape(values.shape[0] // 8, 8, values.shape[1]), axis=0)


def tiles(total, size, body):
    def step(index, carry):
        body(pl.multiple_of(index * size, size))
        return carry

    lax.fori_loop(0, total // size, step, 0)


def mish_parts(before):
    grown = jnp.exp(jnp.minimum(before, 20.0))
    top = grown * (grown + 2.0)
    return grown, top


def join(halves):
    return jnp.concatenate(halves, axis=1)


class Norms:
    def __init__(self, exchange, rows, pixels):
        self.exchange, self.rows, self.pixels = exchange, rows, pixels

    def statistics(self, z_ref):
        rows, width = self.rows, z_ref.shape[1]
        size = 96

        def add_up(index, total):
            return total + fold(z_ref[pl.ds(pl.multiple_of(index * size, size), size), :])

        zero = jnp.zeros((8, width), F32)
        total = lax.fori_loop(0, rows // size, add_up, zero)
        mean = jnp.sum(total, axis=0, keepdims=True) / rows

        def spread(index, total):
            away = z_ref[pl.ds(pl.multiple_of(index * size, size), size), :] - mean
            return total + fold(away * away)

        total = lax.fori_loop(0, rows // size, spread, zero)
        square = jnp.sum(total, axis=0, keepdims=True)
        self.exchange.push(two_rows(mean, square))
        self.exchange.take()
        slots, count = self.exchange.slots, self.exchange.at.count

        def means(index, total):
            return total + slots[index]

        whole = lax.fori_loop(0, count, means, zero)[0:1] / count

        def squares(index, total):
            block = slots[index]
            away = block[0:1] - whole
            return total + block[1:2] + rows * (away * away)

        variance = lax.fori_loop(0, count, squares, jnp.zeros((1, width), F32)) / self.pixels
        return whole, lax.rsqrt(variance + epsilon)


def forward_kernel(
    batch_count,
    side,
    feat,
    flags,
    wd_in,
    ws_in,
    wf_in,
    w2_in,
    wt_in,
    wm_in,
    gain_d,
    shift_d,
    gain_s,
    shift_s,
    gain_b,
    shift_b,
    gain_t,
    shift_t,
    gain_m,
    shift_m,
    mixed,
    feat_out,
    down_out,
    half_out,
    join_out,
    wide_out,
    slim_out,
    inv_wide,
    inv_slim,
    wd,
    ws,
    wf,
    w2,
    wt,
    wm,
    raw,
    fbuf,
    dbuf,
    hbuf,
    jbuf,
    hat_wide,
    hat_slim,
    acc_wide,
    acc_slim,
    z_wide,
    z_slim,
    branch,
    slots_wide,
    slots_slim,
    wide_sem,
    slim_sem,
    wide_rsem,
    slim_rsem,
    send,
    recv,
    wsem,
    osem,
):
    at = Places(batch_count)
    me = at.chan
    rows = z_wide.shape[0]
    half_rows = rows // 2
    pixels = rows * batch_count
    area = side * side

    weight_copies = {}

    def bring(name, pairs):
        copies = []
        for source, target in pairs:
            slot = sum(len(done) for done in weight_copies.values()) + len(copies)
            copies.append(pltpu.make_async_copy(source, target, wsem.at[slot]))
        weight_copies[name] = copies
        for copy in copies:
            copy.start()

    def have(name):
        for copy in weight_copies[name]:
            copy.wait()

    bring("down", [(wd_in.at[tap], wd.at[tap]) for tap in range(9)])
    bring("split", [(ws_in.at[part], ws.at[:, pl.ds(LANES * part, LANES)]) for part in range(2)])
    for layer in range(2):
        bring(f"first{layer}", [(wf_in.at[layer], wf.at[layer])])
        bring(
            f"second{layer}",
            [
                (w2_in.at[layer, tap], w2.at[layer, :, pl.ds(LANES * tap, LANES)])
                for tap in range(9)
            ],
        )
    bring("trans", [(wt_in, wt)])
    bring("merge", [(wm_in, wm)])

    saved = []

    def save(source, target):
        copy = pltpu.make_async_copy(source, target, osem.at[len(saved)])
        copy.start()
        saved.append(copy)

    base = [0]

    def gather(view, chunks):
        made = Gather(at, view, chunks, send, recv, base[0])
        base[0] += 3 * chunks
        return made

    def by_half(ref):
        return lambda owner, chunk: ref.at[owner, pl.ds(chunk * half_rows, half_rows)]

    feat_go = gather(lambda owner, phase: fbuf.at[owner, phase], 4)
    down_go = gather(by_half(dbuf), 2)
    half_go = [gather(by_half(hbuf.at[index]), 2) for index in range(5)]
    side_go = gather(by_half(jbuf.at[1]), 2)
    top_go = gather(by_half(jbuf.at[0]), 2)
    wide_ex = [
        Exchange(at, slots_wide.at[index], wide_sem.at[index], wide_rsem.at[index])
        for index in range(3)
    ]
    slim_ex = [
        Exchange(at, slots_slim.at[index], slim_sem.at[index], slim_rsem.at[index])
        for index in range(5)
    ]

    at.greet()

    for phase in range(4):
        row_par, col_par = phase // 2, phase % 2

        if col_par == 0:

            def widen(index, carry):
                raw[index] = feat[2 * index + row_par].astype(F32)
                return carry

            lax.fori_loop(0, feat.shape[0] // 2, widen, 0)

        def pick(start):
            both = [
                raw[2 * (start // (2 * side)) + step, pl.ds(col_par, side, stride=2), :]
                for step in range(2)
            ]
            fbuf[me, phase, pl.ds(start, 2 * side), :] = jnp.concatenate(both, axis=0).astype(BF16)

        tiles(rows, 2 * side, pick)
        feat_go.start(phase)

    acc_wide[...] = jnp.zeros_like(acc_wide)
    have("down")

    def down_pair(phase, pair):
        row_par, col_par = phase // 2, phase % 2
        row_taps = (0, 2) if row_par else (1,)
        col_taps = (0, 2) if col_par else (1,)
        size = 192

        def body(start):
            block = join(
                [fbuf[2 * pair + step, phase, pl.ds(start, size), :] for step in range(2)]
            )
            for row_tap in row_taps:
                for col_tap in col_taps:
                    part = jnp.dot(
                        block,
                        wd[3 * row_tap + col_tap, pl.ds(pl.multiple_of(pair * 256, 256), 256), :],
                        preferred_element_type=F32,
                    )
                    place = pl.ds(start + (2 * side if row_tap == 0 else side), size)
                    if row_tap == 0:
                        part = part * flags[place, 0:1]
                    kind = 1 if col_tap == 0 else 0
                    acc_wide[kind, place, :] += part

        tiles(rows, size, body)

    for phase in range(4):
        feat_go.wait_mate(phase)
        down_pair(phase, at.pair)
        feat_go.forward(phase)
    for phase in range(4):
        feat_go.wait_far(phase)
        down_pair(phase, 1 - at.pair)
    save(fbuf, feat_out)

    vsize = 4 * side

    def settle_down(start):
        place = pl.ds(start + side, vsize)
        z_wide[pl.ds(start, vsize), :] = acc_wide[0, place, :] + flags[place, 1:2] * pltpu.roll(
            acc_wide[1, place, :], 1, 0
        )

    tiles(rows, vsize, settle_down)

    def activate(exchange, z_ref, hat_ref, gain, shift, inv_ref, give, begin):
        mean, inverse = Norms(exchange, rows, pixels).statistics(z_ref)
        inv_ref[...] = jnp.broadcast_to(inverse, inv_ref.shape)

        def body(start):
            place = pl.ds(start, vsize)
            normed = (z_ref[place, :] - mean) * inverse
            hat_ref[place, :] = normed
            before = normed * gain + shift
            _, top = mish_parts(before)
            give(place, before * (top / (top + 2.0)))

        for chunk in range(2):

            def inner(start):
                body(start + chunk * half_rows)

            tiles(half_rows, vsize, inner)
            begin(chunk)

    def keep_down(place, value):
        dbuf[me, place, :] = value.astype(BF16)

    activate(
        wide_ex[0], z_wide, hat_wide.at[0], gain_d[...], shift_d[...], inv_wide.at[0], keep_down,
        down_go.start,
    )
    save(hat_wide.at[0], wide_out.at[0])
    have("split")

    msize = 192

    def split_block(owner, chunk, first):
        def body(start):
            place = pl.ds(start + chunk * half_rows, msize)
            part = jnp.dot(
                dbuf[owner, place, :],
                ws[pl.ds(pl.multiple_of(owner * 256, 256), 256), :],
                preferred_element_type=F32,
            )
            if first:
                z_wide[place, :] = part
            else:
                z_wide[place, :] += part

        tiles(half_rows, msize, body)

    for chunk in range(2):
        split_block(me, chunk, True)
    for chunk in range(2):
        down_go.wait_mate(chunk)
        split_block(at.mate, chunk, False)
    for chunk in range(2):
        down_go.forward(chunk)
        split_block(at.cross, chunk, False)
    for chunk in range(2):
        down_go.wait_far(chunk)
        split_block(at.far, chunk, False)
    save(dbuf, down_out)

    def keep_split(place, value):
        branch[place, :] = value[:, :LANES]
        hbuf[0, me, place, :] = value[:, :LANES].astype(BF16)
        jbuf[1, me, place, :] = value[:, LANES:].astype(BF16)

    activate(
        wide_ex[1],
        z_wide,
        hat_wide.at[1],
        join([gain_s[0:1, :], gain_s[1:2, :]]),
        join([shift_s[0:1, :], shift_s[1:2, :]]),
        inv_wide.at[1],
        keep_split,
        half_go[0].start,
    )
    save(hat_wide.at[1], wide_out.at[1])
    for chunk in range(2):
        side_go.start(chunk)

    def two_of(ref, pair, place):
        return join([ref[2 * pair + step, place, :] for step in range(2)])

    def thin_pair(source, weight, pair, chunk, first):
        def body(start):
            place = pl.ds(start + chunk * half_rows, msize)
            part = jnp.dot(
                two_of(source, pair, place),
                weight[pl.ds(pl.multiple_of(pair * 256, 256), 256), :],
                preferred_element_type=F32,
            )
            if first:
                z_slim[place, :] = part
            else:
                z_slim[place, :] += part

        tiles(half_rows, msize, body)

    def thin_conv(index, weight):
        source, go = hbuf.at[index], half_go[index]
        for chunk in range(2):
            go.wait_mate(chunk)
            thin_pair(source, weight, at.pair, chunk, True)
        for chunk in range(2):
            go.forward(chunk)
        for chunk in range(2):
            go.wait_far(chunk)
            thin_pair(source, weight, 1 - at.pair, chunk, False)
        save(source, half_out.at[index])

    def tap_pair(source, weight, pair, chunk):
        def body(start):
            begin = start + chunk * half_rows
            part = jnp.dot(
                two_of(source, pair, pl.ds(begin, msize)),
                weight[pl.ds(pl.multiple_of(pair * 256, 256), 256), :],
                preferred_element_type=F32,
            )
            for col_tap in range(3):
                for row_tap in range(3):
                    tap = 3 * row_tap + col_tap
                    piece = part[:, LANES * tap : LANES * (tap + 1)]
                    place = pl.ds(begin + side - side * (row_tap - 1), msize)
                    if row_tap != 1:
                        column = 2 if row_tap == 0 else 3
                        piece = piece * flags[place, column : column + 1]
                    acc_slim[col_tap, place, :] += piece

        tiles(half_rows, msize, body)

    def tap_conv(index, weight):
        source, go = hbuf.at[index], half_go[index]
        acc_slim[...] = jnp.zeros_like(acc_slim)
        for chunk in range(2):
            go.wait_mate(chunk)
            tap_pair(source, weight, at.pair, chunk)
        for chunk in range(2):
            go.forward(chunk)
        for chunk in range(2):
            go.wait_far(chunk)
            tap_pair(source, weight, 1 - at.pair, chunk)
        save(source, half_out.at[index])

        def settle(start):
            place = pl.ds(start + side, vsize)
            z_slim[pl.ds(start, vsize), :] = (
                acc_slim[1, place, :]
                + flags[place, 4:5] * pltpu.roll(acc_slim[0, place, :], 1, 0)
                + flags[place, 5:6] * pltpu.roll(acc_slim[2, place, :], vsize - 1, 0)
            )

        tiles(rows, vsize, settle)

    def slim_act(index, gain, shift, give, begin):
        activate(
            slim_ex[index], z_slim, hat_slim.at[index], gain, shift, inv_slim.at[index], give, begin
        )
        save(hat_slim.at[index], slim_out.at[index])

    for layer in range(2):
        have(f"first{layer}")
        thin_conv(2 * layer, wf.at[layer])

        def keep_inner(place, value):
            hbuf[2 * layer + 1, me, place, :] = value.astype(BF16)

        slim_act(
            2 * layer,
            gain_b[2 * layer : 2 * layer + 1, :],
            shift_b[2 * layer : 2 * layer + 1, :],
            keep_inner,
            half_go[2 * layer + 1].start,
        )
        have(f"second{layer}")
        tap_conv(2 * layer + 1, w2.at[layer])

        def keep_branch(place, value):
            total = branch[place, :] + value
            branch[place, :] = total
            hbuf[2 * layer + 2, me, place, :] = total.astype(BF16)

        slim_act(
            2 * layer + 1,
            gain_b[2 * layer + 1 : 2 * layer + 2, :],
            shift_b[2 * layer + 1 : 2 * layer + 2, :],
            keep_branch,
            half_go[2 * layer + 2].start,
        )
        if layer == 0:
            for chunk in range(2):
                side_go.forward(chunk)
    have("trans")
    thin_conv(4, wt)

    def keep_top(place, value):
        jbuf[0, me, place, :] = value.astype(BF16)

    slim_act(4, gain_t[...], shift_t[...], keep_top, top_go.start)
    have("merge")

    def merge_pair(part_index, pair, chunk, first):
        def body(start):
            place = pl.ds(start + chunk * half_rows, msize)
            part = jnp.dot(
                two_of(jbuf.at[part_index], pair, place),
                wm[pl.ds(pl.multiple_of(part_index * 512 + pair * 256, 256), 256), :],
                preferred_element_type=F32,
            )
            if first:
                z_wide[place, :] = part
            else:
                z_wide[place, :] += part

        tiles(half_rows, msize, body)

    for chunk in range(2):
        side_go.wait_mate(chunk)
        merge_pair(1, at.pair, chunk, True)
    for chunk in range(2):
        side_go.wait_far(chunk)
        merge_pair(1, 1 - at.pair, chunk, False)
    for chunk in range(2):
        top_go.wait_mate(chunk)
        merge_pair(0, at.pair, chunk, False)
    for chunk in range(2):
        top_go.forward(chunk)
    for chunk in range(2):
        top_go.wait_far(chunk)
        merge_pair(0, 1 - at.pair, chunk, False)
    save(jbuf, join_out)

    def keep_mixed(place, value):
        mixed[place, :] = value.astype(BF16)

    activate(
        wide_ex[2], z_wide, hat_wide.at[2], gain_m[...], shift_m[...], inv_wide.at[2], keep_mixed,
        lambda chunk: None,
    )
    save(hat_wide.at[2], wide_out.at[2])

    for made in (feat_go, down_go, *half_go, side_go, top_go):
        made.drain()
    for made in (*wide_ex, *slim_ex):
        made.drain()
    for copy in saved:
        copy.wait()


def forward_call(batch_count, side, feat, flags, weights, vectors):
    rows = feat.shape[0] * side // 2
    wide = 2 * LANES
    hbm = pl.BlockSpec(memory_space=pl.ANY)
    vmem = pl.BlockSpec(memory_space=pltpu.VMEM)
    dma = pltpu.SemaphoreType.DMA
    shape = jax.ShapeDtypeStruct
    kept = [
        shape((4, 4, rows, LANES), BF16),
        shape((4, rows, wide), BF16),
        shape((5, 4, rows, LANES), BF16),
        shape((2, 4, rows, LANES), BF16),
        shape((3, rows, wide), F32),
        shape((5, rows, LANES), F32),
    ]
    taps_width = 9 * LANES
    scratch = [
        pltpu.VMEM((9, 512, wide), BF16),
        pltpu.VMEM((1024, wide), BF16),
        pltpu.VMEM((2, 512, LANES), BF16),
        pltpu.VMEM((2, 512, taps_width), BF16),
        pltpu.VMEM((512, LANES), BF16),
        pltpu.VMEM((1024, wide), BF16),
        pltpu.VMEM((feat.shape[0] // 2, feat.shape[1], LANES), F32),
        *[pltpu.VMEM(one.shape, one.dtype) for one in kept],
        pltpu.VMEM((2, rows + 2 * side, wide), F32),
        pltpu.VMEM((3, rows + 2 * side, LANES), F32),
        pltpu.VMEM((rows, wide), F32),
        pltpu.VMEM((rows, LANES), F32),
        pltpu.VMEM((rows, LANES), F32),
        pltpu.VMEM((3, batch_count, 8, wide), F32),
        pltpu.VMEM((5, batch_count, 8, LANES), F32),
        dma((3, batch_count)),
        dma((5, batch_count)),
        dma((3, batch_count)),
        dma((5, batch_count)),
        dma((60,)),
        dma((60,)),
        dma((40,)),
        dma((20,)),
    ]
    return pl.pallas_call(
        functools.partial(forward_kernel, batch_count, side),
        out_shape=[
            shape((rows, wide), BF16),
            *kept,
            shape((3, 8, wide), F32),
            shape((5, 8, LANES), F32),
        ],
        in_specs=[vmem, vmem] + [hbm] * 6 + [vmem] * 10,
        out_specs=[vmem] + [hbm] * 6 + [vmem, vmem],
        scratch_shapes=scratch,
        compiler_params=pltpu.CompilerParams(
            collective_id=0, has_side_effects=True, vmem_limit_bytes=VMEM_LIMIT
        ),
    )(feat, flags, *weights, *vectors)


class Scatter:
    def __init__(self, places, views, send, recv, base):
        self.at = places
        self.term, self.from_mate, self.from_cross, self.across = views
        self.send, self.recv, self.base = send, recv, base
        self.used = []

    def copy(self, source, target, chunk, kind, partner):
        slot = self.base + 3 * chunk + kind
        return pltpu.make_async_remote_copy(
            src_ref=source,
            dst_ref=target,
            send_sem=self.send.at[slot],
            recv_sem=self.recv.at[slot],
            device_id={"chan": partner},
            device_id_type=MESH,
        )

    def far_copy(self, chunk):
        return self.copy(
            self.term(self.at.far, chunk), self.from_mate(0, chunk), chunk, 0, self.at.mate
        )

    def mate_copy(self, chunk):
        return self.copy(
            self.term(self.at.mate, chunk), self.from_mate(1, chunk), chunk, 1, self.at.mate
        )

    def cross_copy(self, chunk):
        return self.copy(self.across(chunk), self.from_cross(chunk), chunk, 2, self.at.cross)

    def relay(self, chunk, size):
        self.far_copy(chunk).wait_recv()
        mine, theirs, both = (
            self.term(self.at.cross, chunk),
            self.from_mate(0, chunk),
            self.across(chunk),
        )

        def add(start):
            place = pl.ds(start, size)
            both[place, :] = (mine[place, :].astype(F32) + theirs[place, :].astype(F32)).astype(
                BF16
            )

        tiles(mine.shape[0], size, add)
        self.cross_copy(chunk).start()

    def finish(self, chunk, size, give):
        self.mate_copy(chunk).wait_recv()
        self.cross_copy(chunk).wait_recv()
        parts = (self.term(self.at.chan, chunk), self.from_mate(1, chunk), self.from_cross(chunk))

        def add(start):
            place = pl.ds(start, size)
            first, second, third = [part[place, :].astype(F32) for part in parts]
            give(start, first + second + third)

        tiles(parts[0].shape[0], size, add)
        self.used.append(chunk)

    def drain(self):
        for chunk in self.used:
            self.far_copy(chunk).wait_send()
            self.mate_copy(chunk).wait_send()
            self.cross_copy(chunk).wait_send()


def tile_of(rows):
    return max(size for size in range(8, 321, 8) if rows % size == 0)


class Links:
    rate, latency = 50000.0, 2.5

    def __init__(self):
        self.free = {}

    def plan(self, now, bit, size):
        span = size / self.rate
        loads = {2: ((1, span), (2, 2 * span))}.get(bit, ((bit, span),))
        return {link: max(now, self.free.get(link, 0.0)) + load for link, load in loads}


class Reducer:
    def __init__(self, places, buf, landing, out, order, sems, base, own_sem):
        self.at, self.buf, self.landing, self.out = places, buf, landing, out
        self.order, (self.send, self.recv), self.base = order, sems, base
        self.own_sem = own_sem
        self.low, self.size, self.taken, self.step = 0, buf.shape[0], 0, 0
        self.due = 0.0

    def next_load(self):
        steps = len(self.order)
        if self.step < steps:
            bit, size = self.order[self.step], self.size // 2
        else:
            bit, size = self.order[2 * steps - 1 - self.step], self.size
        return bit, 2 * size * self.buf.shape[1]

    def partner(self, bit):
        side = lax.rem(self.at.batch // (1 << bit), 2)
        return side, self.at.batch + (1 - 2 * side) * (1 << bit)

    def copy(self, source, target, partner):
        return pltpu.make_async_remote_copy(
            src_ref=source,
            dst_ref=target,
            send_sem=self.send.at[self.base + self.step],
            recv_sem=self.recv.at[self.base + self.step],
            device_id={"batch": partner},
            device_id_type=MESH,
        )

    def rows(self, low, size):
        return pl.ds(pl.multiple_of(low, 8), size)

    def launch(self):
        steps = len(self.order)
        if self.step < steps:
            side, partner = self.partner(self.order[self.step])
            half = self.size // 2
            gone = self.low + (1 - side) * half
            self.flying = self.copy(
                self.buf.at[self.rows(gone, half)],
                self.landing.at[pl.ds(self.taken, half)],
                partner,
            )
            self.kept = self.low + side * half
            self.flying.start()
            return
        side, partner = self.partner(self.order[2 * steps - 1 - self.step])
        target = self.out.at[self.rows(self.low, self.size)]
        source = target
        if self.step == steps:
            source = self.buf.at[self.rows(self.low, self.size)]
            self.own = pltpu.make_async_copy(source, target, self.own_sem)
            self.own.start()
        self.flying = self.copy(source, target, partner)
        self.flying.start()
        other = self.out.at[self.rows(self.low + (1 - 2 * side) * self.size, self.size)]
        self.coming = self.copy(other, other, partner)
        self.next_low = self.low - side * self.size

    def advance(self):
        steps = len(self.order)
        if self.step < steps:
            self.flying.wait()
            half = self.size // 2
            size = tile_of(half)
            taken, kept = self.taken, self.kept

            def add(start):
                place = self.rows(kept + start, size)
                self.buf[place, :] = (
                    self.buf[place, :].astype(F32)
                    + self.landing[pl.ds(taken + start, size), :].astype(F32)
                ).astype(BF16)

            tiles(half, size, add)
            self.low, self.size, self.taken = kept, half, taken + half
        else:
            self.coming.wait_recv()
            self.flying.wait_send()
            if self.step == steps:
                self.own.wait()
            self.low, self.size = self.next_low, 2 * self.size
        self.step += 1
        return self.step == 2 * steps


first_row = (10240, 0)
second_row = (512, 5120)
trans_row = 9728
split_row = 10752
tap_ends = (2, 5, 7, 9)
big_rows = 12800


def landing_rows(rows, batch_count):
    return rows - rows // batch_count


def backward_kernel(
    batch_count,
    side,
    orders,
    grad_in,
    flags,
    wd_in,
    ws_in,
    wf_in,
    w2_in,
    wt_in,
    wm_in,
    feat_in,
    down_in,
    half_in,
    join_in,
    wide_in,
    slim_in,
    inv_wide,
    inv_slim,
    gain_d,
    shift_d,
    gain_s,
    shift_s,
    gain_b,
    shift_b,
    gain_t,
    shift_t,
    gain_m,
    shift_m,
    feat_grad,
    vec_wide,
    vec_slim,
    merge_out,
    big_out,
    down_out,
    grad,
    wd,
    ws,
    wf,
    w2,
    wt,
    wm,
    fbuf,
    dbuf,
    hbuf,
    jbuf,
    hat_wide,
    hat_slim,
    up_wide,
    up_slim,
    branch,
    bypass,
    shifted,
    spread,
    dz_wide,
    dz_slim,
    pbuf,
    rmate,
    rcross,
    across,
    rcross_d,
    across_d,
    sum_merge,
    sum_big,
    sum_down,
    land_merge,
    land_big,
    slots_wide,
    slots_slim,
    wide_sem,
    slim_sem,
    wide_rsem,
    slim_rsem,
    send,
    recv,
    bsend,
    brecv,
    wsem,
    osem,
):
    at = Places(batch_count)
    rows = up_wide.shape[0]
    half_rows = rows // 2
    pixels = rows * batch_count
    vsize = 4 * side
    msize = 192

    fetched = {}
    count = [0]

    def bring(name, *pairs):
        copies = []
        for source, target in pairs:
            copies.append(pltpu.make_async_copy(source, target, wsem.at[count[0]]))
            count[0] += 1
        fetched[name] = copies
        for copy in copies:
            copy.start()

    def have(name):
        for copy in fetched[name]:
            copy.wait()

    bring("grad", (grad_in, grad), (wide_in.at[2], hat_wide.at[2]))
    bring("merge", (wm_in, wm))
    bring("joined", (join_in, jbuf))
    bring("hat4", (slim_in.at[4], hat_slim.at[4]))
    bring("trans", (wt_in, wt))
    bring("half4", (half_in.at[4], hbuf.at[4]))
    for layer in (1, 0):
        index = 2 * layer + 1
        bring(f"hat{index}", (slim_in.at[index], hat_slim.at[index]))
        bring(
            f"second{layer}",
            *[
                (w2_in.at[layer, tap], w2.at[layer, :, pl.ds(LANES * tap, LANES)])
                for tap in range(9)
            ],
        )
        bring(f"half{index}", (half_in.at[index], hbuf.at[index]))
        index = 2 * layer
        bring(f"hat{index}", (slim_in.at[index], hat_slim.at[index]))
        bring(f"first{layer}", (wf_in.at[layer], wf.at[layer]))
        bring(f"half{index}", (half_in.at[index], hbuf.at[index]))
    bring("hat_split", (wide_in.at[1], hat_wide.at[1]))
    bring("split", *[(ws_in.at[part], ws.at[:, pl.ds(LANES * part, LANES)]) for part in range(2)])
    bring("down_low", (down_in, dbuf))
    bring("hat_down", (wide_in.at[0], hat_wide.at[0]))
    bring("features", (feat_in, fbuf))
    bring("down", *[(wd_in.at[tap], wd.at[tap]) for tap in range(9)])

    wide_ex = [
        Exchange(at, slots_wide.at[index], wide_sem.at[index], wide_rsem.at[index])
        for index in range(3)
    ]
    slim_ex = [
        Exchange(at, slots_slim.at[index], slim_sem.at[index], slim_rsem.at[index])
        for index in range(5)
    ]

    base = [0]

    def scatter(stage, parts):
        kit = stage % 2

        def cut(ref):
            return lambda *where: ref.at[(*where[:-1], pl.ds(where[-1] * half_rows, half_rows))]

        def term(owner, chunk):
            return cut(pbuf)(chunk // 2, owner, chunk % 2)

        def from_mate(block, chunk):
            return cut(rmate)(kit, chunk // 2, block, chunk % 2)

        def from_cross(chunk):
            return cut(rcross)(kit, chunk // 2, chunk % 2)

        def over(chunk):
            return cut(across)(chunk // 2, chunk % 2)

        made = Scatter(at, (term, from_mate, from_cross, over), send, recv, base[0])
        base[0] += 6 * parts
        return made

    steps = 2 * len(orders[0])
    bbase = [0]

    queue, held = [], []
    links = Links()
    quiet = [(start + 0.5, start + 6) for start in (30, 41, 59, 75, 93, 108, 130)]

    def begin(buf, landing, order, out, now):
        made = Reducer(
            at,
            buf,
            landing,
            out,
            orders[order],
            (bsend, brecv),
            bbase[0],
            osem.at[bbase[0] // steps],
        )
        bbase[0] += steps
        held.append(made)
        resume(now)

    def resume(now):
        for made in list(held):
            plan = links.plan(now, *made.next_load())
            over = max(plan.values())
            if any(now < end and over > start for start, end in quiet):
                continue
            links.free.update(plan)
            made.due = over + links.latency
            made.launch()
            held.remove(made)
            queue.append(made)

    def step_on(made, now):
        queue.remove(made)
        if not made.advance():
            held.append(made)
            resume(now)

    def pause(now):
        while queue:
            made = min(queue, key=lambda one: one.due)
            if made.due > now:
                break
            step_on(made, now)
        resume(now)

    big_taken = [0]

    def begin_rows(low, size, order, now):
        room = landing_rows(size, batch_count)
        where = pl.ds(low, size)
        landing = land_big.at[pl.ds(big_taken[0], room)]
        begin(sum_big.at[where], landing, order, big_out.at[where], now)
        big_taken[0] += room

    at.greet()

    for ref in (shifted,):
        ref[...] = jnp.zeros_like(ref)

    def norm_back(exchange, load, back, hat, gain, shift, inverse, vec_ref, give, now):
        width = back.shape[1]

        def first(index, carry):
            place = pl.ds(pl.multiple_of(index * vsize, vsize), vsize)
            normed = hat[place, :]
            before = normed * gain + shift
            grown, top = mish_parts(before)
            share = 1.0 / (top + 2.0)
            slope = top * share + before * (4.0 * grown * (1.0 + grown) * share * share)
            value = load(place) * slope
            back[place, :] = value
            return (carry[0] + fold(value), carry[1] + fold(value * normed))

        zero = jnp.zeros((8, width), F32)
        one, two = lax.fori_loop(0, rows // vsize, first, (zero, zero))
        exchange.push(
            two_rows(jnp.sum(one, axis=0, keepdims=True), jnp.sum(two, axis=0, keepdims=True))
        )
        pause(now + 2)
        exchange.take()
        pause(now + 6)
        slots = exchange.slots

        def gather_up(index, total):
            return total + slots[index]

        total = lax.fori_loop(0, batch_count, gather_up, zero)
        vec_ref[...] = total
        scale = gain * inverse
        shift_part, gain_part = total[0:1] / pixels, total[1:2] / pixels

        def second(start):
            place = pl.ds(start, vsize)
            give(start, scale * (back[place, :] - shift_part - hat[place, :] * gain_part))

        tiles(rows, vsize, second)

    across_dims = (((1,), (1,)), ((), ()))
    along_dims = (((0,), (0,)), ((), ()))

    def back_pair(left, weight, pair, chunk, part):
        def body(start):
            begin_at = start + chunk * half_rows
            terms = lax.dot_general(
                left(pl.ds(begin_at, msize)), weight, across_dims, preferred_element_type=F32
            ).astype(BF16)
            for step in range(2):
                pbuf[part, 2 * pair + step, pl.ds(begin_at, msize), :] = terms[
                    :, LANES * step : LANES * (step + 1)
                ]

        tiles(half_rows, msize, body)

    def pair_rows(pair, offset=0):
        return pl.ds(pl.multiple_of(offset + pair * 256, 256), 256)

    def spread_out(go, left, weight_at, parts, now, span):
        chunks = 2 * parts
        for chunk in range(chunks):
            back_pair(left, weight_at(chunk // 2, 1 - at.pair), 1 - at.pair, chunk % 2, chunk // 2)
            go.far_copy(chunk).start()
        pause(now + 0.45 * span)
        for chunk in range(chunks):
            go.relay(chunk, vsize)
        pause(now + 0.5 * span)
        for chunk in range(chunks):
            back_pair(left, weight_at(chunk // 2, at.pair), at.pair, chunk % 2, chunk // 2)
            go.mate_copy(chunk).start()

    def two_of(ref, pair):
        return join([ref[2 * pair + step] for step in range(2)])

    have("grad")
    merge_go = scatter(0, 2)

    def keep_wide(start, value):
        dz_wide[pl.ds(start, vsize), :] = value.astype(BF16)

    norm_back(
        wide_ex[2],
        lambda place: grad[place, :].astype(F32),
        up_wide,
        hat_wide.at[2],
        gain_m[...],
        shift_m[...],
        inv_wide[2, 0:1, :],
        vec_wide.at[2],
        keep_wide,
        6,
    )
    have("merge")
    spread_out(
        merge_go,
        lambda place: dz_wide[place, :],
        lambda part, pair: wm[pair_rows(pair, 512 * part), :],
        2,
        12,
        18,
    )
    have("joined")
    for part in range(2):
        for pair in range(2):
            sum_merge[pl.ds(512 * part + 256 * pair, 256), :] = lax.dot_general(
                two_of(jbuf.at[part], pair), dz_wide[...], along_dims, preferred_element_type=F32
            ).astype(BF16)
    begin(sum_merge, land_merge, 0, merge_out, 24)

    def top_up(chunk):
        def give(start, value):
            up_slim[pl.ds(start + chunk * half_rows, vsize), :] = value

        return give

    for chunk in range(2):
        merge_go.finish(chunk, vsize, top_up(chunk))

    def keep_slim(start, value):
        dz_slim[pl.ds(start, vsize), :] = value.astype(BF16)

    def slim_back(index, load, gain, shift, give, now):
        have(f"hat{index}")
        norm_back(
            slim_ex[index],
            load,
            up_slim,
            hat_slim.at[index],
            gain,
            shift,
            inv_slim[index, 0:1, :],
            vec_slim.at[index],
            give,
            now,
        )

    def settle_with(go, settle, now, span):
        pause(now + 0.7 * span)
        for chunk in range(2):
            go.finish(chunk, vsize, settle(chunk))
            pause(now + (0.85 + 0.15 * chunk) * span)

    def thin_back(stage, index, weight, name, offset, settle, now, span):
        go = scatter(stage, 1)
        have(name)
        spread_out(
            go,
            lambda place: dz_slim[place, :],
            lambda part, pair: weight[pair_rows(pair), :],
            1,
            now,
            span,
        )
        have(f"half{index}")
        for pair in range(2):
            sum_big[pl.ds(offset + 256 * pair, 256), :] = lax.dot_general(
                two_of(hbuf.at[index], pair), dz_slim[...], along_dims, preferred_element_type=F32
            ).astype(BF16)
        settle_with(go, settle, now, span)
        return go

    slim_back(4, lambda place: up_slim[place, :], gain_t[...], shift_t[...], keep_slim, 30)

    def branch_new(chunk):
        def give(start, value):
            branch[pl.ds(start + chunk * half_rows, vsize), :] = value

        return give

    def branch_more(chunk):
        def give(start, value):
            branch[pl.ds(start + chunk * half_rows, vsize), :] += value

        return give

    def bypass_up(chunk):
        def give(start, value):
            bypass[pl.ds(start + chunk * half_rows, vsize), :] = value

        return give

    def finish_bypass():
        for chunk in range(2):
            merge_go.finish(2 + chunk, vsize, bypass_up(chunk))
        merge_go.drain()

    finish_bypass()
    thin_back(1, 4, wt, "trans", trans_row, branch_new, 30, 11).drain()

    def nine(start, value):
        place = pl.ds(start + side, vsize)
        value = value.astype(BF16).astype(F32)
        shifted[1, place, :] = value
        shifted[0, place, :] = pltpu.roll(value * flags[place, 4:5], vsize - 1, 0)
        shifted[2, place, :] = pltpu.roll(value * flags[place, 5:6], 1, 0)

    def nine_rows(start):
        for row_tap in range(3):
            source = pl.ds(start + side - side * (row_tap - 1), vsize)
            for col_tap in range(3):
                tap = 3 * row_tap + col_tap
                value = shifted[col_tap, source, :]
                if row_tap != 1:
                    column = 2 if row_tap == 0 else 3
                    value = value * flags[source, column : column + 1]
                spread[pl.ds(start, vsize), LANES * tap : LANES * (tap + 1)] = value.astype(BF16)

    def tap_back(stage, layer, offset, settle, begin_sums, now, span):
        index = 2 * layer + 1
        go = scatter(stage, 1)
        tiles(rows, vsize, nine_rows)
        have(f"second{layer}")
        spread_out(
            go,
            lambda place: spread[place, :],
            lambda part, pair: w2[layer, pair_rows(pair), :],
            1,
            now,
            span,
        )
        have(f"half{index}")
        for pair in range(2):
            left = two_of(hbuf.at[index], pair)
            for row_tap in range(3):
                three = lax.dot_general(
                    left,
                    spread[:, 3 * LANES * row_tap : 3 * LANES * (row_tap + 1)],
                    along_dims,
                    preferred_element_type=F32,
                ).astype(BF16)
                for col_tap in range(3):
                    row = offset + 512 * (3 * row_tap + col_tap) + 256 * pair
                    sum_big[pl.ds(row, 256), :] = three[
                        :, LANES * col_tap : LANES * (col_tap + 1)
                    ]
        begin_sums(now + 0.7 * span)
        settle_with(go, settle, now, span)
        go.drain()

    def late_sums(now):
        begin_rows(second_row[1], 2560, 0, now)
        begin_rows(second_row[1] + 2560, 2560, 1, now)

    def early_sums(now):
        begin_rows(0, 2560, 0, now)
        begin_rows(2560, 2560, 1, now)

    for layer in (1, 0):
        stage = 2 if layer == 1 else 4
        now = 41 if layer == 1 else 75
        slim_back(
            2 * layer + 1,
            lambda place: branch[place, :],
            gain_b[2 * layer + 1 : 2 * layer + 2, :],
            shift_b[2 * layer + 1 : 2 * layer + 2, :],
            nine,
            now,
        )
        tap_back(
            stage,
            layer,
            second_row[layer],
            top_up,
            late_sums if layer == 1 else early_sums,
            now,
            18,
        )
        now += 18
        slim_back(
            2 * layer,
            lambda place: up_slim[place, :],
            gain_b[2 * layer : 2 * layer + 1, :],
            shift_b[2 * layer : 2 * layer + 1, :],
            keep_slim,
            now,
        )
        thin_back(
            stage + 1,
            2 * layer,
            wf.at[layer],
            f"first{layer}",
            first_row[layer],
            branch_more,
            now,
            15,
        ).drain()

    have("hat_split")
    norm_back(
        wide_ex[1],
        lambda place: join([branch[place, :], bypass[place, :]]),
        up_wide,
        hat_wide.at[1],
        join([gain_s[0:1, :], gain_s[1:2, :]]),
        join([shift_s[0:1, :], shift_s[1:2, :]]),
        inv_wide[1, 0:1, :],
        vec_wide.at[1],
        keep_wide,
        108,
    )
    have("split")
    split_go = scatter(6, 2)

    def split_terms(owner, chunk):
        def body(start):
            place = pl.ds(start + chunk * half_rows, msize)
            terms = lax.dot_general(
                dz_wide[place, :],
                ws[pl.ds(pl.multiple_of(owner * 256, 256), 256), :],
                across_dims,
                preferred_element_type=F32,
            ).astype(BF16)
            for part in range(2):
                pbuf[part, owner, place, :] = terms[:, LANES * part : LANES * (part + 1)]

        tiles(half_rows, msize, body)

    for chunk in range(2):
        split_terms(at.far, chunk)
        for part in range(2):
            split_go.far_copy(2 * part + chunk).start()
    pause(115)
    for chunk in range(2):
        split_terms(at.cross, chunk)
        for part in range(2):
            split_go.relay(2 * part + chunk, vsize)
    pause(118)
    for chunk in range(2):
        split_terms(at.mate, chunk)
        for part in range(2):
            split_go.mate_copy(2 * part + chunk).start()
    for chunk in range(2):
        split_terms(at.chan, chunk)
    have("down_low")
    for owner in range(4):
        result = lax.dot_general(
            dbuf[rows * owner : rows * (owner + 1), :], dz_wide[...], along_dims, preferred_element_type=F32
        ).astype(BF16)
        for part in range(2):
            sum_big[pl.ds(split_row + 1024 * part + 256 * owner, 256), :] = result[
                :, LANES * part : LANES * (part + 1)
            ]
    begin_rows(first_row[0], 2560, 0, 122)
    pause(122)

    def wide_up(part, chunk):
        def give(start, value):
            up_wide[
                pl.ds(start + chunk * half_rows, vsize), LANES * part : LANES * (part + 1)
            ] = value

        return give

    for chunk in range(2):
        for part in range(2):
            split_go.finish(2 * part + chunk, vsize, wide_up(part, chunk))
            pause(124 + 4 * chunk + 2 * part)
    split_go.drain()

    def keep_down(start, value):
        place = pl.ds(start + side, vsize)
        value = value.astype(BF16).astype(F32)
        moved = pltpu.roll(value * flags[place, 1:2], vsize - 1, 0)
        for half in range(2):
            lanes = slice(LANES * half, LANES * (half + 1))
            shifted[half, place, :] = value[:, lanes]
            shifted[2 + half, place, :] = moved[:, lanes]

    have("hat_down")
    norm_back(
        wide_ex[0],
        lambda place: up_wide[place, :],
        up_wide,
        hat_wide.at[0],
        gain_d[...],
        shift_d[...],
        inv_wide[0, 0:1, :],
        vec_wide.at[0],
        keep_down,
        130,
    )

    def four_rows(start):
        place = pl.ds(start, vsize)
        here, below = pl.ds(start + side, vsize), pl.ds(start + 2 * side, vsize)
        keep = flags[below, 0:1]
        for kind in range(2):
            for half in range(2):
                lane = 256 * kind + LANES * half
                spread[place, lane : lane + LANES] = shifted[2 * kind + half, here, :].astype(BF16)
                spread[place, 512 + lane : 512 + lane + LANES] = (
                    shifted[2 * kind + half, below, :] * keep
                ).astype(BF16)

    tiles(rows, vsize, four_rows)
    have("features")

    def version(row_tap, col_tap):
        return 256 * (2 * (row_tap == 0) + (col_tap == 0))

    def phase_of(row_tap, col_tap):
        return 2 * (row_tap != 1) + (col_tap != 1)

    now = 137.0
    taken = 0
    for tap in range(9):
        row_tap, col_tap = tap // 3, tap % 3
        lane = version(row_tap, col_tap)
        phase = phase_of(row_tap, col_tap)
        for pair in range(2):
            left = join([fbuf[2 * pair + step, phase] for step in range(2)])
            sum_down[pl.ds(512 * tap + 256 * pair, 256), :] = lax.dot_general(
                left, spread[:, lane : lane + 256], along_dims, preferred_element_type=F32
            ).astype(BF16)
        now += 0.5
        if tap + 1 in tap_ends:
            low = 512 * (([0, *tap_ends])[tap_ends.index(tap + 1)])
            size = 512 * (tap + 1) - low
            piece = pl.ds(low, size)
            room = landing_rows(size, batch_count)
            turn = tap_ends.index(tap + 1) % 3 == 1
            begin(sum_down.at[piece], dbuf.at[pl.ds(taken, room)], int(turn), down_out.at[piece], now)
            taken += room
            pause(now)
    have("down")

    down_go = Scatter(
        at,
        (
            lambda owner, phase: hbuf.at[phase, owner],
            lambda block, phase: jbuf.at[block, phase],
            lambda phase: rcross_d.at[phase],
            lambda phase: across_d.at[phase],
        ),
        send,
        recv,
        base[0],
    )
    order = (3, 2, 1, 0)

    def feature_terms(phase, pair):
        row_taps = (0, 2) if phase // 2 else (1,)
        col_taps = (0, 2) if phase % 2 else (1,)

        def body(start):
            place = pl.ds(start, msize)
            total = None
            for row_tap in row_taps:
                for col_tap in col_taps:
                    lane = version(row_tap, col_tap)
                    one = lax.dot_general(
                        spread[place, lane : lane + 256],
                        wd[3 * row_tap + col_tap, pair_rows(pair), :],
                        across_dims,
                        preferred_element_type=F32,
                    )
                    total = one if total is None else total + one
            terms = total.astype(BF16)
            for step in range(2):
                hbuf[phase, 2 * pair + step, place, :] = terms[:, LANES * step : LANES * (step + 1)]

        tiles(rows, msize, body)

    for phase in order:
        feature_terms(phase, 1 - at.pair)
        down_go.far_copy(phase).start()
        now += 1.5
        pause(now)
    for phase in order:
        down_go.relay(phase, vsize)
        feature_terms(phase, at.pair)
        down_go.mate_copy(phase).start()
        now += 1.7
        pause(now)

    def place_back(phase):
        row_par, col_par = phase // 2, phase % 2

        def give(start, value):
            line = start // side
            for step in range(vsize // side):
                feat_grad[2 * (line + step) + row_par, pl.ds(col_par, side, stride=2), :] = value[
                    side * step : side * (step + 1), :
                ]

        return give

    arriving = [(147 + 5.9 * turn + 8.5, phase) for turn, phase in enumerate(order)]
    while queue or held or arriving:
        resume(now)
        made = min(queue, key=lambda one: one.due) if queue else None
        if arriving and (made is None or arriving[0][0] <= made.due):
            due, phase = arriving.pop(0)
            now = max(now, due)
            down_go.finish(phase, vsize, place_back(phase))
        else:
            now = max(now, made.due)
            step_on(made, now)
    down_go.drain()
    for made in (*wide_ex, *slim_ex):
        made.drain()


def backward_call(batch_count, side, grad_in, flags, weights, kept, inverses, vectors):
    rows = grad_in.shape[0]
    wide = 2 * LANES
    hbm = pl.BlockSpec(memory_space=pl.ANY)
    vmem = pl.BlockSpec(memory_space=pltpu.VMEM)
    dma = pltpu.SemaphoreType.DMA
    shape = jax.ShapeDtypeStruct
    bits = batch_count.bit_length() - 1
    near = list(range(bits))
    turned = [1, 0, *near[2:]] if bits > 1 else near
    feat_rows = 2 * rows // side
    sums = [
        shape((1024, wide), BF16),
        shape((big_rows, LANES), BF16),
        shape((4608, wide), BF16),
    ]
    scratch = [
        pltpu.VMEM((rows, wide), BF16),
        pltpu.VMEM((9, 512, wide), BF16),
        pltpu.VMEM((1024, wide), BF16),
        pltpu.VMEM((2, 512, LANES), BF16),
        pltpu.VMEM((2, 512, 9 * LANES), BF16),
        pltpu.VMEM((512, LANES), BF16),
        pltpu.VMEM((1024, wide), BF16),
        pltpu.VMEM((4, 4, rows, LANES), BF16),
        pltpu.VMEM((4 * rows, wide), BF16),
        pltpu.VMEM((5, 4, rows, LANES), BF16),
        pltpu.VMEM((2, 4, rows, LANES), BF16),
        pltpu.VMEM((3, rows, wide), F32),
        pltpu.VMEM((5, rows, LANES), F32),
        pltpu.VMEM((rows, wide), F32),
        pltpu.VMEM((rows, LANES), F32),
        pltpu.VMEM((rows, LANES), F32),
        pltpu.VMEM((rows, LANES), F32),
        pltpu.VMEM((4, rows + 2 * side, LANES), F32),
        pltpu.VMEM((rows, 9 * LANES), BF16),
        pltpu.VMEM((rows, wide), BF16),
        pltpu.VMEM((rows, LANES), BF16),
        pltpu.VMEM((2, 4, rows, LANES), BF16),
        pltpu.VMEM((2, 2, 2, rows, LANES), BF16),
        pltpu.VMEM((2, 2, rows, LANES), BF16),
        pltpu.VMEM((2, rows, LANES), BF16),
        pltpu.VMEM((4, rows, LANES), BF16),
        pltpu.VMEM((4, rows, LANES), BF16),
        *[pltpu.VMEM(one.shape, one.dtype) for one in sums],
        *[
            pltpu.VMEM((landing_rows(one.shape[0], batch_count), one.shape[1]), one.dtype)
            for one in sums[:2]
        ],
        pltpu.VMEM((3, batch_count, 8, wide), F32),
        pltpu.VMEM((5, batch_count, 8, LANES), F32),
        dma((3, batch_count)),
        dma((5, batch_count)),
        dma((3, batch_count)),
        dma((5, batch_count)),
        dma((72,)),
        dma((72,)),
        dma((15 * 2 * bits,)),
        dma((15 * 2 * bits,)),
        dma((60,)),
        dma((15,)),
    ]
    return pl.pallas_call(
        functools.partial(backward_kernel, batch_count, side, (near, turned)),
        out_shape=[
            shape((feat_rows, 2 * side, LANES), F32),
            shape((3, 8, wide), F32),
            shape((5, 8, LANES), F32),
            *sums,
        ],
        in_specs=[hbm, vmem] + [hbm] * 6 + [hbm] * 6 + [vmem] * 2 + [vmem] * 10,
        out_specs=[vmem] * 3 + [hbm] * 3,
        scratch_shapes=scratch,
        compiler_params=pltpu.CompilerParams(
            collective_id=1, has_side_effects=True, vmem_limit_bytes=VMEM_LIMIT
        ),
    )(grad_in, flags, *weights, *kept, *inverses, *vectors)


def local(
    features,
    tile_split,
    out_grad,
    w_down,
    gain_down,
    shift_down,
    w_split,
    gain_split,
    shift_split,
    w_first,
    w_second,
    gain_block,
    shift_block,
    w_trans,
    gain_trans,
    shift_trans,
    w_merge,
    gain_merge,
    shift_merge,
):
    side = out_grad.shape[1]
    count = lax.axis_size("batch")
    flags = mask_columns(tile_split, side)

    def row(vec):
        return vec.reshape(1, -1)

    weights = (
        w_down.reshape(9, w_down.shape[2], w_down.shape[3]),
        w_split,
        w_first,
        w_second.reshape(2, 9, w_second.shape[3], w_second.shape[4]),
        w_trans,
        w_merge,
    )
    vectors = (
        row(gain_down),
        row(shift_down),
        gain_split,
        shift_split,
        gain_block.reshape(4, -1),
        shift_block.reshape(4, -1),
        row(gain_trans),
        row(shift_trans),
        row(gain_merge),
        row(shift_merge),
    )
    mixed, *kept = forward_call(
        count,
        side,
        features.reshape(-1, features.shape[2], features.shape[3]),
        flags,
        weights,
        vectors,
    )
    kept[1] = kept[1].reshape(-1, kept[1].shape[2])
    grad_rows = out_grad.reshape(-1, out_grad.shape[3])
    feat_grad, vec_wide, vec_slim, merge, big, down = backward_call(
        count, side, grad_rows, flags, weights, kept[:6], kept[6:], vectors
    )
    rows = w_trans.shape[0]
    two = second_row[0]
    second_grad = big[two : two + 18 * rows].reshape(w_second.shape)
    first_grad = jnp.stack([big[low : low + rows] for low in first_row])
    return (
        mixed.reshape(out_grad.shape),
        feat_grad.reshape(features.shape),
        down.reshape(w_down.shape).astype(F32),
        vec_wide[0, 1],
        vec_wide[0, 0],
        big[split_row:].reshape(w_split.shape).astype(F32),
        vec_wide[1, 1].reshape(gain_split.shape),
        vec_wide[1, 0].reshape(shift_split.shape),
        first_grad.astype(F32),
        second_grad.astype(F32),
        vec_slim[:4, 1].reshape(gain_block.shape),
        vec_slim[:4, 0].reshape(shift_block.shape),
        big[trans_row : trans_row + rows].astype(F32),
        vec_slim[4, 1],
        vec_slim[4, 0],
        merge.astype(F32),
        vec_wide[2, 1],
        vec_wide[2, 0],
    )


def solution(mesh):
    placed = (
        P("batch", None, None, "chan"),
        P("batch", None),
        P("batch", None, None, "chan"),
        P(None, None, None, "chan"),
        P("chan"),
        P("chan"),
        P(None, None, "chan"),
        P(None, "chan"),
        P(None, "chan"),
        P(None, None, "chan"),
        P(None, None, None, None, "chan"),
        P(None, None, "chan"),
        P(None, None, "chan"),
        P(None, "chan"),
        P("chan"),
        P("chan"),
        P(None, "chan"),
        P("chan"),
        P("chan"),
    )
    return jax.shard_map(
        local,
        mesh=mesh,
        in_specs=placed,
        out_specs=(
            P("batch", None, None, "chan"),
            P("batch", None, None, "chan"),
            P(None, None, None, "chan"),
            P("chan"),
            P("chan"),
            P(None, None, "chan"),
            P(None, "chan"),
            P(None, "chan"),
            P(None, None, "chan"),
            P(None, None, None, None, "chan"),
            P(None, None, "chan"),
            P(None, None, "chan"),
            P(None, "chan"),
            P("chan"),
            P("chan"),
            P(None, "chan"),
            P("chan"),
            P("chan"),
        ),
        check_vma=False,
    )
```

```python
import functools

import jax
import jax.numpy as jnp
from jax import lax
from jax.experimental import pallas as pl
from jax.experimental.pallas import tpu as pltpu
from jax.sharding import PartitionSpec as P

epsilon = 1e-05
F32 = jnp.float32
BF16 = jnp.bfloat16
MESH = pl.DeviceIdType.MESH
LANES = 128
VMEM_LIMIT = 60 * 1024 * 1024


def tap_masks(splits, side_len, stride):
    places = jnp.arange(side_len, dtype=jnp.int32)
    offset = jnp.arange(3, dtype=jnp.int32) - 1
    source = stride * places[:, None] + offset[None, :]
    inside = (source >= 0) & (source < stride * side_len)

    def along_axis(cut_at):
        cut_at = cut_at[:, None, None]
        same_tile = (source[None] < stride * cut_at) == (places[None, :, None] < cut_at)
        return (inside[None] & same_tile).astype(jnp.float32)

    return (along_axis(splits[:, 0]), along_axis(splits[:, 1]))


def mask_columns(tile_split, side_len):
    number = tile_split.shape[0]
    rows_two, cols_two = tap_masks(tile_split, side_len, 2)
    rows_one, cols_one = tap_masks(tile_split, side_len, 1)

    def by_row(flags):
        return jnp.broadcast_to(flags[:, :, None], (number, side_len, side_len)).reshape(-1)

    def by_col(flags):
        return jnp.broadcast_to(flags[:, None, :], (number, side_len, side_len)).reshape(-1)

    stacked = jnp.stack(
        [
            by_row(rows_two[:, :, 0]),
            by_col(cols_two[:, :, 0]),
            by_row(rows_one[:, :, 0]),
            by_row(rows_one[:, :, 2]),
            by_col(cols_one[:, :, 0]),
            by_col(cols_one[:, :, 2]),
        ],
        axis=1,
    )
    return jnp.pad(stacked, ((side_len, side_len), (0, 2)))


class Places:
    def __init__(self, batch_count):
        self.count = batch_count
        self.chan = lax.axis_index("chan")
        self.batch = lax.axis_index("batch")
        self.mate = self.chan + 1 - 2 * lax.rem(self.chan, 2)
        self.cross = lax.rem(self.chan + 2, 4)
        self.far = lax.rem(self.mate + 2, 4)
        self.pair = self.chan // 2

    def greet(self):
        barrier = pltpu.get_barrier_semaphore()
        for partner in (self.mate, self.cross):
            pl.semaphore_signal(
                barrier, inc=1, device_id={"chan": partner}, device_id_type=MESH
            )

        def hail(step, carry):
            peer = lax.rem(self.batch + step, self.count)
            pl.semaphore_signal(barrier, inc=1, device_id={"batch": peer}, device_id_type=MESH)
            return carry

        lax.fori_loop(1, self.count, hail, 0)
        pl.semaphore_wait(barrier, 2 + self.count - 1)


class Gather:
    def __init__(self, places, view, chunks, send, recv, base):
        self.at, self.view, self.chunks = places, view, chunks
        self.send, self.recv, self.base = send, recv, base

    def copy(self, owner, chunk, kind, partner):
        ref = self.view(owner, chunk)
        slot = self.base + 3 * chunk + kind
        return pltpu.make_async_remote_copy(
            src_ref=ref,
            dst_ref=ref,
            send_sem=self.send.at[slot],
            recv_sem=self.recv.at[slot],
            device_id={"chan": partner},
            device_id_type=MESH,
        )

    def start(self, chunk):
        self.copy(self.at.chan, chunk, 1, self.at.cross).start()
        self.copy(self.at.chan, chunk, 0, self.at.mate).start()

    def wait_mate(self, chunk):
        self.copy(self.at.mate, chunk, 0, self.at.mate).wait_recv()

    def forward(self, chunk):
        self.copy(self.at.cross, chunk, 1, self.at.cross).wait_recv()
        self.copy(self.at.cross, chunk, 2, self.at.mate).start()

    def wait_far(self, chunk):
        self.copy(self.at.far, chunk, 2, self.at.mate).wait_recv()

    def drain(self):
        for chunk in range(self.chunks):
            self.copy(self.at.chan, chunk, 0, self.at.mate).wait_send()
            self.copy(self.at.chan, chunk, 1, self.at.cross).wait_send()
            self.copy(self.at.cross, chunk, 2, self.at.mate).wait_send()


class Exchange:
    def __init__(self, places, slots, send, recv):
        self.at, self.slots, self.send, self.recv = places, slots, send, recv

    def copy(self, step, owner, peer):
        ref = self.slots.at[owner]
        return pltpu.make_async_remote_copy(
            src_ref=ref,
            dst_ref=ref,
            send_sem=self.send.at[step],
            recv_sem=self.recv.at[step],
            device_id={"batch": peer},
            device_id_type=MESH,
        )

    def push(self, block):
        at = self.at
        self.slots[at.batch] = block

        def start(step, carry):
            self.copy(step, at.batch, lax.rem(at.batch + step, at.count)).start()
            return carry

        lax.fori_loop(1, at.count, start, 0)

    def take(self):
        at = self.at

        def arrive(step, carry):
            owner = lax.rem(at.batch + at.count - step, at.count)
            self.copy(step, owner, owner).wait_recv()
            return carry

        lax.fori_loop(1, at.count, arrive, 0)

    def drain(self):
        at = self.at

        def sent(step, carry):
            self.copy(step, at.batch, lax.rem(at.batch + step, at.count)).wait_send()
            return carry

        lax.fori_loop(1, at.count, sent, 0)


def two_rows(first, second):
    return jnp.where(
        lax.broadcasted_iota(jnp.int32, (8, first.shape[1]), 0) == 0, first, second
    )


def fold(values):
    return jnp.sum(values.reshape(values.shape[0] // 8, 8, values.shape[1]), axis=0)


def tiles(total, size, body):
    def step(index, carry):
        body(pl.multiple_of(index * size, size))
        return carry

    lax.fori_loop(0, total // size, step, 0)


def mish_parts(before):
    grown = jnp.exp(jnp.minimum(before, 20.0))
    top = grown * (grown + 2.0)
    return grown, top


def join(halves):
    return jnp.concatenate(halves, axis=1)


class Norms:
    def __init__(self, exchange, rows, pixels):
        self.exchange, self.rows, self.pixels = exchange, rows, pixels

    def statistics(self, z_ref):
        rows, width = self.rows, z_ref.shape[1]
        size = 96

        def add_up(index, total):
            return total + fold(z_ref[pl.ds(pl.multiple_of(index * size, size), size), :])

        zero = jnp.zeros((8, width), F32)
        total = lax.fori_loop(0, rows // size, add_up, zero)
        mean = jnp.sum(total, axis=0, keepdims=True) / rows

        def spread(index, total):
            away = z_ref[pl.ds(pl.multiple_of(index * size, size), size), :] - mean
            return total + fold(away * away)

        total = lax.fori_loop(0, rows // size, spread, zero)
        square = jnp.sum(total, axis=0, keepdims=True)
        self.exchange.push(two_rows(mean, square))
        self.exchange.take()
        slots, count = self.exchange.slots, self.exchange.at.count

        def means(index, total):
            return total + slots[index]

        whole = lax.fori_loop(0, count, means, zero)[0:1] / count

        def squares(index, total):
            block = slots[index]
            away = block[0:1] - whole
            return total + block[1:2] + rows * (away * away)

        variance = lax.fori_loop(0, count, squares, jnp.zeros((1, width), F32)) / self.pixels
        return whole, lax.rsqrt(variance + epsilon)


class Scatter:
    def __init__(self, places, views, send, recv, base):
        self.at = places
        self.term, self.from_mate, self.from_cross, self.across = views
        self.send, self.recv, self.base = send, recv, base
        self.used = []

    def copy(self, source, target, chunk, kind, partner):
        slot = self.base + 3 * chunk + kind
        return pltpu.make_async_remote_copy(
            src_ref=source,
            dst_ref=target,
            send_sem=self.send.at[slot],
            recv_sem=self.recv.at[slot],
            device_id={"chan": partner},
            device_id_type=MESH,
        )

    def far_copy(self, chunk):
        return self.copy(
            self.term(self.at.far, chunk), self.from_mate(0, chunk), chunk, 0, self.at.mate
        )

    def mate_copy(self, chunk):
        return self.copy(
            self.term(self.at.mate, chunk), self.from_mate(1, chunk), chunk, 1, self.at.mate
        )

    def cross_copy(self, chunk):
        return self.copy(self.across(chunk), self.from_cross(chunk), chunk, 2, self.at.cross)

    def relay(self, chunk, size):
        self.far_copy(chunk).wait_recv()
        mine, theirs, both = (
            self.term(self.at.cross, chunk),
            self.from_mate(0, chunk),
            self.across(chunk),
        )

        def add(start):
            place = pl.ds(start, size)
            both[place, :] = (mine[place, :].astype(F32) + theirs[place, :].astype(F32)).astype(
                BF16
            )

        tiles(mine.shape[0], size, add)
        self.cross_copy(chunk).start()

    def finish(self, chunk, size, give):
        self.mate_copy(chunk).wait_recv()
        self.cross_copy(chunk).wait_recv()
        parts = (self.term(self.at.chan, chunk), self.from_mate(1, chunk), self.from_cross(chunk))

        def add(start):
            place = pl.ds(start, size)
            first, second, third = [part[place, :].astype(F32) for part in parts]
            give(start, first + second + third)

        tiles(parts[0].shape[0], size, add)
        self.used.append(chunk)

    def drain(self):
        for chunk in self.used:
            self.far_copy(chunk).wait_send()
            self.mate_copy(chunk).wait_send()
            self.cross_copy(chunk).wait_send()


def tile_of(rows):
    return max(size for size in range(8, 321, 8) if rows % size == 0)


class Links:
    rate, latency = 50000.0, 2.5

    def __init__(self):
        self.free = {}

    def plan(self, now, bit, size):
        span = size / self.rate
        loads = {2: ((1, span), (2, 2 * span))}.get(bit, ((bit, span),))
        return {link: max(now, self.free.get(link, 0.0)) + load for link, load in loads}


class Reducer:
    def __init__(self, places, buf, landing, out, order, sems, base, own_sem):
        self.at, self.buf, self.landing, self.out = places, buf, landing, out
        self.order, (self.send, self.recv), self.base = order, sems, base
        self.own_sem = own_sem
        self.low, self.size, self.taken, self.step = 0, buf.shape[0], 0, 0
        self.due = 0.0

    def next_load(self):
        steps = len(self.order)
        if self.step < steps:
            bit, size = self.order[self.step], self.size // 2
        else:
            bit, size = self.order[2 * steps - 1 - self.step], self.size
        return bit, 2 * size * self.buf.shape[1]

    def partner(self, bit):
        side = lax.rem(self.at.batch // (1 << bit), 2)
        return side, self.at.batch + (1 - 2 * side) * (1 << bit)

    def copy(self, source, target, partner):
        return pltpu.make_async_remote_copy(
            src_ref=source,
            dst_ref=target,
            send_sem=self.send.at[self.base + self.step],
            recv_sem=self.recv.at[self.base + self.step],
            device_id={"batch": partner},
            device_id_type=MESH,
        )

    def rows(self, low, size):
        return pl.ds(pl.multiple_of(low, 8), size)

    def launch(self):
        steps = len(self.order)
        if self.step < steps:
            side, partner = self.partner(self.order[self.step])
            half = self.size // 2
            gone = self.low + (1 - side) * half
            self.flying = self.copy(
                self.buf.at[self.rows(gone, half)],
                self.landing.at[pl.ds(self.taken, half)],
                partner,
            )
            self.kept = self.low + side * half
            self.flying.start()
            return
        side, partner = self.partner(self.order[2 * steps - 1 - self.step])
        target = self.out.at[self.rows(self.low, self.size)]
        source = target
        if self.step == steps:
            source = self.buf.at[self.rows(self.low, self.size)]
            self.own = pltpu.make_async_copy(source, target, self.own_sem)
            self.own.start()
        self.flying = self.copy(source, target, partner)
        self.flying.start()
        other = self.out.at[self.rows(self.low + (1 - 2 * side) * self.size, self.size)]
        self.coming = self.copy(other, other, partner)
        self.next_low = self.low - side * self.size

    def advance(self):
        steps = len(self.order)
        if self.step < steps:
            self.flying.wait()
            half = self.size // 2
            size = tile_of(half)
            taken, kept = self.taken, self.kept

            def add(start):
                place = self.rows(kept + start, size)
                self.buf[place, :] = (
                    self.buf[place, :].astype(F32)
                    + self.landing[pl.ds(taken + start, size), :].astype(F32)
                ).astype(BF16)

            tiles(half, size, add)
            self.low, self.size, self.taken = kept, half, taken + half
        else:
            self.coming.wait_recv()
            self.flying.wait_send()
            if self.step == steps:
                self.own.wait()
            self.low, self.size = self.next_low, 2 * self.size
        self.step += 1
        return self.step == 2 * steps


first_row = (10240, 0)
second_row = (512, 5120)
trans_row = 9728
split_row = 10752
tap_ends = (2, 5, 7, 9)
big_rows = 12800


def landing_rows(rows, batch_count):
    return rows - rows // batch_count


def section_kernel(
    batch_count,
    side,
    orders,
    flags,
    gain_d,
    shift_d,
    gain_s,
    shift_s,
    gain_b,
    shift_b,
    gain_t,
    shift_t,
    gain_m,
    shift_m,
    feat_in,
    grad_in,
    wd_in,
    ws_in,
    wf_in,
    w2_in,
    wt_in,
    wm_in,
    mixed,
    feat_grad,
    vec_wide,
    vec_slim,
    merge_out,
    big_out,
    down_out,
    feat,
    grad,
    wd,
    ws,
    wf,
    w2,
    wt,
    wm,
    fbuf,
    dbuf,
    hbuf,
    jbuf,
    hat_wide,
    hat_slim,
    inv_wide,
    inv_slim,
    acc,
    z_wide,
    z_slim,
    branch,
    bypass,
    spread,
    dz_wide,
    dz_slim,
    pbuf,
    rmate,
    rcross,
    across,
    rcross_d,
    sum_merge,
    sum_big,
    sum_down,
    land_big,
    slots_wide,
    slots_slim,
    wide_sem,
    slim_sem,
    wide_rsem,
    slim_rsem,
    send,
    recv,
    tsend,
    trecv,
    bsend,
    brecv,
    wsem,
    osem,
):
    raw = feat_grad
    at = Places(batch_count)
    me = at.chan
    rows = z_wide.shape[0]
    half_rows = rows // 2
    pixels = rows * batch_count
    area = side * side

    weight_copies = {}

    def bring(name, pairs):
        copies = []
        for source, target in pairs:
            slot = sum(len(done) for done in weight_copies.values()) + len(copies)
            copies.append(pltpu.make_async_copy(source, target, wsem.at[slot]))
        weight_copies[name] = copies
        for copy in copies:
            copy.start()

    def have(name):
        for copy in weight_copies[name]:
            copy.wait()

    bring("features", [(feat_in, feat)])
    bring("down", [(wd_in.at[tap], wd.at[tap]) for tap in range(9)])
    bring("split", [(ws_in.at[part], ws.at[:, pl.ds(LANES * part, LANES)]) for part in range(2)])
    for layer in range(2):
        bring(f"first{layer}", [(wf_in.at[layer], wf.at[layer])])
        bring(
            f"second{layer}",
            [
                (w2_in.at[layer, tap], w2.at[layer, :, pl.ds(LANES * tap, LANES)])
                for tap in range(9)
            ],
        )
    bring("trans", [(wt_in, wt)])
    bring("merge", [(wm_in, wm)])
    bring("grad", [(grad_in, grad)])

    base = [0]

    def gather(view, chunks):
        made = Gather(at, view, chunks, send, recv, base[0])
        base[0] += 3 * chunks
        return made

    def by_half(ref):
        return lambda owner, chunk: ref.at[owner, pl.ds(chunk * half_rows, half_rows)]

    feat_go = gather(lambda owner, phase: fbuf.at[owner, phase], 4)
    def down_rows(owner, start, size):
        return pl.ds(pl.multiple_of(owner * rows + start, 16), size)

    down_go = gather(
        lambda owner, chunk: dbuf.at[down_rows(owner, chunk * half_rows, half_rows)], 2
    )
    half_go = [gather(by_half(hbuf.at[index]), 2) for index in range(5)]
    side_go = gather(by_half(jbuf.at[1]), 2)
    top_go = gather(by_half(jbuf.at[0]), 2)
    wide_ex = [
        Exchange(at, slots_wide.at[index], wide_sem.at[index], wide_rsem.at[index])
        for index in range(3)
    ]
    slim_ex = [
        Exchange(at, slots_slim.at[index], slim_sem.at[index], slim_rsem.at[index])
        for index in range(5)
    ]

    at.greet()

    have("features")

    for phase in range(4):
        row_par, col_par = phase // 2, phase % 2

        if col_par == 0:

            def widen(index, carry):
                line = pl.multiple_of((2 * index + row_par) * 2 * side, 16)
                raw[index] = feat[pl.ds(line, 2 * side), :].astype(F32)
                return carry

            lax.fori_loop(0, raw.shape[0] // 2, widen, 0)

        def pick(start):
            both = [
                raw[2 * (start // (2 * side)) + step, pl.ds(col_par, side, stride=2), :]
                for step in range(2)
            ]
            fbuf[me, phase, pl.ds(start, 2 * side), :] = jnp.concatenate(both, axis=0).astype(BF16)

        tiles(rows, 2 * side, pick)
        feat_go.start(phase)

    acc[...] = jnp.zeros_like(acc)
    have("down")

    def down_pair(phase, pair):
        row_par, col_par = phase // 2, phase % 2
        row_taps = (0, 2) if row_par else (1,)
        col_taps = (0, 2) if col_par else (1,)
        size = 192

        def body(start):
            block = join(
                [fbuf[2 * pair + step, phase, pl.ds(start, size), :] for step in range(2)]
            )
            for row_tap in row_taps:
                for col_tap in col_taps:
                    part = jnp.dot(
                        block,
                        wd[3 * row_tap + col_tap, pl.ds(pl.multiple_of(pair * 256, 256), 256), :],
                        preferred_element_type=F32,
                    )
                    place = pl.ds(start + (2 * side if row_tap == 0 else side), size)
                    if row_tap == 0:
                        part = part * flags[place, 0:1]
                    kind = 1 if col_tap == 0 else 0
                    for half in range(2):
                        acc[2 * kind + half, place, :] += part[:, LANES * half : LANES * (half + 1)]

        tiles(rows, size, body)

    for phase in range(4):
        feat_go.wait_mate(phase)
        down_pair(phase, at.pair)
        feat_go.forward(phase)
    for phase in range(4):
        feat_go.wait_far(phase)
        down_pair(phase, 1 - at.pair)

    vsize = 4 * side

    def settle_down(start):
        place = pl.ds(start + side, vsize)
        for half in range(2):
            z_wide[pl.ds(start, vsize), LANES * half : LANES * (half + 1)] = acc[
                half, place, :
            ] + flags[place, 1:2] * pltpu.roll(acc[2 + half, place, :], 1, 0)

    tiles(rows, vsize, settle_down)

    def activate(exchange, z_ref, hat_ref, gain, shift, inv_ref, give, begin):
        mean, inverse = Norms(exchange, rows, pixels).statistics(z_ref)
        inv_ref[...] = jnp.broadcast_to(inverse, inv_ref.shape)

        def body(start):
            place = pl.ds(start, vsize)
            normed = (z_ref[place, :] - mean) * inverse
            hat_ref[place, :] = normed
            before = normed * gain + shift
            _, top = mish_parts(before)
            give(start, before * (top / (top + 2.0)))

        for chunk in range(2):

            def inner(start):
                body(start + chunk * half_rows)

            tiles(half_rows, vsize, inner)
            begin(chunk)

    def keep_down(start, value):
        dbuf[down_rows(me, start, vsize), :] = value.astype(BF16)

    activate(
        wide_ex[0], z_wide, hat_wide.at[0], gain_d[...], shift_d[...], inv_wide.at[0], keep_down,
        down_go.start,
    )
    have("split")

    msize = 192

    def split_block(owner, chunk, first):
        def body(start):
            place = pl.ds(start + chunk * half_rows, msize)
            part = jnp.dot(
                dbuf[down_rows(owner, start + chunk * half_rows, msize), :],
                ws[pl.ds(pl.multiple_of(owner * 256, 256), 256), :],
                preferred_element_type=F32,
            )
            if first:
                z_wide[place, :] = part
            else:
                z_wide[place, :] += part

        tiles(half_rows, msize, body)

    for chunk in range(2):
        split_block(me, chunk, True)
    for chunk in range(2):
        down_go.wait_mate(chunk)
        split_block(at.mate, chunk, False)
    for chunk in range(2):
        down_go.forward(chunk)
        split_block(at.cross, chunk, False)
    for chunk in range(2):
        down_go.wait_far(chunk)
        split_block(at.far, chunk, False)

    def keep_split(start, value):
        place = pl.ds(start, vsize)
        branch[place, :] = value[:, :LANES]
        hbuf[0, me, place, :] = value[:, :LANES].astype(BF16)
        jbuf[1, me, place, :] = value[:, LANES:].astype(BF16)

    activate(
        wide_ex[1],
        z_wide,
        hat_wide.at[1],
        join([gain_s[0:1, :], gain_s[1:2, :]]),
        join([shift_s[0:1, :], shift_s[1:2, :]]),
        inv_wide.at[1],
        keep_split,
        half_go[0].start,
    )
    for chunk in range(2):
        side_go.start(chunk)

    def two_of(ref, pair, place):
        return join([ref[2 * pair + step, place, :] for step in range(2)])

    def thin_pair(source, weight, pair, chunk, first):
        def body(start):
            place = pl.ds(start + chunk * half_rows, msize)
            part = jnp.dot(
                two_of(source, pair, place),
                weight[pl.ds(pl.multiple_of(pair * 256, 256), 256), :],
                preferred_element_type=F32,
            )
            if first:
                z_slim[place, :] = part
            else:
                z_slim[place, :] += part

        tiles(half_rows, msize, body)

    def thin_conv(index, weight):
        source, go = hbuf.at[index], half_go[index]
        for chunk in range(2):
            go.wait_mate(chunk)
            thin_pair(source, weight, at.pair, chunk, True)
        for chunk in range(2):
            go.forward(chunk)
        for chunk in range(2):
            go.wait_far(chunk)
            thin_pair(source, weight, 1 - at.pair, chunk, False)

    def tap_pair(source, weight, pair, chunk):
        def body(start):
            begin = start + chunk * half_rows
            part = jnp.dot(
                two_of(source, pair, pl.ds(begin, msize)),
                weight[pl.ds(pl.multiple_of(pair * 256, 256), 256), :],
                preferred_element_type=F32,
            )
            for col_tap in range(3):
                for row_tap in range(3):
                    tap = 3 * row_tap + col_tap
                    piece = part[:, LANES * tap : LANES * (tap + 1)]
                    place = pl.ds(begin + side - side * (row_tap - 1), msize)
                    if row_tap != 1:
                        column = 2 if row_tap == 0 else 3
                        piece = piece * flags[place, column : column + 1]
                    acc[col_tap, place, :] += piece

        tiles(half_rows, msize, body)

    def tap_conv(index, weight):
        source, go = hbuf.at[index], half_go[index]
        acc[0:3] = jnp.zeros((3, *acc.shape[1:]), F32)
        for chunk in range(2):
            go.wait_mate(chunk)
            tap_pair(source, weight, at.pair, chunk)
        for chunk in range(2):
            go.forward(chunk)
        for chunk in range(2):
            go.wait_far(chunk)
            tap_pair(source, weight, 1 - at.pair, chunk)

        def settle(start):
            place = pl.ds(start + side, vsize)
            z_slim[pl.ds(start, vsize), :] = (
                acc[1, place, :]
                + flags[place, 4:5] * pltpu.roll(acc[0, place, :], 1, 0)
                + flags[place, 5:6] * pltpu.roll(acc[2, place, :], vsize - 1, 0)
            )

        tiles(rows, vsize, settle)

    def slim_act(index, gain, shift, give, begin):
        activate(
            slim_ex[index], z_slim, hat_slim.at[index], gain, shift, inv_slim.at[index], give, begin
        )

    for layer in range(2):
        have(f"first{layer}")
        thin_conv(2 * layer, wf.at[layer])

        def keep_inner(start, value):
            place = pl.ds(start, vsize)
            hbuf[2 * layer + 1, me, place, :] = value.astype(BF16)

        slim_act(
            2 * layer,
            gain_b[2 * layer : 2 * layer + 1, :],
            shift_b[2 * layer : 2 * layer + 1, :],
            keep_inner,
            half_go[2 * layer + 1].start,
        )
        have(f"second{layer}")
        tap_conv(2 * layer + 1, w2.at[layer])

        def keep_branch(start, value):
            place = pl.ds(start, vsize)
            total = branch[place, :] + value
            branch[place, :] = total
            hbuf[2 * layer + 2, me, place, :] = total.astype(BF16)

        slim_act(
            2 * layer + 1,
            gain_b[2 * layer + 1 : 2 * layer + 2, :],
            shift_b[2 * layer + 1 : 2 * layer + 2, :],
            keep_branch,
            half_go[2 * layer + 2].start,
        )
        if layer == 0:
            for chunk in range(2):
                side_go.forward(chunk)
    have("trans")
    thin_conv(4, wt)

    def keep_top(start, value):
        place = pl.ds(start, vsize)
        jbuf[0, me, place, :] = value.astype(BF16)

    slim_act(4, gain_t[...], shift_t[...], keep_top, top_go.start)
    have("merge")

    def merge_pair(part_index, pair, chunk, first):
        def body(start):
            place = pl.ds(start + chunk * half_rows, msize)
            part = jnp.dot(
                two_of(jbuf.at[part_index], pair, place),
                wm[pl.ds(pl.multiple_of(part_index * 512 + pair * 256, 256), 256), :],
                preferred_element_type=F32,
            )
            if first:
                z_wide[place, :] = part
            else:
                z_wide[place, :] += part

        tiles(half_rows, msize, body)

    for chunk in range(2):
        side_go.wait_mate(chunk)
        merge_pair(1, at.pair, chunk, True)
    for chunk in range(2):
        side_go.wait_far(chunk)
        merge_pair(1, 1 - at.pair, chunk, False)
    for chunk in range(2):
        top_go.wait_mate(chunk)
        merge_pair(0, at.pair, chunk, False)
    for chunk in range(2):
        top_go.forward(chunk)
    for chunk in range(2):
        top_go.wait_far(chunk)
        merge_pair(0, 1 - at.pair, chunk, False)

    def keep_mixed(start, value):
        place = pl.ds(start, vsize)
        spread[place, 0:256] = value.astype(BF16)

    activate(
        wide_ex[2], z_wide, hat_wide.at[2], gain_m[...], shift_m[...], inv_wide.at[2], keep_mixed,
        lambda chunk: None,
    )

    for made in (feat_go, down_go, *half_go, side_go, top_go):
        made.drain()
    for made in (*wide_ex, *slim_ex):
        made.drain()
    mixed_copy = pltpu.make_async_copy(spread.at[:, pl.ds(0, 256)], mixed, osem.at[15])
    mixed_copy.start()

    wide_ex = [wide_ex[index] for index in (2, 1, 0)]

    base = [0]

    def scatter(stage, parts):
        kit = stage % 2

        def cut(ref):
            return lambda *where: ref.at[(*where[:-1], pl.ds(where[-1] * half_rows, half_rows))]

        def term(owner, chunk):
            return cut(pbuf)(chunk // 2, owner, chunk % 2)

        def from_mate(block, chunk):
            return cut(rmate)(kit, chunk // 2, block, chunk % 2)

        def from_cross(chunk):
            return cut(rcross)(kit, chunk // 2, chunk % 2)

        def over(chunk):
            return cut(across)(chunk // 2, chunk % 2)

        made = Scatter(at, (term, from_mate, from_cross, over), tsend, trecv, base[0])
        base[0] += 6 * parts
        return made

    steps = 2 * len(orders[0])
    bbase = [0]

    queue, held = [], []
    links = Links()
    quiet = [(start + 0.5, start + 6) for start in (30, 41, 59, 75, 93, 108, 130)]

    def begin(buf, landing, order, out, now):
        made = Reducer(
            at,
            buf,
            landing,
            out,
            orders[order],
            (bsend, brecv),
            bbase[0],
            osem.at[bbase[0] // steps],
        )
        bbase[0] += steps
        held.append(made)
        resume(now)

    def resume(now):
        for made in list(held):
            plan = links.plan(now, *made.next_load())
            over = max(plan.values())
            if any(now < end and over > start for start, end in quiet):
                continue
            links.free.update(plan)
            made.due = over + links.latency
            made.launch()
            held.remove(made)
            queue.append(made)

    def step_on(made, now):
        queue.remove(made)
        if not made.advance():
            held.append(made)
            resume(now)

    def pause(now):
        while queue:
            made = min(queue, key=lambda one: one.due)
            if made.due > now:
                break
            step_on(made, now)
        resume(now)

    big_taken = [0]

    def begin_rows(low, size, order, now):
        room = landing_rows(size, batch_count)
        where = pl.ds(low, size)
        landing = land_big.at[pl.ds(big_taken[0], room)]
        begin(sum_big.at[where], landing, order, big_out.at[where], now)
        big_taken[0] += room

    for low in (0, rows + side):
        acc[:, low : low + side, :] = jnp.zeros((acc.shape[0], side, LANES), F32)

    def norm_back(exchange, load, back, hat, gain, shift, inverse, vec_ref, give, now):
        width = back.shape[1]

        def first(index, carry):
            place = pl.ds(pl.multiple_of(index * vsize, vsize), vsize)
            normed = hat[place, :]
            before = normed * gain + shift
            grown, top = mish_parts(before)
            share = 1.0 / (top + 2.0)
            slope = top * share + before * (4.0 * grown * (1.0 + grown) * share * share)
            value = load(place) * slope
            back[place, :] = value
            return (carry[0] + fold(value), carry[1] + fold(value * normed))

        zero = jnp.zeros((8, width), F32)
        one, two = lax.fori_loop(0, rows // vsize, first, (zero, zero))
        exchange.push(
            two_rows(jnp.sum(one, axis=0, keepdims=True), jnp.sum(two, axis=0, keepdims=True))
        )
        pause(now + 2)
        exchange.take()
        pause(now + 6)
        slots = exchange.slots

        def gather_up(index, total):
            return total + slots[index]

        total = lax.fori_loop(0, batch_count, gather_up, zero)
        vec_ref[...] = total
        scale = gain * inverse
        shift_part, gain_part = total[0:1] / pixels, total[1:2] / pixels

        def second(start):
            place = pl.ds(start, vsize)
            give(start, scale * (back[place, :] - shift_part - hat[place, :] * gain_part))

        tiles(rows, vsize, second)

    across_dims = (((1,), (1,)), ((), ()))
    along_dims = (((0,), (0,)), ((), ()))

    def back_pair(left, weight, pair, chunk, part):
        def body(start):
            begin_at = start + chunk * half_rows
            terms = lax.dot_general(
                left(pl.ds(begin_at, msize)), weight, across_dims, preferred_element_type=F32
            ).astype(BF16)
            for step in range(2):
                pbuf[part, 2 * pair + step, pl.ds(begin_at, msize), :] = terms[
                    :, LANES * step : LANES * (step + 1)
                ]

        tiles(half_rows, msize, body)

    def pair_rows(pair, offset=0):
        return pl.ds(pl.multiple_of(offset + pair * 256, 256), 256)

    def spread_out(go, left, weight_at, parts, now, span):
        chunks = 2 * parts
        for chunk in range(chunks):
            back_pair(left, weight_at(chunk // 2, 1 - at.pair), 1 - at.pair, chunk % 2, chunk // 2)
            go.far_copy(chunk).start()
        pause(now + 0.45 * span)
        for chunk in range(chunks):
            go.relay(chunk, vsize)
        pause(now + 0.5 * span)
        for chunk in range(chunks):
            back_pair(left, weight_at(chunk // 2, at.pair), at.pair, chunk % 2, chunk // 2)
            go.mate_copy(chunk).start()

    def two_of(ref, pair):
        return join([ref[2 * pair + step] for step in range(2)])

    have("grad")
    merge_go = scatter(0, 2)

    def keep_wide(start, value):
        dz_wide[pl.ds(start, vsize), :] = value.astype(BF16)

    norm_back(
        wide_ex[2],
        lambda place: grad[place, :].astype(F32),
        z_wide,
        hat_wide.at[2],
        gain_m[...],
        shift_m[...],
        inv_wide[2, 0:1, :],
        vec_wide.at[2],
        keep_wide,
        6,
    )
    spread_out(
        merge_go,
        lambda place: dz_wide[place, :],
        lambda part, pair: wm[pair_rows(pair, 512 * part), :],
        2,
        12,
        18,
    )
    for part in range(2):
        for pair in range(2):
            sum_merge[pl.ds(512 * part + 256 * pair, 256), :] = lax.dot_general(
                two_of(jbuf.at[part], pair), dz_wide[...], along_dims, preferred_element_type=F32
            ).astype(BF16)
    begin(sum_merge, grad.at[pl.ds(0, landing_rows(1024, batch_count))], 0, merge_out, 24)

    def top_up(chunk):
        def give(start, value):
            z_slim[pl.ds(start + chunk * half_rows, vsize), :] = value

        return give

    for chunk in range(2):
        merge_go.finish(chunk, vsize, top_up(chunk))

    def keep_slim(start, value):
        dz_slim[pl.ds(start, vsize), :] = value.astype(BF16)

    def slim_back(index, load, gain, shift, give, now):
        norm_back(
            slim_ex[index],
            load,
            z_slim,
            hat_slim.at[index],
            gain,
            shift,
            inv_slim[index, 0:1, :],
            vec_slim.at[index],
            give,
            now,
        )

    def settle_with(go, settle, now, span):
        pause(now + 0.7 * span)
        for chunk in range(2):
            go.finish(chunk, vsize, settle(chunk))
            pause(now + (0.85 + 0.15 * chunk) * span)

    def thin_back(stage, index, weight, offset, settle, now, span):
        go = scatter(stage, 1)
        spread_out(
            go,
            lambda place: dz_slim[place, :],
            lambda part, pair: weight[pair_rows(pair), :],
            1,
            now,
            span,
        )
        for pair in range(2):
            sum_big[pl.ds(offset + 256 * pair, 256), :] = lax.dot_general(
                two_of(hbuf.at[index], pair), dz_slim[...], along_dims, preferred_element_type=F32
            ).astype(BF16)
        settle_with(go, settle, now, span)
        return go

    slim_back(4, lambda place: z_slim[place, :], gain_t[...], shift_t[...], keep_slim, 30)

    def branch_new(chunk):
        def give(start, value):
            branch[pl.ds(start + chunk * half_rows, vsize), :] = value

        return give

    def branch_more(chunk):
        def give(start, value):
            branch[pl.ds(start + chunk * half_rows, vsize), :] += value

        return give

    def bypass_up(chunk):
        def give(start, value):
            bypass[pl.ds(start + chunk * half_rows, vsize), :] = value

        return give

    def finish_bypass():
        for chunk in range(2):
            merge_go.finish(2 + chunk, vsize, bypass_up(chunk))
        merge_go.drain()

    finish_bypass()
    thin_back(1, 4, wt, trans_row, branch_new, 30, 11).drain()

    def nine(start, value):
        place = pl.ds(start + side, vsize)
        value = value.astype(BF16).astype(F32)
        acc[1, place, :] = value
        acc[0, place, :] = pltpu.roll(value * flags[place, 4:5], vsize - 1, 0)
        acc[2, place, :] = pltpu.roll(value * flags[place, 5:6], 1, 0)

    def nine_rows(start):
        for row_tap in range(3):
            source = pl.ds(start + side - side * (row_tap - 1), vsize)
            for col_tap in range(3):
                tap = 3 * row_tap + col_tap
                value = acc[col_tap, source, :]
                if row_tap != 1:
                    column = 2 if row_tap == 0 else 3
                    value = value * flags[source, column : column + 1]
                spread[pl.ds(start, vsize), LANES * tap : LANES * (tap + 1)] = value.astype(BF16)

    def tap_back(stage, layer, offset, settle, begin_sums, now, span):
        index = 2 * layer + 1
        go = scatter(stage, 1)
        if stage == 2:
            mixed_copy.wait()
        tiles(rows, vsize, nine_rows)
        spread_out(
            go,
            lambda place: spread[place, :],
            lambda part, pair: w2[layer, pair_rows(pair), :],
            1,
            now,
            span,
        )
        for pair in range(2):
            left = two_of(hbuf.at[index], pair)
            for row_tap in range(3):
                three = lax.dot_general(
                    left,
                    spread[:, 3 * LANES * row_tap : 3 * LANES * (row_tap + 1)],
                    along_dims,
                    preferred_element_type=F32,
                ).astype(BF16)
                for col_tap in range(3):
                    row = offset + 512 * (3 * row_tap + col_tap) + 256 * pair
                    sum_big[pl.ds(row, 256), :] = three[
                        :, LANES * col_tap : LANES * (col_tap + 1)
                    ]
        begin_sums(now + 0.7 * span)
        settle_with(go, settle, now, span)
        go.drain()

    def late_sums(now):
        begin_rows(second_row[1], 2560, 0, now)
        begin_rows(second_row[1] + 2560, 2560, 1, now)

    def early_sums(now):
        begin_rows(0, 2560, 0, now)
        begin_rows(2560, 2560, 1, now)

    for layer in (1, 0):
        stage = 2 if layer == 1 else 4
        now = 41 if layer == 1 else 75
        slim_back(
            2 * layer + 1,
            lambda place: branch[place, :],
            gain_b[2 * layer + 1 : 2 * layer + 2, :],
            shift_b[2 * layer + 1 : 2 * layer + 2, :],
            nine,
            now,
        )
        tap_back(
            stage,
            layer,
            second_row[layer],
            top_up,
            late_sums if layer == 1 else early_sums,
            now,
            18,
        )
        now += 18
        slim_back(
            2 * layer,
            lambda place: z_slim[place, :],
            gain_b[2 * layer : 2 * layer + 1, :],
            shift_b[2 * layer : 2 * layer + 1, :],
            keep_slim,
            now,
        )
        thin_back(
            stage + 1,
            2 * layer,
            wf.at[layer],
            first_row[layer],
            branch_more,
            now,
            15,
        ).drain()

    norm_back(
        wide_ex[1],
        lambda place: join([branch[place, :], bypass[place, :]]),
        z_wide,
        hat_wide.at[1],
        join([gain_s[0:1, :], gain_s[1:2, :]]),
        join([shift_s[0:1, :], shift_s[1:2, :]]),
        inv_wide[1, 0:1, :],
        vec_wide.at[1],
        keep_wide,
        108,
    )
    split_go = scatter(6, 2)

    def split_terms(owner, chunk):
        def body(start):
            place = pl.ds(start + chunk * half_rows, msize)
            terms = lax.dot_general(
                dz_wide[place, :],
                ws[pl.ds(pl.multiple_of(owner * 256, 256), 256), :],
                across_dims,
                preferred_element_type=F32,
            ).astype(BF16)
            for part in range(2):
                pbuf[part, owner, place, :] = terms[:, LANES * part : LANES * (part + 1)]

        tiles(half_rows, msize, body)

    for chunk in range(2):
        split_terms(at.far, chunk)
        for part in range(2):
            split_go.far_copy(2 * part + chunk).start()
    pause(115)
    for chunk in range(2):
        split_terms(at.cross, chunk)
        for part in range(2):
            split_go.relay(2 * part + chunk, vsize)
    pause(118)
    for chunk in range(2):
        split_terms(at.mate, chunk)
        for part in range(2):
            split_go.mate_copy(2 * part + chunk).start()
    for chunk in range(2):
        split_terms(at.chan, chunk)
    for owner in range(4):
        result = lax.dot_general(
            dbuf[rows * owner : rows * (owner + 1), :], dz_wide[...], along_dims, preferred_element_type=F32
        ).astype(BF16)
        for part in range(2):
            sum_big[pl.ds(split_row + 1024 * part + 256 * owner, 256), :] = result[
                :, LANES * part : LANES * (part + 1)
            ]
    begin_rows(first_row[0], 2560, 0, 122)
    pause(122)

    def wide_up(part, chunk):
        def give(start, value):
            z_wide[
                pl.ds(start + chunk * half_rows, vsize), LANES * part : LANES * (part + 1)
            ] = value

        return give

    for chunk in range(2):
        for part in range(2):
            split_go.finish(2 * part + chunk, vsize, wide_up(part, chunk))
            pause(124 + 4 * chunk + 2 * part)
    split_go.drain()

    def keep_down(start, value):
        place = pl.ds(start + side, vsize)
        value = value.astype(BF16).astype(F32)
        moved = pltpu.roll(value * flags[place, 1:2], vsize - 1, 0)
        for half in range(2):
            lanes = slice(LANES * half, LANES * (half + 1))
            acc[half, place, :] = value[:, lanes]
            acc[2 + half, place, :] = moved[:, lanes]

    norm_back(
        wide_ex[0],
        lambda place: z_wide[place, :],
        z_wide,
        hat_wide.at[0],
        gain_d[...],
        shift_d[...],
        inv_wide[0, 0:1, :],
        vec_wide.at[0],
        keep_down,
        130,
    )

    def four_rows(start):
        place = pl.ds(start, vsize)
        here, below = pl.ds(start + side, vsize), pl.ds(start + 2 * side, vsize)
        keep = flags[below, 0:1]
        for kind in range(2):
            for half in range(2):
                lane = 256 * kind + LANES * half
                spread[place, lane : lane + LANES] = acc[2 * kind + half, here, :].astype(BF16)
                spread[place, 512 + lane : 512 + lane + LANES] = (
                    acc[2 * kind + half, below, :] * keep
                ).astype(BF16)

    tiles(rows, vsize, four_rows)

    def version(row_tap, col_tap):
        return 256 * (2 * (row_tap == 0) + (col_tap == 0))

    def phase_of(row_tap, col_tap):
        return 2 * (row_tap != 1) + (col_tap != 1)

    now = 137.0
    taken = 0
    for tap in range(9):
        row_tap, col_tap = tap // 3, tap % 3
        lane = version(row_tap, col_tap)
        phase = phase_of(row_tap, col_tap)
        for pair in range(2):
            left = join([fbuf[2 * pair + step, phase] for step in range(2)])
            sum_down[pl.ds(512 * tap + 256 * pair, 256), :] = lax.dot_general(
                left, spread[:, lane : lane + 256], along_dims, preferred_element_type=F32
            ).astype(BF16)
        now += 0.5
        if tap + 1 in tap_ends:
            low = 512 * (([0, *tap_ends])[tap_ends.index(tap + 1)])
            size = 512 * (tap + 1) - low
            piece = pl.ds(low, size)
            room = landing_rows(size, batch_count)
            turn = tap_ends.index(tap + 1) % 3 == 1
            begin(sum_down.at[piece], dbuf.at[pl.ds(taken, room)], int(turn), down_out.at[piece], now)
            taken += room
            pause(now)

    down_go = Scatter(
        at,
        (
            lambda owner, phase: hbuf.at[phase, owner],
            lambda block, phase: jbuf.at[block, phase],
            lambda phase: rcross_d.at[phase],
            lambda phase: feat.at[pl.ds(phase * rows, rows)],
        ),
        tsend,
        trecv,
        base[0],
    )
    order = (3, 2, 1, 0)

    def feature_terms(phase, pair):
        row_taps = (0, 2) if phase // 2 else (1,)
        col_taps = (0, 2) if phase % 2 else (1,)

        def body(start):
            place = pl.ds(start, msize)
            total = None
            for row_tap in row_taps:
                for col_tap in col_taps:
                    lane = version(row_tap, col_tap)
                    one = lax.dot_general(
                        spread[place, lane : lane + 256],
                        wd[3 * row_tap + col_tap, pair_rows(pair), :],
                        across_dims,
                        preferred_element_type=F32,
                    )
                    total = one if total is None else total + one
            terms = total.astype(BF16)
            for step in range(2):
                hbuf[phase, 2 * pair + step, place, :] = terms[:, LANES * step : LANES * (step + 1)]

        tiles(rows, msize, body)

    for phase in order:
        feature_terms(phase, 1 - at.pair)
        down_go.far_copy(phase).start()
        now += 1.5
        pause(now)
    for phase in order:
        down_go.relay(phase, vsize)
        feature_terms(phase, at.pair)
        down_go.mate_copy(phase).start()
        now += 1.7
        pause(now)

    def place_back(phase):
        row_par, col_par = phase // 2, phase % 2

        def give(start, value):
            line = start // side
            for step in range(vsize // side):
                feat_grad[2 * (line + step) + row_par, pl.ds(col_par, side, stride=2), :] = value[
                    side * step : side * (step + 1), :
                ]

        return give

    arriving = [(147 + 5.9 * turn + 8.5, phase) for turn, phase in enumerate(order)]
    while queue or held or arriving:
        resume(now)
        made = min(queue, key=lambda one: one.due) if queue else None
        if arriving and (made is None or arriving[0][0] <= made.due):
            due, phase = arriving.pop(0)
            now = max(now, due)
            down_go.finish(phase, vsize, place_back(phase))
        else:
            now = max(now, made.due)
            step_on(made, now)
    down_go.drain()
    for made in (*wide_ex, *slim_ex):
        made.drain()


def section_call(batch_count, side, flags, vectors, feat, grad_in, weights):
    rows = grad_in.shape[0]
    wide = 2 * LANES
    hbm = pl.BlockSpec(memory_space=pl.ANY)
    vmem = pl.BlockSpec(memory_space=pltpu.VMEM)
    dma = pltpu.SemaphoreType.DMA
    shape = jax.ShapeDtypeStruct
    bits = batch_count.bit_length() - 1
    near = list(range(bits))
    turned = [1, 0, *near[2:]] if bits > 1 else near
    sums = [
        shape((1024, wide), BF16),
        shape((big_rows, LANES), BF16),
        shape((4608, wide), BF16),
    ]
    slots = [
        pltpu.VMEM((3, batch_count, 8, wide), F32),
        pltpu.VMEM((5, batch_count, 8, LANES), F32),
    ]
    turns = [dma((3, batch_count)), dma((5, batch_count))]
    scratch = [
        pltpu.VMEM(feat.shape, BF16),
        pltpu.VMEM((rows, wide), BF16),
        pltpu.VMEM((9, 512, wide), BF16),
        pltpu.VMEM((1024, wide), BF16),
        pltpu.VMEM((2, 512, LANES), BF16),
        pltpu.VMEM((2, 512, 9 * LANES), BF16),
        pltpu.VMEM((512, LANES), BF16),
        pltpu.VMEM((1024, wide), BF16),
        pltpu.VMEM((4, 4, rows, LANES), BF16),
        pltpu.VMEM((4 * rows, wide), BF16),
        pltpu.VMEM((5, 4, rows, LANES), BF16),
        pltpu.VMEM((2, 4, rows, LANES), BF16),
        pltpu.VMEM((3, rows, wide), F32),
        pltpu.VMEM((5, rows, LANES), F32),
        pltpu.VMEM((3, 8, wide), F32),
        pltpu.VMEM((5, 8, LANES), F32),
        pltpu.VMEM((4, rows + 2 * side, LANES), F32),
        pltpu.VMEM((rows, wide), F32),
        pltpu.VMEM((rows, LANES), F32),
        pltpu.VMEM((rows, LANES), F32),
        pltpu.VMEM((rows, LANES), F32),
        pltpu.VMEM((rows, 9 * LANES), BF16),
        pltpu.VMEM((rows, wide), BF16),
        pltpu.VMEM((rows, LANES), BF16),
        pltpu.VMEM((2, 4, rows, LANES), BF16),
        pltpu.VMEM((2, 2, 2, rows, LANES), BF16),
        pltpu.VMEM((2, 2, rows, LANES), BF16),
        pltpu.VMEM((2, rows, LANES), BF16),
        pltpu.VMEM((4, rows, LANES), BF16),
        *[pltpu.VMEM(one.shape, one.dtype) for one in sums],
        pltpu.VMEM((landing_rows(big_rows, batch_count), LANES), BF16),
        *slots,
        *turns,
        *turns,
        dma((60,)),
        dma((60,)),
        dma((72,)),
        dma((72,)),
        dma((15 * 2 * bits,)),
        dma((15 * 2 * bits,)),
        dma((40,)),
        dma((16,)),
    ]
    return pl.pallas_call(
        functools.partial(section_kernel, batch_count, side, (near, turned)),
        out_shape=[
            shape((rows, wide), BF16),
            shape((2 * rows // side, 2 * side, LANES), F32),
            shape((3, 8, wide), F32),
            shape((5, 8, LANES), F32),
            *sums,
        ],
        in_specs=[vmem] * 11 + [hbm] * 8,
        out_specs=[hbm] + [vmem] * 3 + [hbm] * 3,
        scratch_shapes=scratch,
        compiler_params=pltpu.CompilerParams(
            collective_id=0, has_side_effects=True, vmem_limit_bytes=VMEM_LIMIT
        ),
    )(flags, *vectors, feat, grad_in, *weights)


def local(
    features,
    tile_split,
    out_grad,
    w_down,
    gain_down,
    shift_down,
    w_split,
    gain_split,
    shift_split,
    w_first,
    w_second,
    gain_block,
    shift_block,
    w_trans,
    gain_trans,
    shift_trans,
    w_merge,
    gain_merge,
    shift_merge,
):
    side = out_grad.shape[1]
    count = lax.axis_size("batch")
    flags = mask_columns(tile_split, side)

    def row(vec):
        return vec.reshape(1, -1)

    weights = (
        w_down.reshape(9, w_down.shape[2], w_down.shape[3]),
        w_split,
        w_first,
        w_second.reshape(2, 9, w_second.shape[3], w_second.shape[4]),
        w_trans,
        w_merge,
    )
    vectors = (
        row(gain_down),
        row(shift_down),
        gain_split,
        shift_split,
        gain_block.reshape(4, -1),
        shift_block.reshape(4, -1),
        row(gain_trans),
        row(shift_trans),
        row(gain_merge),
        row(shift_merge),
    )
    mixed, feat_grad, vec_wide, vec_slim, merge, big, down = section_call(
        count,
        side,
        flags,
        vectors,
        features.reshape(-1, features.shape[3]),
        out_grad.reshape(-1, out_grad.shape[3]),
        weights,
    )
    rows = w_trans.shape[0]
    two = second_row[0]
    second_grad = big[two : two + 18 * rows].reshape(w_second.shape)
    first_grad = jnp.stack([big[low : low + rows] for low in first_row])
    return (
        mixed.reshape(out_grad.shape),
        feat_grad.reshape(features.shape),
        down.reshape(w_down.shape).astype(F32),
        vec_wide[0, 1],
        vec_wide[0, 0],
        big[split_row:].reshape(w_split.shape).astype(F32),
        vec_wide[1, 1].reshape(gain_split.shape),
        vec_wide[1, 0].reshape(shift_split.shape),
        first_grad.astype(F32),
        second_grad.astype(F32),
        vec_slim[:4, 1].reshape(gain_block.shape),
        vec_slim[:4, 0].reshape(shift_block.shape),
        big[trans_row : trans_row + rows].astype(F32),
        vec_slim[4, 1],
        vec_slim[4, 0],
        merge.astype(F32),
        vec_wide[2, 1],
        vec_wide[2, 0],
    )


def solution(mesh):
    placed = (
        P("batch", None, None, "chan"),
        P("batch", None),
        P("batch", None, None, "chan"),
        P(None, None, None, "chan"),
        P("chan"),
        P("chan"),
        P(None, None, "chan"),
        P(None, "chan"),
        P(None, "chan"),
        P(None, None, "chan"),
        P(None, None, None, None, "chan"),
        P(None, None, "chan"),
        P(None, None, "chan"),
        P(None, "chan"),
        P("chan"),
        P("chan"),
        P(None, "chan"),
        P("chan"),
        P("chan"),
    )
    return jax.shard_map(
        local,
        mesh=mesh,
        in_specs=placed,
        out_specs=(
            P("batch", None, None, "chan"),
            P("batch", None, None, "chan"),
            P(None, None, None, "chan"),
            P("chan"),
            P("chan"),
            P(None, None, "chan"),
            P(None, "chan"),
            P(None, "chan"),
            P(None, None, "chan"),
            P(None, None, None, None, "chan"),
            P(None, None, "chan"),
            P(None, None, "chan"),
            P(None, "chan"),
            P("chan"),
            P("chan"),
            P(None, "chan"),
            P("chan"),
            P("chan"),
        ),
        check_vma=False,
    )
```

```python
import functools

import jax
import jax.numpy as jnp
from jax import lax
from jax.experimental import pallas as pl
from jax.experimental.pallas import tpu as pltpu
from jax.sharding import PartitionSpec as P

epsilon = 1e-05
F32 = jnp.float32
BF16 = jnp.bfloat16
MESH = pl.DeviceIdType.MESH
LANES = 128
VMEM_LIMIT = 60 * 1024 * 1024


def tap_masks(splits, side_len, stride):
    places = jnp.arange(side_len, dtype=jnp.int32)
    offset = jnp.arange(3, dtype=jnp.int32) - 1
    source = stride * places[:, None] + offset[None, :]
    inside = (source >= 0) & (source < stride * side_len)

    def along_axis(cut_at):
        cut_at = cut_at[:, None, None]
        same_tile = (source[None] < stride * cut_at) == (places[None, :, None] < cut_at)
        return (inside[None] & same_tile).astype(jnp.float32)

    return (along_axis(splits[:, 0]), along_axis(splits[:, 1]))


def mask_columns(tile_split, side_len):
    number = tile_split.shape[0]
    rows_two, cols_two = tap_masks(tile_split, side_len, 2)
    rows_one, cols_one = tap_masks(tile_split, side_len, 1)

    def by_row(flags):
        return jnp.broadcast_to(flags[:, :, None], (number, side_len, side_len)).reshape(-1)

    def by_col(flags):
        return jnp.broadcast_to(flags[:, None, :], (number, side_len, side_len)).reshape(-1)

    stacked = jnp.stack(
        [
            by_row(rows_two[:, :, 0]),
            by_col(cols_two[:, :, 0]),
            by_row(rows_one[:, :, 0]),
            by_row(rows_one[:, :, 2]),
            by_col(cols_one[:, :, 0]),
            by_col(cols_one[:, :, 2]),
        ],
        axis=1,
    )
    return jnp.pad(stacked, ((side_len, side_len), (0, 2)))


class Places:
    def __init__(self, batch_count):
        self.count = batch_count
        self.chan = lax.axis_index("chan")
        self.batch = lax.axis_index("batch")
        self.mate = self.chan + 1 - 2 * lax.rem(self.chan, 2)
        self.cross = lax.rem(self.chan + 2, 4)
        self.far = lax.rem(self.mate + 2, 4)
        self.pair = self.chan // 2

    def greet(self):
        barrier = pltpu.get_barrier_semaphore()
        for partner in (self.mate, self.cross):
            pl.semaphore_signal(
                barrier, inc=1, device_id={"chan": partner}, device_id_type=MESH
            )

        def hail(step, carry):
            peer = lax.rem(self.batch + step, self.count)
            pl.semaphore_signal(barrier, inc=1, device_id={"batch": peer}, device_id_type=MESH)
            return carry

        lax.fori_loop(1, self.count, hail, 0)
        pl.semaphore_wait(barrier, 2 + self.count - 1)


class Gather:
    def __init__(self, places, view, chunks, send, recv, base):
        self.at, self.view, self.chunks = places, view, chunks
        self.send, self.recv, self.base = send, recv, base

    def copy(self, owner, chunk, kind, partner):
        ref = self.view(owner, chunk)
        slot = self.base + 3 * chunk + kind
        return pltpu.make_async_remote_copy(
            src_ref=ref,
            dst_ref=ref,
            send_sem=self.send.at[slot],
            recv_sem=self.recv.at[slot],
            device_id={"chan": partner},
            device_id_type=MESH,
        )

    def start(self, chunk):
        self.copy(self.at.chan, chunk, 1, self.at.cross).start()
        self.copy(self.at.chan, chunk, 0, self.at.mate).start()

    def wait_mate(self, chunk):
        self.copy(self.at.mate, chunk, 0, self.at.mate).wait_recv()

    def forward(self, chunk):
        self.copy(self.at.cross, chunk, 1, self.at.cross).wait_recv()
        self.copy(self.at.cross, chunk, 2, self.at.mate).start()

    def wait_far(self, chunk):
        self.copy(self.at.far, chunk, 2, self.at.mate).wait_recv()

    def drain(self):
        for chunk in range(self.chunks):
            self.copy(self.at.chan, chunk, 0, self.at.mate).wait_send()
            self.copy(self.at.chan, chunk, 1, self.at.cross).wait_send()
            self.copy(self.at.cross, chunk, 2, self.at.mate).wait_send()


class Exchange:
    def __init__(self, places, slots, send, recv):
        self.at, self.slots, self.send, self.recv = places, slots, send, recv

    def copy(self, step, owner, peer):
        ref = self.slots.at[owner]
        return pltpu.make_async_remote_copy(
            src_ref=ref,
            dst_ref=ref,
            send_sem=self.send.at[step],
            recv_sem=self.recv.at[step],
            device_id={"batch": peer},
            device_id_type=MESH,
        )

    def push(self, block):
        at = self.at
        self.slots[at.batch] = block

        def start(step, carry):
            self.copy(step, at.batch, lax.rem(at.batch + step, at.count)).start()
            return carry

        lax.fori_loop(1, at.count, start, 0)

    def take(self):
        at = self.at

        def arrive(step, carry):
            owner = lax.rem(at.batch + at.count - step, at.count)
            self.copy(step, owner, owner).wait_recv()
            return carry

        lax.fori_loop(1, at.count, arrive, 0)

    def drain(self):
        at = self.at

        def sent(step, carry):
            self.copy(step, at.batch, lax.rem(at.batch + step, at.count)).wait_send()
            return carry

        lax.fori_loop(1, at.count, sent, 0)


def two_rows(first, second):
    return jnp.where(
        lax.broadcasted_iota(jnp.int32, (8, first.shape[1]), 0) == 0, first, second
    )


def fold(values):
    return jnp.sum(values.reshape(values.shape[0] // 8, 8, values.shape[1]), axis=0)


def tiles(total, size, body):
    def step(index, carry):
        body(pl.multiple_of(index * size, size))
        return carry

    lax.fori_loop(0, total // size, step, 0)


def mish_parts(before):
    grown = jnp.exp(jnp.minimum(before, 20.0))
    top = grown * (grown + 2.0)
    return grown, top


def join(halves):
    return jnp.concatenate(halves, axis=1)


CHUNKS = 4


class Norms:
    def __init__(self, exchange, rows, pixels):
        self.exchange, self.rows, self.pixels = exchange, rows, pixels

    def statistics(self, z_ref):
        rows, width = self.rows, z_ref.shape[1]
        size = 96

        def add_up(index, total):
            return total + fold(z_ref[pl.ds(pl.multiple_of(index * size, size), size), :])

        zero = jnp.zeros((8, width), F32)
        total = lax.fori_loop(0, rows // size, add_up, zero)
        mean = jnp.sum(total, axis=0, keepdims=True) / rows

        def spread(index, total):
            away = z_ref[pl.ds(pl.multiple_of(index * size, size), size), :] - mean
            return total + fold(away * away)

        total = lax.fori_loop(0, rows // size, spread, zero)
        square = jnp.sum(total, axis=0, keepdims=True)
        self.exchange.push(two_rows(mean, square))
        self.exchange.take()
        slots, count = self.exchange.slots, self.exchange.at.count

        def means(index, total):
            return total + slots[index]

        whole = lax.fori_loop(0, count, means, zero)[0:1] / count

        def squares(index, total):
            block = slots[index]
            away = block[0:1] - whole
            return total + block[1:2] + rows * (away * away)

        variance = lax.fori_loop(0, count, squares, jnp.zeros((1, width), F32)) / self.pixels
        return whole, lax.rsqrt(variance + epsilon)


class Scatter:
    def __init__(self, places, views, send, recv, base):
        self.at = places
        self.term, self.from_mate, self.from_cross, self.across = views
        self.send, self.recv, self.base = send, recv, base
        self.used = []

    def copy(self, source, target, chunk, kind, partner):
        slot = self.base + 3 * chunk + kind
        return pltpu.make_async_remote_copy(
            src_ref=source,
            dst_ref=target,
            send_sem=self.send.at[slot],
            recv_sem=self.recv.at[slot],
            device_id={"chan": partner},
            device_id_type=MESH,
        )

    def far_copy(self, chunk):
        return self.copy(
            self.term(self.at.far, chunk), self.from_mate(0, chunk), chunk, 0, self.at.mate
        )

    def mate_copy(self, chunk):
        return self.copy(
            self.term(self.at.mate, chunk), self.from_mate(1, chunk), chunk, 1, self.at.mate
        )

    def cross_copy(self, chunk):
        return self.copy(self.across(chunk), self.from_cross(chunk), chunk, 2, self.at.cross)

    def relay(self, chunk, size):
        self.far_copy(chunk).wait_recv()
        mine, theirs, both = (
            self.term(self.at.cross, chunk),
            self.from_mate(0, chunk),
            self.across(chunk),
        )

        def add(start):
            place = pl.ds(start, size)
            both[place, :] = (mine[place, :].astype(F32) + theirs[place, :].astype(F32)).astype(
                BF16
            )

        tiles(mine.shape[0], size, add)
        self.cross_copy(chunk).start()

    def finish(self, chunk, size, give):
        self.mate_copy(chunk).wait_recv()
        self.cross_copy(chunk).wait_recv()
        parts = (self.term(self.at.chan, chunk), self.from_mate(1, chunk), self.from_cross(chunk))

        def add(start):
            place = pl.ds(start, size)
            first, second, third = [part[place, :].astype(F32) for part in parts]
            give(start, first + second + third)

        tiles(parts[0].shape[0], size, add)
        self.used.append(chunk)

    def drain(self):
        for chunk in self.used:
            self.far_copy(chunk).wait_send()
            self.mate_copy(chunk).wait_send()
            self.cross_copy(chunk).wait_send()


def tile_of(rows):
    return max(size for size in range(8, 321, 8) if rows % size == 0)


class Links:
    rate, latency = 50000.0, 2.5

    def __init__(self):
        self.free = {}

    def plan(self, now, bit, size):
        span = size / self.rate
        loads = {2: ((1, span), (2, 2 * span))}.get(bit, ((bit, span),))
        return {link: max(now, self.free.get(link, 0.0)) + load for link, load in loads}


class Reducer:
    def __init__(self, places, buf, landing, out, order, sems, base, own_sem):
        self.at, self.buf, self.landing, self.out = places, buf, landing, out
        self.order, (self.send, self.recv), self.base = order, sems, base
        self.own_sem = own_sem
        self.low, self.size, self.taken, self.step = 0, buf.shape[0], 0, 0
        self.due = 0.0

    def next_load(self):
        steps = len(self.order)
        if self.step < steps:
            bit, size = self.order[self.step], self.size // 2
        else:
            bit, size = self.order[2 * steps - 1 - self.step], self.size
        return bit, 2 * size * self.buf.shape[1]

    def partner(self, bit):
        side = lax.rem(self.at.batch // (1 << bit), 2)
        return side, self.at.batch + (1 - 2 * side) * (1 << bit)

    def copy(self, source, target, partner):
        return pltpu.make_async_remote_copy(
            src_ref=source,
            dst_ref=target,
            send_sem=self.send.at[self.base + self.step],
            recv_sem=self.recv.at[self.base + self.step],
            device_id={"batch": partner},
            device_id_type=MESH,
        )

    def rows(self, low, size):
        return pl.ds(pl.multiple_of(low, 8), size)

    def launch(self):
        steps = len(self.order)
        if self.step < steps:
            side, partner = self.partner(self.order[self.step])
            half = self.size // 2
            gone = self.low + (1 - side) * half
            self.flying = self.copy(
                self.buf.at[self.rows(gone, half)],
                self.landing.at[pl.ds(self.taken, half)],
                partner,
            )
            self.kept = self.low + side * half
            self.flying.start()
            return
        side, partner = self.partner(self.order[2 * steps - 1 - self.step])
        target = self.out.at[self.rows(self.low, self.size)]
        source = target
        if self.step == steps:
            source = self.buf.at[self.rows(self.low, self.size)]
            self.own = pltpu.make_async_copy(source, target, self.own_sem)
            self.own.start()
        self.flying = self.copy(source, target, partner)
        self.flying.start()
        other = self.out.at[self.rows(self.low + (1 - 2 * side) * self.size, self.size)]
        self.coming = self.copy(other, other, partner)
        self.next_low = self.low - side * self.size

    def advance(self):
        steps = len(self.order)
        if self.step < steps:
            self.flying.wait()
            half = self.size // 2
            size = tile_of(half)
            taken, kept = self.taken, self.kept

            def add(start):
                place = self.rows(kept + start, size)
                self.buf[place, :] = (
                    self.buf[place, :].astype(F32)
                    + self.landing[pl.ds(taken + start, size), :].astype(F32)
                ).astype(BF16)

            tiles(half, size, add)
            self.low, self.size, self.taken = kept, half, taken + half
        else:
            self.coming.wait_recv()
            self.flying.wait_send()
            if self.step == steps:
                self.own.wait()
            self.low, self.size = self.next_low, 2 * self.size
        self.step += 1
        return self.step == 2 * steps


first_row = (10240, 0)
second_row = (512, 5120)
trans_row = 9728
split_row = 10752
tap_ends = (2, 5, 7, 9)
big_rows = 12800


def landing_rows(rows, batch_count):
    return rows - rows // batch_count


def section_kernel(
    batch_count,
    side,
    orders,
    flags,
    gain_d,
    shift_d,
    gain_s,
    shift_s,
    gain_b,
    shift_b,
    gain_t,
    shift_t,
    gain_m,
    shift_m,
    feat_in,
    grad_in,
    wd_in,
    ws_in,
    wf_in,
    w2_in,
    wt_in,
    wm_in,
    mixed,
    feat_grad,
    vec_wide,
    vec_slim,
    merge_out,
    big_out,
    down_out,
    feat,
    grad,
    wd,
    ws,
    wf,
    w2,
    wt,
    wm,
    fbuf,
    dbuf,
    hbuf,
    jbuf,
    hat_wide,
    hat_slim,
    inv_wide,
    inv_slim,
    acc,
    z_wide,
    z_slim,
    branch,
    bypass,
    spread,
    dz_wide,
    dz_slim,
    pbuf,
    rmate,
    rcross,
    across,
    rcross_d,
    sum_merge,
    sum_big,
    sum_down,
    land_big,
    slots_wide,
    slots_slim,
    wide_sem,
    slim_sem,
    wide_rsem,
    slim_rsem,
    send,
    recv,
    tsend,
    trecv,
    bsend,
    brecv,
    wsem,
    osem,
):
    raw = feat_grad
    at = Places(batch_count)
    me = at.chan
    rows = z_wide.shape[0]
    half_rows = rows // 2
    bsize = 192
    parts = CHUNKS
    part_rows = rows // parts
    pixels = rows * batch_count
    area = side * side

    weight_copies = {}

    def bring(name, pairs):
        copies = []
        for source, target in pairs:
            slot = sum(len(done) for done in weight_copies.values()) + len(copies)
            copies.append(pltpu.make_async_copy(source, target, wsem.at[slot]))
        weight_copies[name] = copies
        for copy in copies:
            copy.start()

    def have(name):
        for copy in weight_copies[name]:
            copy.wait()

    bring("features", [(feat_in, feat)])
    bring("down", [(wd_in.at[tap], wd.at[tap]) for tap in range(9)])
    bring("split", [(ws_in.at[part], ws.at[:, pl.ds(LANES * part, LANES)]) for part in range(2)])
    for layer in range(2):
        bring(f"first{layer}", [(wf_in.at[layer], wf.at[layer])])
        bring(
            f"second{layer}",
            [
                (w2_in.at[layer, tap], w2.at[layer, :, pl.ds(LANES * tap, LANES)])
                for tap in range(9)
            ],
        )
    bring("trans", [(wt_in, wt)])
    bring("merge", [(wm_in, wm)])
    bring("grad", [(grad_in, grad)])

    base = [0]

    def gather(view, chunks):
        made = Gather(at, view, chunks, send, recv, base[0])
        base[0] += 3 * chunks
        return made

    def by_half(ref):
        return lambda owner, chunk: ref.at[owner, pl.ds(chunk * part_rows, part_rows)]

    feat_go = gather(lambda owner, phase: fbuf.at[owner, phase], 4)
    def down_rows(owner, start, size):
        return pl.ds(pl.multiple_of(owner * rows + start, 16), size)

    down_go = gather(
        lambda owner, chunk: dbuf.at[down_rows(owner, chunk * part_rows, part_rows)], parts
    )
    half_go = [gather(by_half(hbuf.at[index]), parts) for index in range(5)]
    side_go = gather(by_half(jbuf.at[1]), parts)
    top_go = gather(by_half(jbuf.at[0]), parts)
    wide_ex = [
        Exchange(at, slots_wide.at[index], wide_sem.at[index], wide_rsem.at[index])
        for index in range(3)
    ]
    slim_ex = [
        Exchange(at, slots_slim.at[index], slim_sem.at[index], slim_rsem.at[index])
        for index in range(5)
    ]

    at.greet()

    have("features")

    for phase in range(4):
        row_par, col_par = phase // 2, phase % 2

        if col_par == 0:

            def widen(index, carry):
                line = pl.multiple_of((2 * index + row_par) * 2 * side, 16)
                raw[index] = feat[pl.ds(line, 2 * side), :].astype(F32)
                return carry

            lax.fori_loop(0, raw.shape[0] // 2, widen, 0)

        def pick(start):
            both = [
                raw[2 * (start // (2 * side)) + step, pl.ds(col_par, side, stride=2), :]
                for step in range(2)
            ]
            fbuf[me, phase, pl.ds(start, 2 * side), :] = jnp.concatenate(both, axis=0).astype(BF16)

        tiles(rows, 2 * side, pick)
        feat_go.start(phase)

    acc[...] = jnp.zeros_like(acc)
    have("down")

    def down_pair(phase, pair):
        row_par, col_par = phase // 2, phase % 2
        row_taps = (0, 2) if row_par else (1,)
        col_taps = (0, 2) if col_par else (1,)
        size = 192

        def body(start):
            block = join(
                [fbuf[2 * pair + step, phase, pl.ds(start, size), :] for step in range(2)]
            )
            for row_tap in row_taps:
                for col_tap in col_taps:
                    part = jnp.dot(
                        block,
                        wd[3 * row_tap + col_tap, pl.ds(pl.multiple_of(pair * 256, 256), 256), :],
                        preferred_element_type=F32,
                    )
                    place = pl.ds(start + (2 * side if row_tap == 0 else side), size)
                    if row_tap == 0:
                        part = part * flags[place, 0:1]
                    kind = 1 if col_tap == 0 else 0
                    for half in range(2):
                        acc[2 * kind + half, place, :] += part[:, LANES * half : LANES * (half + 1)]

        tiles(rows, size, body)

    for phase in range(4):
        feat_go.wait_mate(phase)
        down_pair(phase, at.pair)
        feat_go.forward(phase)
    for phase in range(4):
        feat_go.wait_far(phase)
        down_pair(phase, 1 - at.pair)

    vsize = 4 * side

    def settle_down(start):
        place = pl.ds(start + side, vsize)
        for half in range(2):
            z_wide[pl.ds(start, vsize), LANES * half : LANES * (half + 1)] = acc[
                half, place, :
            ] + flags[place, 1:2] * pltpu.roll(acc[2 + half, place, :], 1, 0)

    tiles(rows, vsize, settle_down)

    def activate(exchange, z_ref, hat_ref, gain, shift, inv_ref, give, begin):
        mean, inverse = Norms(exchange, rows, pixels).statistics(z_ref)
        inv_ref[...] = jnp.broadcast_to(inverse, inv_ref.shape)

        def body(start):
            place = pl.ds(start, vsize)
            normed = (z_ref[place, :] - mean) * inverse
            hat_ref[place, :] = normed
            before = normed * gain + shift
            _, top = mish_parts(before)
            give(start, before * (top / (top + 2.0)))

        for chunk in range(parts):

            def inner(start):
                body(start + chunk * part_rows)

            tiles(part_rows, vsize, inner)
            begin(chunk)

    def keep_down(start, value):
        dbuf[down_rows(me, start, vsize), :] = value.astype(BF16)

    activate(
        wide_ex[0], z_wide, hat_wide.at[0], gain_d[...], shift_d[...], inv_wide.at[0], keep_down,
        down_go.start,
    )
    have("split")

    msize = max(size for size in (288, 192) if part_rows % size == 0)

    def split_block(owner, chunk, first):
        def body(start):
            place = pl.ds(start + chunk * part_rows, msize)
            part = jnp.dot(
                dbuf[down_rows(owner, start + chunk * part_rows, msize), :],
                ws[pl.ds(pl.multiple_of(owner * 256, 256), 256), :],
                preferred_element_type=F32,
            )
            if first:
                z_wide[place, :] = part
            else:
                z_wide[place, :] += part

        tiles(part_rows, msize, body)

    for chunk in range(parts):
        split_block(me, chunk, True)
    for chunk in range(parts):
        down_go.wait_mate(chunk)
        split_block(at.mate, chunk, False)
    for chunk in range(parts):
        down_go.forward(chunk)
        split_block(at.cross, chunk, False)
    for chunk in range(parts):
        down_go.wait_far(chunk)
        split_block(at.far, chunk, False)

    def keep_split(start, value):
        place = pl.ds(start, vsize)
        branch[place, :] = value[:, :LANES]
        hbuf[0, me, place, :] = value[:, :LANES].astype(BF16)
        jbuf[1, me, place, :] = value[:, LANES:].astype(BF16)

    activate(
        wide_ex[1],
        z_wide,
        hat_wide.at[1],
        join([gain_s[0:1, :], gain_s[1:2, :]]),
        join([shift_s[0:1, :], shift_s[1:2, :]]),
        inv_wide.at[1],
        keep_split,
        half_go[0].start,
    )
    for chunk in range(parts):
        side_go.start(chunk)

    def two_of(ref, pair, place):
        return join([ref[2 * pair + step, place, :] for step in range(2)])

    def thin_pair(source, weight, pair, chunk, first):
        def body(start):
            place = pl.ds(start + chunk * part_rows, msize)
            part = jnp.dot(
                two_of(source, pair, place),
                weight[pl.ds(pl.multiple_of(pair * 256, 256), 256), :],
                preferred_element_type=F32,
            )
            if first:
                z_slim[place, :] = part
            else:
                z_slim[place, :] += part

        tiles(part_rows, msize, body)

    def thin_conv(index, weight):
        source, go = hbuf.at[index], half_go[index]
        for chunk in range(parts):
            go.wait_mate(chunk)
            thin_pair(source, weight, at.pair, chunk, True)
        for chunk in range(parts):
            go.forward(chunk)
        for chunk in range(parts):
            go.wait_far(chunk)
            thin_pair(source, weight, 1 - at.pair, chunk, False)

    def tap_pair(source, weight, pair, chunk):
        def body(start):
            begin = start + chunk * part_rows
            part = jnp.dot(
                two_of(source, pair, pl.ds(begin, msize)),
                weight[pl.ds(pl.multiple_of(pair * 256, 256), 256), :],
                preferred_element_type=F32,
            )
            for col_tap in range(3):
                for row_tap in range(3):
                    tap = 3 * row_tap + col_tap
                    piece = part[:, LANES * tap : LANES * (tap + 1)]
                    place = pl.ds(begin + side - side * (row_tap - 1), msize)
                    if row_tap != 1:
                        column = 2 if row_tap == 0 else 3
                        piece = piece * flags[place, column : column + 1]
                    acc[col_tap, place, :] += piece

        tiles(part_rows, msize, body)

    def tap_conv(index, weight):
        source, go = hbuf.at[index], half_go[index]
        acc[0:3] = jnp.zeros((3, *acc.shape[1:]), F32)
        for chunk in range(parts):
            go.wait_mate(chunk)
            tap_pair(source, weight, at.pair, chunk)
        for chunk in range(parts):
            go.forward(chunk)
        for chunk in range(parts):
            go.wait_far(chunk)
            tap_pair(source, weight, 1 - at.pair, chunk)

        def settle(start):
            place = pl.ds(start + side, vsize)
            z_slim[pl.ds(start, vsize), :] = (
                acc[1, place, :]
                + flags[place, 4:5] * pltpu.roll(acc[0, place, :], 1, 0)
                + flags[place, 5:6] * pltpu.roll(acc[2, place, :], vsize - 1, 0)
            )

        tiles(rows, vsize, settle)

    def slim_act(index, gain, shift, give, begin):
        activate(
            slim_ex[index], z_slim, hat_slim.at[index], gain, shift, inv_slim.at[index], give, begin
        )

    for layer in range(2):
        have(f"first{layer}")
        thin_conv(2 * layer, wf.at[layer])

        def keep_inner(start, value):
            place = pl.ds(start, vsize)
            hbuf[2 * layer + 1, me, place, :] = value.astype(BF16)

        slim_act(
            2 * layer,
            gain_b[2 * layer : 2 * layer + 1, :],
            shift_b[2 * layer : 2 * layer + 1, :],
            keep_inner,
            half_go[2 * layer + 1].start,
        )
        have(f"second{layer}")
        tap_conv(2 * layer + 1, w2.at[layer])

        def keep_branch(start, value):
            place = pl.ds(start, vsize)
            total = branch[place, :] + value
            branch[place, :] = total
            hbuf[2 * layer + 2, me, place, :] = total.astype(BF16)

        slim_act(
            2 * layer + 1,
            gain_b[2 * layer + 1 : 2 * layer + 2, :],
            shift_b[2 * layer + 1 : 2 * layer + 2, :],
            keep_branch,
            half_go[2 * layer + 2].start,
        )
        if layer == 0:
            for chunk in range(parts):
                side_go.forward(chunk)
    have("trans")
    thin_conv(4, wt)

    def keep_top(start, value):
        place = pl.ds(start, vsize)
        jbuf[0, me, place, :] = value.astype(BF16)

    slim_act(4, gain_t[...], shift_t[...], keep_top, top_go.start)
    have("merge")

    def merge_pair(part_index, pair, chunk, first):
        def body(start):
            place = pl.ds(start + chunk * part_rows, msize)
            part = jnp.dot(
                two_of(jbuf.at[part_index], pair, place),
                wm[pl.ds(pl.multiple_of(part_index * 512 + pair * 256, 256), 256), :],
                preferred_element_type=F32,
            )
            if first:
                z_wide[place, :] = part
            else:
                z_wide[place, :] += part

        tiles(part_rows, msize, body)

    for chunk in range(parts):
        side_go.wait_mate(chunk)
        merge_pair(1, at.pair, chunk, True)
    for chunk in range(parts):
        side_go.wait_far(chunk)
        merge_pair(1, 1 - at.pair, chunk, False)
    for chunk in range(parts):
        top_go.wait_mate(chunk)
        merge_pair(0, at.pair, chunk, False)
    for chunk in range(parts):
        top_go.forward(chunk)
    for chunk in range(parts):
        top_go.wait_far(chunk)
        merge_pair(0, 1 - at.pair, chunk, False)

    def keep_mixed(start, value):
        place = pl.ds(start, vsize)
        spread[place, 0:256] = value.astype(BF16)

    activate(
        wide_ex[2], z_wide, hat_wide.at[2], gain_m[...], shift_m[...], inv_wide.at[2], keep_mixed,
        lambda chunk: None,
    )

    for made in (feat_go, down_go, *half_go, side_go, top_go):
        made.drain()
    for made in (*wide_ex, *slim_ex):
        made.drain()
    mixed_copy = pltpu.make_async_copy(spread.at[:, pl.ds(0, 256)], mixed, osem.at[15])
    mixed_copy.start()

    wide_ex = [wide_ex[index] for index in (2, 1, 0)]

    base = [0]

    def scatter(stage, parts):
        kit = stage % 2

        def cut(ref):
            return lambda *where: ref.at[(*where[:-1], pl.ds(where[-1] * half_rows, half_rows))]

        def term(owner, chunk):
            return cut(pbuf)(chunk // 2, owner, chunk % 2)

        def from_mate(block, chunk):
            return cut(rmate)(kit, chunk // 2, block, chunk % 2)

        def from_cross(chunk):
            return cut(rcross)(kit, chunk // 2, chunk % 2)

        def over(chunk):
            return cut(across)(chunk // 2, chunk % 2)

        made = Scatter(at, (term, from_mate, from_cross, over), tsend, trecv, base[0])
        base[0] += 6 * parts
        return made

    steps = 2 * len(orders[0])
    bbase = [0]

    queue, held = [], []
    links = Links()
    quiet = [(start + 0.5, start + 6) for start in (30, 41, 59, 75, 93, 108, 130)]

    def begin(buf, landing, order, out, now):
        made = Reducer(
            at,
            buf,
            landing,
            out,
            orders[order],
            (bsend, brecv),
            bbase[0],
            osem.at[bbase[0] // steps],
        )
        bbase[0] += steps
        held.append(made)
        resume(now)

    def resume(now):
        for made in list(held):
            plan = links.plan(now, *made.next_load())
            over = max(plan.values())
            if any(now < end and over > start for start, end in quiet):
                continue
            links.free.update(plan)
            made.due = over + links.latency
            made.launch()
            held.remove(made)
            queue.append(made)

    def step_on(made, now):
        queue.remove(made)
        if not made.advance():
            held.append(made)
            resume(now)

    def pause(now):
        while queue:
            made = min(queue, key=lambda one: one.due)
            if made.due > now:
                break
            step_on(made, now)
        resume(now)

    big_taken = [0]

    def begin_rows(low, size, order, now):
        room = landing_rows(size, batch_count)
        where = pl.ds(low, size)
        landing = land_big.at[pl.ds(big_taken[0], room)]
        begin(sum_big.at[where], landing, order, big_out.at[where], now)
        big_taken[0] += room

    for low in (0, rows + side):
        acc[:, low : low + side, :] = jnp.zeros((acc.shape[0], side, LANES), F32)

    def norm_back(exchange, load, back, hat, gain, shift, inverse, vec_ref, give, now):
        width = back.shape[1]

        def first(index, carry):
            place = pl.ds(pl.multiple_of(index * vsize, vsize), vsize)
            normed = hat[place, :]
            before = normed * gain + shift
            grown, top = mish_parts(before)
            share = 1.0 / (top + 2.0)
            slope = top * share + before * (4.0 * grown * (1.0 + grown) * share * share)
            value = load(place) * slope
            back[place, :] = value
            return (carry[0] + fold(value), carry[1] + fold(value * normed))

        zero = jnp.zeros((8, width), F32)
        one, two = lax.fori_loop(0, rows // vsize, first, (zero, zero))
        exchange.push(
            two_rows(jnp.sum(one, axis=0, keepdims=True), jnp.sum(two, axis=0, keepdims=True))
        )
        pause(now + 2)
        exchange.take()
        pause(now + 6)
        slots = exchange.slots

        def gather_up(index, total):
            return total + slots[index]

        total = lax.fori_loop(0, batch_count, gather_up, zero)
        vec_ref[...] = total
        scale = gain * inverse
        shift_part, gain_part = total[0:1] / pixels, total[1:2] / pixels

        def second(start):
            place = pl.ds(start, vsize)
            give(start, scale * (back[place, :] - shift_part - hat[place, :] * gain_part))

        tiles(rows, vsize, second)

    across_dims = (((1,), (1,)), ((), ()))
    along_dims = (((0,), (0,)), ((), ()))

    def back_pair(left, weight, pair, chunk, part):
        def body(start):
            begin_at = start + chunk * half_rows
            terms = lax.dot_general(
                left(pl.ds(begin_at, bsize)), weight, across_dims, preferred_element_type=F32
            ).astype(BF16)
            for step in range(2):
                pbuf[part, 2 * pair + step, pl.ds(begin_at, bsize), :] = terms[
                    :, LANES * step : LANES * (step + 1)
                ]

        tiles(half_rows, bsize, body)

    def pair_rows(pair, offset=0):
        return pl.ds(pl.multiple_of(offset + pair * 256, 256), 256)

    def spread_out(go, left, weight_at, parts, now, span):
        chunks = 2 * parts
        for chunk in range(chunks):
            back_pair(left, weight_at(chunk // 2, 1 - at.pair), 1 - at.pair, chunk % 2, chunk // 2)
            go.far_copy(chunk).start()
        pause(now + 0.45 * span)
        for chunk in range(chunks):
            go.relay(chunk, vsize)
        pause(now + 0.5 * span)
        for chunk in range(chunks):
            back_pair(left, weight_at(chunk // 2, at.pair), at.pair, chunk % 2, chunk // 2)
            go.mate_copy(chunk).start()

    def two_of(ref, pair):
        return join([ref[2 * pair + step] for step in range(2)])

    have("grad")
    merge_go = scatter(0, 2)

    def keep_wide(start, value):
        dz_wide[pl.ds(start, vsize), :] = value.astype(BF16)

    norm_back(
        wide_ex[2],
        lambda place: grad[place, :].astype(F32),
        z_wide,
        hat_wide.at[2],
        gain_m[...],
        shift_m[...],
        inv_wide[2, 0:1, :],
        vec_wide.at[2],
        keep_wide,
        6,
    )
    spread_out(
        merge_go,
        lambda place: dz_wide[place, :],
        lambda part, pair: wm[pair_rows(pair, 512 * part), :],
        2,
        12,
        18,
    )
    for part in range(2):
        for pair in range(2):
            sum_merge[pl.ds(512 * part + 256 * pair, 256), :] = lax.dot_general(
                two_of(jbuf.at[part], pair), dz_wide[...], along_dims, preferred_element_type=F32
            ).astype(BF16)
    begin(sum_merge, grad.at[pl.ds(0, landing_rows(1024, batch_count))], 0, merge_out, 24)

    def top_up(chunk):
        def give(start, value):
            z_slim[pl.ds(start + chunk * half_rows, vsize), :] = value

        return give

    for chunk in range(2):
        merge_go.finish(chunk, vsize, top_up(chunk))

    def keep_slim(start, value):
        dz_slim[pl.ds(start, vsize), :] = value.astype(BF16)

    def slim_back(index, load, gain, shift, give, now):
        norm_back(
            slim_ex[index],
            load,
            z_slim,
            hat_slim.at[index],
            gain,
            shift,
            inv_slim[index, 0:1, :],
            vec_slim.at[index],
            give,
            now,
        )

    def settle_with(go, settle, now, span):
        pause(now + 0.7 * span)
        for chunk in range(2):
            go.finish(chunk, vsize, settle(chunk))
            pause(now + (0.85 + 0.15 * chunk) * span)

    def thin_back(stage, index, weight, offset, settle, now, span):
        go = scatter(stage, 1)
        spread_out(
            go,
            lambda place: dz_slim[place, :],
            lambda part, pair: weight[pair_rows(pair), :],
            1,
            now,
            span,
        )
        for pair in range(2):
            sum_big[pl.ds(offset + 256 * pair, 256), :] = lax.dot_general(
                two_of(hbuf.at[index], pair), dz_slim[...], along_dims, preferred_element_type=F32
            ).astype(BF16)
        settle_with(go, settle, now, span)
        return go

    slim_back(4, lambda place: z_slim[place, :], gain_t[...], shift_t[...], keep_slim, 30)

    def branch_new(chunk):
        def give(start, value):
            branch[pl.ds(start + chunk * half_rows, vsize), :] = value

        return give

    def branch_more(chunk):
        def give(start, value):
            branch[pl.ds(start + chunk * half_rows, vsize), :] += value

        return give

    def bypass_up(chunk):
        def give(start, value):
            bypass[pl.ds(start + chunk * half_rows, vsize), :] = value

        return give

    def finish_bypass():
        for chunk in range(2):
            merge_go.finish(2 + chunk, vsize, bypass_up(chunk))
        merge_go.drain()

    finish_bypass()
    thin_back(1, 4, wt, trans_row, branch_new, 30, 11).drain()

    def nine(start, value):
        place = pl.ds(start + side, vsize)
        value = value.astype(BF16).astype(F32)
        acc[1, place, :] = value
        acc[0, place, :] = pltpu.roll(value * flags[place, 4:5], vsize - 1, 0)
        acc[2, place, :] = pltpu.roll(value * flags[place, 5:6], 1, 0)

    def nine_rows(start):
        for row_tap in range(3):
            source = pl.ds(start + side - side * (row_tap - 1), vsize)
            for col_tap in range(3):
                tap = 3 * row_tap + col_tap
                value = acc[col_tap, source, :]
                if row_tap != 1:
                    column = 2 if row_tap == 0 else 3
                    value = value * flags[source, column : column + 1]
                spread[pl.ds(start, vsize), LANES * tap : LANES * (tap + 1)] = value.astype(BF16)

    def tap_back(stage, layer, offset, settle, begin_sums, now, span):
        index = 2 * layer + 1
        go = scatter(stage, 1)
        if stage == 2:
            mixed_copy.wait()
        tiles(rows, vsize, nine_rows)
        spread_out(
            go,
            lambda place: spread[place, :],
            lambda part, pair: w2[layer, pair_rows(pair), :],
            1,
            now,
            span,
        )
        for pair in range(2):
            left = two_of(hbuf.at[index], pair)
            for row_tap in range(3):
                three = lax.dot_general(
                    left,
                    spread[:, 3 * LANES * row_tap : 3 * LANES * (row_tap + 1)],
                    along_dims,
                    preferred_element_type=F32,
                ).astype(BF16)
                for col_tap in range(3):
                    row = offset + 512 * (3 * row_tap + col_tap) + 256 * pair
                    sum_big[pl.ds(row, 256), :] = three[
                        :, LANES * col_tap : LANES * (col_tap + 1)
                    ]
        begin_sums(now + 0.7 * span)
        settle_with(go, settle, now, span)
        go.drain()

    def late_sums(now):
        begin_rows(second_row[1], 2560, 0, now)
        begin_rows(second_row[1] + 2560, 2560, 1, now)

    def early_sums(now):
        begin_rows(0, 2560, 0, now)
        begin_rows(2560, 2560, 1, now)

    for layer in (1, 0):
        stage = 2 if layer == 1 else 4
        now = 41 if layer == 1 else 75
        slim_back(
            2 * layer + 1,
            lambda place: branch[place, :],
            gain_b[2 * layer + 1 : 2 * layer + 2, :],
            shift_b[2 * layer + 1 : 2 * layer + 2, :],
            nine,
            now,
        )
        tap_back(
            stage,
            layer,
            second_row[layer],
            top_up,
            late_sums if layer == 1 else early_sums,
            now,
            18,
        )
        now += 18
        slim_back(
            2 * layer,
            lambda place: z_slim[place, :],
            gain_b[2 * layer : 2 * layer + 1, :],
            shift_b[2 * layer : 2 * layer + 1, :],
            keep_slim,
            now,
        )
        thin_back(
            stage + 1,
            2 * layer,
            wf.at[layer],
            first_row[layer],
            branch_more,
            now,
            15,
        ).drain()

    norm_back(
        wide_ex[1],
        lambda place: join([branch[place, :], bypass[place, :]]),
        z_wide,
        hat_wide.at[1],
        join([gain_s[0:1, :], gain_s[1:2, :]]),
        join([shift_s[0:1, :], shift_s[1:2, :]]),
        inv_wide[1, 0:1, :],
        vec_wide.at[1],
        keep_wide,
        108,
    )
    split_go = scatter(6, 2)

    def split_terms(owner, chunk):
        def body(start):
            place = pl.ds(start + chunk * half_rows, bsize)
            terms = lax.dot_general(
                dz_wide[place, :],
                ws[pl.ds(pl.multiple_of(owner * 256, 256), 256), :],
                across_dims,
                preferred_element_type=F32,
            ).astype(BF16)
            for part in range(2):
                pbuf[part, owner, place, :] = terms[:, LANES * part : LANES * (part + 1)]

        tiles(half_rows, bsize, body)

    for chunk in range(2):
        split_terms(at.far, chunk)
        for part in range(2):
            split_go.far_copy(2 * part + chunk).start()
    pause(115)
    for chunk in range(2):
        split_terms(at.cross, chunk)
        for part in range(2):
            split_go.relay(2 * part + chunk, vsize)
    pause(118)
    for chunk in range(2):
        split_terms(at.mate, chunk)
        for part in range(2):
            split_go.mate_copy(2 * part + chunk).start()
    for chunk in range(2):
        split_terms(at.chan, chunk)
    for owner in range(4):
        result = lax.dot_general(
            dbuf[rows * owner : rows * (owner + 1), :], dz_wide[...], along_dims, preferred_element_type=F32
        ).astype(BF16)
        for part in range(2):
            sum_big[pl.ds(split_row + 1024 * part + 256 * owner, 256), :] = result[
                :, LANES * part : LANES * (part + 1)
            ]
    begin_rows(first_row[0], 2560, 0, 122)
    pause(122)

    def wide_up(part, chunk):
        def give(start, value):
            z_wide[
                pl.ds(start + chunk * half_rows, vsize), LANES * part : LANES * (part + 1)
            ] = value

        return give

    for chunk in range(2):
        for part in range(2):
            split_go.finish(2 * part + chunk, vsize, wide_up(part, chunk))
            pause(124 + 4 * chunk + 2 * part)
    split_go.drain()

    def keep_down(start, value):
        place = pl.ds(start + side, vsize)
        value = value.astype(BF16).astype(F32)
        moved = pltpu.roll(value * flags[place, 1:2], vsize - 1, 0)
        for half in range(2):
            lanes = slice(LANES * half, LANES * (half + 1))
            acc[half, place, :] = value[:, lanes]
            acc[2 + half, place, :] = moved[:, lanes]

    norm_back(
        wide_ex[0],
        lambda place: z_wide[place, :],
        z_wide,
        hat_wide.at[0],
        gain_d[...],
        shift_d[...],
        inv_wide[0, 0:1, :],
        vec_wide.at[0],
        keep_down,
        130,
    )

    def four_rows(start):
        place = pl.ds(start, vsize)
        here, below = pl.ds(start + side, vsize), pl.ds(start + 2 * side, vsize)
        keep = flags[below, 0:1]
        for kind in range(2):
            for half in range(2):
                lane = 256 * kind + LANES * half
                spread[place, lane : lane + LANES] = acc[2 * kind + half, here, :].astype(BF16)
                spread[place, 512 + lane : 512 + lane + LANES] = (
                    acc[2 * kind + half, below, :] * keep
                ).astype(BF16)

    tiles(rows, vsize, four_rows)

    def version(row_tap, col_tap):
        return 256 * (2 * (row_tap == 0) + (col_tap == 0))

    def phase_of(row_tap, col_tap):
        return 2 * (row_tap != 1) + (col_tap != 1)

    now = 137.0
    taken = 0
    for tap in range(9):
        row_tap, col_tap = tap // 3, tap % 3
        lane = version(row_tap, col_tap)
        phase = phase_of(row_tap, col_tap)
        for pair in range(2):
            left = join([fbuf[2 * pair + step, phase] for step in range(2)])
            sum_down[pl.ds(512 * tap + 256 * pair, 256), :] = lax.dot_general(
                left, spread[:, lane : lane + 256], along_dims, preferred_element_type=F32
            ).astype(BF16)
        now += 0.5
        if tap + 1 in tap_ends:
            low = 512 * (([0, *tap_ends])[tap_ends.index(tap + 1)])
            size = 512 * (tap + 1) - low
            piece = pl.ds(low, size)
            room = landing_rows(size, batch_count)
            turn = tap_ends.index(tap + 1) % 3 == 1
            begin(sum_down.at[piece], dbuf.at[pl.ds(taken, room)], int(turn), down_out.at[piece], now)
            taken += room
            pause(now)

    down_go = Scatter(
        at,
        (
            lambda owner, phase: hbuf.at[phase, owner],
            lambda block, phase: jbuf.at[block, phase],
            lambda phase: rcross_d.at[phase],
            lambda phase: feat.at[pl.ds(phase * rows, rows)],
        ),
        tsend,
        trecv,
        base[0],
    )
    order = (3, 2, 1, 0)

    def feature_terms(phase, pair):
        row_taps = (0, 2) if phase // 2 else (1,)
        col_taps = (0, 2) if phase % 2 else (1,)

        def body(start):
            place = pl.ds(start, bsize)
            total = None
            for row_tap in row_taps:
                for col_tap in col_taps:
                    lane = version(row_tap, col_tap)
                    one = lax.dot_general(
                        spread[place, lane : lane + 256],
                        wd[3 * row_tap + col_tap, pair_rows(pair), :],
                        across_dims,
                        preferred_element_type=F32,
                    )
                    total = one if total is None else total + one
            terms = total.astype(BF16)
            for step in range(2):
                hbuf[phase, 2 * pair + step, place, :] = terms[:, LANES * step : LANES * (step + 1)]

        tiles(rows, bsize, body)

    for phase in order:
        feature_terms(phase, 1 - at.pair)
        down_go.far_copy(phase).start()
        now += 1.5
        pause(now)
    for phase in order:
        down_go.relay(phase, vsize)
        feature_terms(phase, at.pair)
        down_go.mate_copy(phase).start()
        now += 1.7
        pause(now)

    def place_back(phase):
        row_par, col_par = phase // 2, phase % 2

        def give(start, value):
            line = start // side
            for step in range(vsize // side):
                feat_grad[2 * (line + step) + row_par, pl.ds(col_par, side, stride=2), :] = value[
                    side * step : side * (step + 1), :
                ]

        return give

    arriving = [(147 + 5.9 * turn + 8.5, phase) for turn, phase in enumerate(order)]
    while queue or held or arriving:
        resume(now)
        made = min(queue, key=lambda one: one.due) if queue else None
        if arriving and (made is None or arriving[0][0] <= made.due):
            due, phase = arriving.pop(0)
            now = max(now, due)
            down_go.finish(phase, vsize, place_back(phase))
        else:
            now = max(now, made.due)
            step_on(made, now)
    down_go.drain()
    for made in (*wide_ex, *slim_ex):
        made.drain()


def section_call(batch_count, side, flags, vectors, feat, grad_in, weights):
    rows = grad_in.shape[0]
    wide = 2 * LANES
    hbm = pl.BlockSpec(memory_space=pl.ANY)
    vmem = pl.BlockSpec(memory_space=pltpu.VMEM)
    dma = pltpu.SemaphoreType.DMA
    shape = jax.ShapeDtypeStruct
    bits = batch_count.bit_length() - 1
    near = list(range(bits))
    turned = [1, 0, *near[2:]] if bits > 1 else near
    sums = [
        shape((1024, wide), BF16),
        shape((big_rows, LANES), BF16),
        shape((4608, wide), BF16),
    ]
    slots = [
        pltpu.VMEM((3, batch_count, 8, wide), F32),
        pltpu.VMEM((5, batch_count, 8, LANES), F32),
    ]
    turns = [dma((3, batch_count)), dma((5, batch_count))]
    scratch = [
        pltpu.VMEM(feat.shape, BF16),
        pltpu.VMEM((rows, wide), BF16),
        pltpu.VMEM((9, 512, wide), BF16),
        pltpu.VMEM((1024, wide), BF16),
        pltpu.VMEM((2, 512, LANES), BF16),
        pltpu.VMEM((2, 512, 9 * LANES), BF16),
        pltpu.VMEM((512, LANES), BF16),
        pltpu.VMEM((1024, wide), BF16),
        pltpu.VMEM((4, 4, rows, LANES), BF16),
        pltpu.VMEM((4 * rows, wide), BF16),
        pltpu.VMEM((5, 4, rows, LANES), BF16),
        pltpu.VMEM((2, 4, rows, LANES), BF16),
        pltpu.VMEM((3, rows, wide), F32),
        pltpu.VMEM((5, rows, LANES), F32),
        pltpu.VMEM((3, 8, wide), F32),
        pltpu.VMEM((5, 8, LANES), F32),
        pltpu.VMEM((4, rows + 2 * side, LANES), F32),
        pltpu.VMEM((rows, wide), F32),
        pltpu.VMEM((rows, LANES), F32),
        pltpu.VMEM((rows, LANES), F32),
        pltpu.VMEM((rows, LANES), F32),
        pltpu.VMEM((rows, 9 * LANES), BF16),
        pltpu.VMEM((rows, wide), BF16),
        pltpu.VMEM((rows, LANES), BF16),
        pltpu.VMEM((2, 4, rows, LANES), BF16),
        pltpu.VMEM((2, 2, 2, rows, LANES), BF16),
        pltpu.VMEM((2, 2, rows, LANES), BF16),
        pltpu.VMEM((2, rows, LANES), BF16),
        pltpu.VMEM((4, rows, LANES), BF16),
        *[pltpu.VMEM(one.shape, one.dtype) for one in sums],
        pltpu.VMEM((landing_rows(big_rows, batch_count), LANES), BF16),
        *slots,
        *turns,
        *turns,
        dma((110,)),
        dma((110,)),
        dma((72,)),
        dma((72,)),
        dma((15 * 2 * bits,)),
        dma((15 * 2 * bits,)),
        dma((40,)),
        dma((16,)),
    ]
    return pl.pallas_call(
        functools.partial(section_kernel, batch_count, side, (near, turned)),
        out_shape=[
            shape((rows, wide), BF16),
            shape((2 * rows // side, 2 * side, LANES), F32),
            shape((3, 8, wide), F32),
            shape((5, 8, LANES), F32),
            *sums,
        ],
        in_specs=[vmem] * 11 + [hbm] * 8,
        out_specs=[hbm] + [vmem] * 3 + [hbm] * 3,
        scratch_shapes=scratch,
        compiler_params=pltpu.CompilerParams(
            collective_id=0, has_side_effects=True, vmem_limit_bytes=VMEM_LIMIT
        ),
    )(flags, *vectors, feat, grad_in, *weights)


def local(
    features,
    tile_split,
    out_grad,
    w_down,
    gain_down,
    shift_down,
    w_split,
    gain_split,
    shift_split,
    w_first,
    w_second,
    gain_block,
    shift_block,
    w_trans,
    gain_trans,
    shift_trans,
    w_merge,
    gain_merge,
    shift_merge,
):
    side = out_grad.shape[1]
    count = lax.axis_size("batch")
    flags = mask_columns(tile_split, side)

    def row(vec):
        return vec.reshape(1, -1)

    weights = (
        w_down.reshape(9, w_down.shape[2], w_down.shape[3]),
        w_split,
        w_first,
        w_second.reshape(2, 9, w_second.shape[3], w_second.shape[4]),
        w_trans,
        w_merge,
    )
    vectors = (
        row(gain_down),
        row(shift_down),
        gain_split,
        shift_split,
        gain_block.reshape(4, -1),
        shift_block.reshape(4, -1),
        row(gain_trans),
        row(shift_trans),
        row(gain_merge),
        row(shift_merge),
    )
    mixed, feat_grad, vec_wide, vec_slim, merge, big, down = section_call(
        count,
        side,
        flags,
        vectors,
        features.reshape(-1, features.shape[3]),
        out_grad.reshape(-1, out_grad.shape[3]),
        weights,
    )
    rows = w_trans.shape[0]
    two = second_row[0]
    second_grad = big[two : two + 18 * rows].reshape(w_second.shape)
    first_grad = jnp.stack([big[low : low + rows] for low in first_row])
    return (
        mixed.reshape(out_grad.shape),
        feat_grad.reshape(features.shape),
        down.reshape(w_down.shape).astype(F32),
        vec_wide[0, 1],
        vec_wide[0, 0],
        big[split_row:].reshape(w_split.shape).astype(F32),
        vec_wide[1, 1].reshape(gain_split.shape),
        vec_wide[1, 0].reshape(shift_split.shape),
        first_grad.astype(F32),
        second_grad.astype(F32),
        vec_slim[:4, 1].reshape(gain_block.shape),
        vec_slim[:4, 0].reshape(shift_block.shape),
        big[trans_row : trans_row + rows].astype(F32),
        vec_slim[4, 1],
        vec_slim[4, 0],
        merge.astype(F32),
        vec_wide[2, 1],
        vec_wide[2, 0],
    )


def solution(mesh):
    placed = (
        P("batch", None, None, "chan"),
        P("batch", None),
        P("batch", None, None, "chan"),
        P(None, None, None, "chan"),
        P("chan"),
        P("chan"),
        P(None, None, "chan"),
        P(None, "chan"),
        P(None, "chan"),
        P(None, None, "chan"),
        P(None, None, None, None, "chan"),
        P(None, None, "chan"),
        P(None, None, "chan"),
        P(None, "chan"),
        P("chan"),
        P("chan"),
        P(None, "chan"),
        P("chan"),
        P("chan"),
    )
    return jax.shard_map(
        local,
        mesh=mesh,
        in_specs=placed,
        out_specs=(
            P("batch", None, None, "chan"),
            P("batch", None, None, "chan"),
            P(None, None, None, "chan"),
            P("chan"),
            P("chan"),
            P(None, None, "chan"),
            P(None, "chan"),
            P(None, "chan"),
            P(None, None, "chan"),
            P(None, None, None, None, "chan"),
            P(None, None, "chan"),
            P(None, None, "chan"),
            P(None, "chan"),
            P("chan"),
            P("chan"),
            P(None, "chan"),
            P("chan"),
            P("chan"),
        ),
        check_vma=False,
    )
```

```python
import functools

import jax
import jax.numpy as jnp
from jax import lax
from jax.experimental import pallas as pl
from jax.experimental.pallas import tpu as pltpu
from jax.sharding import PartitionSpec as P

epsilon = 1e-05
F32 = jnp.float32
BF16 = jnp.bfloat16
MESH = pl.DeviceIdType.MESH
LANES = 128
VMEM_LIMIT = 60 * 1024 * 1024


def tap_masks(splits, side_len, stride):
    places = jnp.arange(side_len, dtype=jnp.int32)
    offset = jnp.arange(3, dtype=jnp.int32) - 1
    source = stride * places[:, None] + offset[None, :]
    inside = (source >= 0) & (source < stride * side_len)

    def along_axis(cut_at):
        cut_at = cut_at[:, None, None]
        same_tile = (source[None] < stride * cut_at) == (places[None, :, None] < cut_at)
        return (inside[None] & same_tile).astype(jnp.float32)

    return (along_axis(splits[:, 0]), along_axis(splits[:, 1]))


def mask_columns(tile_split, side_len):
    number = tile_split.shape[0]
    rows_two, cols_two = tap_masks(tile_split, side_len, 2)
    rows_one, cols_one = tap_masks(tile_split, side_len, 1)

    def by_row(flags):
        return jnp.broadcast_to(flags[:, :, None], (number, side_len, side_len)).reshape(-1)

    def by_col(flags):
        return jnp.broadcast_to(flags[:, None, :], (number, side_len, side_len)).reshape(-1)

    stacked = jnp.stack(
        [
            by_row(rows_two[:, :, 0]),
            by_col(cols_two[:, :, 0]),
            by_row(rows_one[:, :, 0]),
            by_row(rows_one[:, :, 2]),
            by_col(cols_one[:, :, 0]),
            by_col(cols_one[:, :, 2]),
        ],
        axis=1,
    )
    return jnp.pad(stacked, ((side_len, side_len), (0, 2)))


class Places:
    def __init__(self, batch_count):
        self.count = batch_count
        self.chan = lax.axis_index("chan")
        self.batch = lax.axis_index("batch")
        self.mate = self.chan + 1 - 2 * lax.rem(self.chan, 2)
        self.cross = lax.rem(self.chan + 2, 4)
        self.far = lax.rem(self.mate + 2, 4)
        self.pair = self.chan // 2

    def greet(self):
        barrier = pltpu.get_barrier_semaphore()
        for partner in (self.mate, self.cross):
            pl.semaphore_signal(
                barrier, inc=1, device_id={"chan": partner}, device_id_type=MESH
            )

        def hail(step, carry):
            peer = lax.rem(self.batch + step, self.count)
            pl.semaphore_signal(barrier, inc=1, device_id={"batch": peer}, device_id_type=MESH)
            return carry

        lax.fori_loop(1, self.count, hail, 0)
        pl.semaphore_wait(barrier, 2 + self.count - 1)


class Gather:
    def __init__(self, places, view, chunks, send, recv, base):
        self.at, self.view, self.chunks = places, view, chunks
        self.send, self.recv, self.base = send, recv, base

    def copy(self, owner, chunk, kind, partner):
        ref = self.view(owner, chunk)
        slot = self.base + 3 * chunk + kind
        return pltpu.make_async_remote_copy(
            src_ref=ref,
            dst_ref=ref,
            send_sem=self.send.at[slot],
            recv_sem=self.recv.at[slot],
            device_id={"chan": partner},
            device_id_type=MESH,
        )

    def start(self, chunk):
        self.copy(self.at.chan, chunk, 1, self.at.cross).start()
        self.copy(self.at.chan, chunk, 0, self.at.mate).start()

    def wait_mate(self, chunk):
        self.copy(self.at.mate, chunk, 0, self.at.mate).wait_recv()

    def forward(self, chunk):
        self.copy(self.at.cross, chunk, 1, self.at.cross).wait_recv()
        self.copy(self.at.cross, chunk, 2, self.at.mate).start()

    def wait_far(self, chunk):
        self.copy(self.at.far, chunk, 2, self.at.mate).wait_recv()

    def drain(self):
        for chunk in range(self.chunks):
            self.copy(self.at.chan, chunk, 0, self.at.mate).wait_send()
            self.copy(self.at.chan, chunk, 1, self.at.cross).wait_send()
            self.copy(self.at.cross, chunk, 2, self.at.mate).wait_send()


class Exchange:
    def __init__(self, places, slots, send, recv):
        self.at, self.slots, self.send, self.recv = places, slots, send, recv

    def copy(self, step, owner, peer):
        ref = self.slots.at[owner]
        return pltpu.make_async_remote_copy(
            src_ref=ref,
            dst_ref=ref,
            send_sem=self.send.at[step],
            recv_sem=self.recv.at[step],
            device_id={"batch": peer},
            device_id_type=MESH,
        )

    def push(self, block):
        at = self.at
        self.slots[at.batch] = block

        def start(step, carry):
            self.copy(step, at.batch, lax.rem(at.batch + step, at.count)).start()
            return carry

        lax.fori_loop(1, at.count, start, 0)

    def take(self):
        at = self.at

        def arrive(step, carry):
            owner = lax.rem(at.batch + at.count - step, at.count)
            self.copy(step, owner, owner).wait_recv()
            return carry

        lax.fori_loop(1, at.count, arrive, 0)

    def drain(self):
        at = self.at

        def sent(step, carry):
            self.copy(step, at.batch, lax.rem(at.batch + step, at.count)).wait_send()
            return carry

        lax.fori_loop(1, at.count, sent, 0)


def two_rows(first, second):
    return jnp.where(
        lax.broadcasted_iota(jnp.int32, (8, first.shape[1]), 0) == 0, first, second
    )


def fold(values):
    return jnp.sum(values.reshape(values.shape[0] // 8, 8, values.shape[1]), axis=0)


def tiles(total, size, body):
    def step(index, carry):
        body(pl.multiple_of(index * size, size))
        return carry

    lax.fori_loop(0, total // size, step, 0)


def mish_parts(before):
    grown = jnp.exp(jnp.minimum(before, 20.0))
    top = grown * (grown + 2.0)
    return grown, top


def join(halves):
    return jnp.concatenate(halves, axis=1)


CHUNKS = 4


class Norms:
    def __init__(self, exchange, rows, pixels):
        self.exchange, self.rows, self.pixels = exchange, rows, pixels

    def statistics(self, z_ref):
        rows, width = self.rows, z_ref.shape[1]
        size = 96

        def add_up(index, total):
            return total + fold(z_ref[pl.ds(pl.multiple_of(index * size, size), size), :])

        zero = jnp.zeros((8, width), F32)
        total = lax.fori_loop(0, rows // size, add_up, zero)
        mean = jnp.sum(total, axis=0, keepdims=True) / rows

        def spread(index, total):
            away = z_ref[pl.ds(pl.multiple_of(index * size, size), size), :] - mean
            return total + fold(away * away)

        total = lax.fori_loop(0, rows // size, spread, zero)
        square = jnp.sum(total, axis=0, keepdims=True)
        self.exchange.push(two_rows(mean, square))
        self.exchange.take()
        slots, count = self.exchange.slots, self.exchange.at.count

        def means(index, total):
            return total + slots[index]

        whole = lax.fori_loop(0, count, means, zero)[0:1] / count

        def squares(index, total):
            block = slots[index]
            away = block[0:1] - whole
            return total + block[1:2] + rows * (away * away)

        variance = lax.fori_loop(0, count, squares, jnp.zeros((1, width), F32)) / self.pixels
        return whole, lax.rsqrt(variance + epsilon)


class Scatter:
    def __init__(self, places, views, send, recv, base):
        self.at = places
        self.term, self.from_mate, self.from_cross, self.across = views
        self.send, self.recv, self.base = send, recv, base
        self.used = []

    def copy(self, source, target, chunk, kind, partner):
        slot = self.base + 3 * chunk + kind
        return pltpu.make_async_remote_copy(
            src_ref=source,
            dst_ref=target,
            send_sem=self.send.at[slot],
            recv_sem=self.recv.at[slot],
            device_id={"chan": partner},
            device_id_type=MESH,
        )

    def far_copy(self, chunk):
        return self.copy(
            self.term(self.at.far, chunk), self.from_mate(0, chunk), chunk, 0, self.at.mate
        )

    def mate_copy(self, chunk):
        return self.copy(
            self.term(self.at.mate, chunk), self.from_mate(1, chunk), chunk, 1, self.at.mate
        )

    def cross_copy(self, chunk):
        return self.copy(self.across(chunk), self.from_cross(chunk), chunk, 2, self.at.cross)

    def relay(self, chunk, size):
        self.far_copy(chunk).wait_recv()
        mine, theirs, both = (
            self.term(self.at.cross, chunk),
            self.from_mate(0, chunk),
            self.across(chunk),
        )

        def add(start):
            place = pl.ds(start, size)
            both[place, :] = (mine[place, :].astype(F32) + theirs[place, :].astype(F32)).astype(
                BF16
            )

        tiles(mine.shape[0], size, add)
        self.cross_copy(chunk).start()

    def finish(self, chunk, size, give):
        self.mate_copy(chunk).wait_recv()
        self.cross_copy(chunk).wait_recv()
        parts = (self.term(self.at.chan, chunk), self.from_mate(1, chunk), self.from_cross(chunk))

        def add(start):
            place = pl.ds(start, size)
            first, second, third = [part[place, :].astype(F32) for part in parts]
            give(start, first + second + third)

        tiles(parts[0].shape[0], size, add)
        self.used.append(chunk)

    def drain(self):
        for chunk in self.used:
            self.far_copy(chunk).wait_send()
            self.mate_copy(chunk).wait_send()
            self.cross_copy(chunk).wait_send()


def tile_of(rows):
    return max(size for size in range(8, 321, 8) if rows % size == 0)


class Links:
    rate, latency = 50000.0, 2.5

    def __init__(self):
        self.free = {}

    def plan(self, now, bit, size):
        span = size / self.rate
        loads = {2: ((1, span), (2, 2 * span))}.get(bit, ((bit, span),))
        return {link: max(now, self.free.get(link, 0.0)) + load for link, load in loads}


class Reducer:
    def __init__(self, places, buf, landing, out, order, sems, base, own_sem):
        self.at, self.buf, self.landing, self.out = places, buf, landing, out
        self.order, (self.send, self.recv), self.base = order, sems, base
        self.own_sem = own_sem
        self.low, self.size, self.taken, self.step = 0, buf.shape[0], 0, 0
        self.due = 0.0

    def next_load(self):
        steps = len(self.order)
        if self.step < steps:
            bit, size = self.order[self.step], self.size // 2
        else:
            bit, size = self.order[2 * steps - 1 - self.step], self.size
        return bit, 2 * size * self.buf.shape[1]

    def partner(self, bit):
        side = lax.rem(self.at.batch // (1 << bit), 2)
        return side, self.at.batch + (1 - 2 * side) * (1 << bit)

    def copy(self, source, target, partner):
        return pltpu.make_async_remote_copy(
            src_ref=source,
            dst_ref=target,
            send_sem=self.send.at[self.base + self.step],
            recv_sem=self.recv.at[self.base + self.step],
            device_id={"batch": partner},
            device_id_type=MESH,
        )

    def rows(self, low, size):
        return pl.ds(pl.multiple_of(low, 8), size)

    def launch(self):
        steps = len(self.order)
        if self.step < steps:
            side, partner = self.partner(self.order[self.step])
            half = self.size // 2
            gone = self.low + (1 - side) * half
            self.flying = self.copy(
                self.buf.at[self.rows(gone, half)],
                self.landing.at[pl.ds(self.taken, half)],
                partner,
            )
            self.kept = self.low + side * half
            self.flying.start()
            return
        side, partner = self.partner(self.order[2 * steps - 1 - self.step])
        target = self.out.at[self.rows(self.low, self.size)]
        source = target
        if self.step == steps:
            source = self.buf.at[self.rows(self.low, self.size)]
            self.own = pltpu.make_async_copy(source, target, self.own_sem)
            self.own.start()
        self.flying = self.copy(source, target, partner)
        self.flying.start()
        other = self.out.at[self.rows(self.low + (1 - 2 * side) * self.size, self.size)]
        self.coming = self.copy(other, other, partner)
        self.next_low = self.low - side * self.size

    def advance(self):
        steps = len(self.order)
        if self.step < steps:
            self.flying.wait()
            half = self.size // 2
            size = tile_of(half)
            taken, kept = self.taken, self.kept

            def add(start):
                place = self.rows(kept + start, size)
                self.buf[place, :] = (
                    self.buf[place, :].astype(F32)
                    + self.landing[pl.ds(taken + start, size), :].astype(F32)
                ).astype(BF16)

            tiles(half, size, add)
            self.low, self.size, self.taken = kept, half, taken + half
        else:
            self.coming.wait_recv()
            self.flying.wait_send()
            if self.step == steps:
                self.own.wait()
            self.low, self.size = self.next_low, 2 * self.size
        self.step += 1
        return self.step == 2 * steps


first_row = (10240, 0)
second_row = (512, 5120)
trans_row = 9728
split_row = 10752
tap_ends = (2, 4, 6, 8, 9)
late_parts = ((0, 1536, 0), (1536, 1536, 1), (3072, 2048, 0))
split_parts = ((0, 1536, 0), (1536, 1024, 1))
big_rows = 12800


def landing_rows(rows, batch_count):
    return rows - rows // batch_count


def section_kernel(
    batch_count,
    side,
    orders,
    flags,
    gain_d,
    shift_d,
    gain_s,
    shift_s,
    gain_b,
    shift_b,
    gain_t,
    shift_t,
    gain_m,
    shift_m,
    feat_in,
    grad_in,
    wd_in,
    ws_in,
    wf_in,
    w2_in,
    wt_in,
    wm_in,
    mixed,
    feat_grad,
    vec_wide,
    vec_slim,
    merge_out,
    big_out,
    down_out,
    feat,
    grad,
    wd,
    ws,
    wf,
    w2,
    wt,
    wm,
    fbuf,
    dbuf,
    hbuf,
    jbuf,
    hat_wide,
    hat_slim,
    inv_wide,
    inv_slim,
    acc,
    z_wide,
    z_slim,
    branch,
    bypass,
    spread,
    dz_wide,
    dz_slim,
    pbuf,
    rmate,
    rcross,
    across,
    rcross_d,
    sum_merge,
    sum_big,
    sum_down,
    land_big,
    slots_wide,
    slots_slim,
    wide_sem,
    slim_sem,
    wide_rsem,
    slim_rsem,
    send,
    recv,
    tsend,
    trecv,
    bsend,
    brecv,
    wsem,
    osem,
):
    raw = feat_grad
    at = Places(batch_count)
    me = at.chan
    rows = z_wide.shape[0]
    half_rows = rows // 2
    bsize = 192
    parts = CHUNKS
    part_rows = rows // parts
    pixels = rows * batch_count
    area = side * side

    weight_copies = {}

    def bring(name, pairs):
        copies = []
        for source, target in pairs:
            slot = sum(len(done) for done in weight_copies.values()) + len(copies)
            copies.append(pltpu.make_async_copy(source, target, wsem.at[slot]))
        weight_copies[name] = copies
        for copy in copies:
            copy.start()

    def have(name):
        for copy in weight_copies[name]:
            copy.wait()

    bring("features", [(feat_in, feat)])
    bring("down", [(wd_in.at[tap], wd.at[tap]) for tap in range(9)])
    bring("split", [(ws_in.at[part], ws.at[:, pl.ds(LANES * part, LANES)]) for part in range(2)])
    for layer in range(2):
        bring(f"first{layer}", [(wf_in.at[layer], wf.at[layer])])
        bring(
            f"second{layer}",
            [
                (w2_in.at[layer, tap], w2.at[layer, :, pl.ds(LANES * tap, LANES)])
                for tap in range(9)
            ],
        )
    bring("trans", [(wt_in, wt)])
    bring("merge", [(wm_in, wm)])
    bring("grad", [(grad_in, grad)])

    base = [0]

    def gather(view, chunks):
        made = Gather(at, view, chunks, send, recv, base[0])
        base[0] += 3 * chunks
        return made

    def by_half(ref):
        return lambda owner, chunk: ref.at[owner, pl.ds(chunk * part_rows, part_rows)]

    feat_go = gather(lambda owner, phase: fbuf.at[owner, phase], 4)
    def down_rows(owner, start, size):
        return pl.ds(pl.multiple_of(owner * rows + start, 16), size)

    down_go = gather(
        lambda owner, chunk: dbuf.at[down_rows(owner, chunk * part_rows, part_rows)], parts
    )
    half_go = [gather(by_half(hbuf.at[index]), parts) for index in range(5)]
    side_go = gather(by_half(jbuf.at[1]), parts)
    top_go = gather(by_half(jbuf.at[0]), parts)
    wide_ex = [
        Exchange(at, slots_wide.at[index], wide_sem.at[index], wide_rsem.at[index])
        for index in range(3)
    ]
    slim_ex = [
        Exchange(at, slots_slim.at[index], slim_sem.at[index], slim_rsem.at[index])
        for index in range(5)
    ]

    at.greet()

    have("features")

    for phase in range(4):
        row_par, col_par = phase // 2, phase % 2

        if col_par == 0:

            def widen(index, carry):
                line = pl.multiple_of((2 * index + row_par) * 2 * side, 16)
                raw[index] = feat[pl.ds(line, 2 * side), :].astype(F32)
                return carry

            lax.fori_loop(0, raw.shape[0] // 2, widen, 0)

        def pick(start):
            both = [
                raw[2 * (start // (2 * side)) + step, pl.ds(col_par, side, stride=2), :]
                for step in range(2)
            ]
            fbuf[me, phase, pl.ds(start, 2 * side), :] = jnp.concatenate(both, axis=0).astype(BF16)

        tiles(rows, 2 * side, pick)
        feat_go.start(phase)

    acc[...] = jnp.zeros_like(acc)
    have("down")

    def down_pair(phase, pair):
        row_par, col_par = phase // 2, phase % 2
        row_taps = (0, 2) if row_par else (1,)
        col_taps = (0, 2) if col_par else (1,)
        size = 192

        def body(start):
            block = join(
                [fbuf[2 * pair + step, phase, pl.ds(start, size), :] for step in range(2)]
            )
            for row_tap in row_taps:
                for col_tap in col_taps:
                    part = jnp.dot(
                        block,
                        wd[3 * row_tap + col_tap, pl.ds(pl.multiple_of(pair * 256, 256), 256), :],
                        preferred_element_type=F32,
                    )
                    place = pl.ds(start + (2 * side if row_tap == 0 else side), size)
                    if row_tap == 0:
                        part = part * flags[place, 0:1]
                    kind = 1 if col_tap == 0 else 0
                    for half in range(2):
                        acc[2 * kind + half, place, :] += part[:, LANES * half : LANES * (half + 1)]

        tiles(rows, size, body)

    for phase in range(4):
        feat_go.wait_mate(phase)
        down_pair(phase, at.pair)
        feat_go.forward(phase)
    for phase in range(4):
        feat_go.wait_far(phase)
        down_pair(phase, 1 - at.pair)

    vsize = 4 * side

    def settle_down(start):
        place = pl.ds(start + side, vsize)
        for half in range(2):
            z_wide[pl.ds(start, vsize), LANES * half : LANES * (half + 1)] = acc[
                half, place, :
            ] + flags[place, 1:2] * pltpu.roll(acc[2 + half, place, :], 1, 0)

    tiles(rows, vsize, settle_down)

    def activate(exchange, z_ref, hat_ref, gain, shift, inv_ref, give, begin):
        mean, inverse = Norms(exchange, rows, pixels).statistics(z_ref)
        inv_ref[...] = jnp.broadcast_to(inverse, inv_ref.shape)

        def body(start):
            place = pl.ds(start, vsize)
            normed = (z_ref[place, :] - mean) * inverse
            hat_ref[place, :] = normed
            before = normed * gain + shift
            _, top = mish_parts(before)
            give(start, before * (top / (top + 2.0)))

        for chunk in range(parts):

            def inner(start):
                body(start + chunk * part_rows)

            tiles(part_rows, vsize, inner)
            begin(chunk)

    def keep_down(start, value):
        dbuf[down_rows(me, start, vsize), :] = value.astype(BF16)

    activate(
        wide_ex[0], z_wide, hat_wide.at[0], gain_d[...], shift_d[...], inv_wide.at[0], keep_down,
        down_go.start,
    )
    have("split")

    msize = max(size for size in (288, 192) if part_rows % size == 0)

    def split_block(owner, chunk, first):
        def body(start):
            place = pl.ds(start + chunk * part_rows, msize)
            part = jnp.dot(
                dbuf[down_rows(owner, start + chunk * part_rows, msize), :],
                ws[pl.ds(pl.multiple_of(owner * 256, 256), 256), :],
                preferred_element_type=F32,
            )
            if first:
                z_wide[place, :] = part
            else:
                z_wide[place, :] += part

        tiles(part_rows, msize, body)

    for chunk in range(parts):
        split_block(me, chunk, True)
    for chunk in range(parts):
        down_go.wait_mate(chunk)
        split_block(at.mate, chunk, False)
    for chunk in range(parts):
        down_go.forward(chunk)
        split_block(at.cross, chunk, False)
    for chunk in range(parts):
        down_go.wait_far(chunk)
        split_block(at.far, chunk, False)

    def keep_split(start, value):
        place = pl.ds(start, vsize)
        branch[place, :] = value[:, :LANES]
        hbuf[0, me, place, :] = value[:, :LANES].astype(BF16)
        jbuf[1, me, place, :] = value[:, LANES:].astype(BF16)

    activate(
        wide_ex[1],
        z_wide,
        hat_wide.at[1],
        join([gain_s[0:1, :], gain_s[1:2, :]]),
        join([shift_s[0:1, :], shift_s[1:2, :]]),
        inv_wide.at[1],
        keep_split,
        half_go[0].start,
    )
    for chunk in range(parts):
        side_go.start(chunk)

    def two_of(ref, pair, place):
        return join([ref[2 * pair + step, place, :] for step in range(2)])

    def thin_pair(source, weight, pair, chunk, first):
        def body(start):
            place = pl.ds(start + chunk * part_rows, msize)
            part = jnp.dot(
                two_of(source, pair, place),
                weight[pl.ds(pl.multiple_of(pair * 256, 256), 256), :],
                preferred_element_type=F32,
            )
            if first:
                z_slim[place, :] = part
            else:
                z_slim[place, :] += part

        tiles(part_rows, msize, body)

    def thin_conv(index, weight):
        source, go = hbuf.at[index], half_go[index]
        for chunk in range(parts):
            go.wait_mate(chunk)
            thin_pair(source, weight, at.pair, chunk, True)
        for chunk in range(parts):
            go.forward(chunk)
        for chunk in range(parts):
            go.wait_far(chunk)
            thin_pair(source, weight, 1 - at.pair, chunk, False)

    def tap_pair(source, weight, pair, chunk):
        def body(start):
            begin = start + chunk * part_rows
            part = jnp.dot(
                two_of(source, pair, pl.ds(begin, msize)),
                weight[pl.ds(pl.multiple_of(pair * 256, 256), 256), :],
                preferred_element_type=F32,
            )
            for col_tap in range(3):
                for row_tap in range(3):
                    tap = 3 * row_tap + col_tap
                    piece = part[:, LANES * tap : LANES * (tap + 1)]
                    place = pl.ds(begin + side - side * (row_tap - 1), msize)
                    if row_tap != 1:
                        column = 2 if row_tap == 0 else 3
                        piece = piece * flags[place, column : column + 1]
                    acc[col_tap, place, :] += piece

        tiles(part_rows, msize, body)

    def tap_conv(index, weight):
        source, go = hbuf.at[index], half_go[index]
        acc[0:3] = jnp.zeros((3, *acc.shape[1:]), F32)
        for chunk in range(parts):
            go.wait_mate(chunk)
            tap_pair(source, weight, at.pair, chunk)
        for chunk in range(parts):
            go.forward(chunk)
        for chunk in range(parts):
            go.wait_far(chunk)
            tap_pair(source, weight, 1 - at.pair, chunk)

        def settle(start):
            place = pl.ds(start + side, vsize)
            z_slim[pl.ds(start, vsize), :] = (
                acc[1, place, :]
                + flags[place, 4:5] * pltpu.roll(acc[0, place, :], 1, 0)
                + flags[place, 5:6] * pltpu.roll(acc[2, place, :], vsize - 1, 0)
            )

        tiles(rows, vsize, settle)

    def slim_act(index, gain, shift, give, begin):
        activate(
            slim_ex[index], z_slim, hat_slim.at[index], gain, shift, inv_slim.at[index], give, begin
        )

    for layer in range(2):
        have(f"first{layer}")
        thin_conv(2 * layer, wf.at[layer])

        def keep_inner(start, value):
            place = pl.ds(start, vsize)
            hbuf[2 * layer + 1, me, place, :] = value.astype(BF16)

        slim_act(
            2 * layer,
            gain_b[2 * layer : 2 * layer + 1, :],
            shift_b[2 * layer : 2 * layer + 1, :],
            keep_inner,
            half_go[2 * layer + 1].start,
        )
        have(f"second{layer}")
        tap_conv(2 * layer + 1, w2.at[layer])

        def keep_branch(start, value):
            place = pl.ds(start, vsize)
            total = branch[place, :] + value
            branch[place, :] = total
            hbuf[2 * layer + 2, me, place, :] = total.astype(BF16)

        slim_act(
            2 * layer + 1,
            gain_b[2 * layer + 1 : 2 * layer + 2, :],
            shift_b[2 * layer + 1 : 2 * layer + 2, :],
            keep_branch,
            half_go[2 * layer + 2].start,
        )
        if layer == 0:
            for chunk in range(parts):
                side_go.forward(chunk)
    have("trans")
    thin_conv(4, wt)

    def keep_top(start, value):
        place = pl.ds(start, vsize)
        jbuf[0, me, place, :] = value.astype(BF16)

    slim_act(4, gain_t[...], shift_t[...], keep_top, top_go.start)
    have("merge")

    def merge_pair(part_index, pair, chunk, first):
        def body(start):
            place = pl.ds(start + chunk * part_rows, msize)
            part = jnp.dot(
                two_of(jbuf.at[part_index], pair, place),
                wm[pl.ds(pl.multiple_of(part_index * 512 + pair * 256, 256), 256), :],
                preferred_element_type=F32,
            )
            if first:
                z_wide[place, :] = part
            else:
                z_wide[place, :] += part

        tiles(part_rows, msize, body)

    for chunk in range(parts):
        side_go.wait_mate(chunk)
        merge_pair(1, at.pair, chunk, True)
    for chunk in range(parts):
        side_go.wait_far(chunk)
        merge_pair(1, 1 - at.pair, chunk, False)
    for chunk in range(parts):
        top_go.wait_mate(chunk)
        merge_pair(0, at.pair, chunk, False)
    for chunk in range(parts):
        top_go.forward(chunk)
    for chunk in range(parts):
        top_go.wait_far(chunk)
        merge_pair(0, 1 - at.pair, chunk, False)

    def keep_mixed(start, value):
        place = pl.ds(start, vsize)
        spread[place, 0:256] = value.astype(BF16)

    activate(
        wide_ex[2], z_wide, hat_wide.at[2], gain_m[...], shift_m[...], inv_wide.at[2], keep_mixed,
        lambda chunk: None,
    )

    for made in (feat_go, down_go, *half_go, side_go, top_go):
        made.drain()
    for made in (*wide_ex, *slim_ex):
        made.drain()
    mixed_copy = pltpu.make_async_copy(spread.at[:, pl.ds(0, 256)], mixed, osem.at[15])
    mixed_copy.start()

    wide_ex = [wide_ex[index] for index in (2, 1, 0)]

    base = [0]

    def scatter(stage, parts):
        kit = stage % 2

        def cut(ref):
            return lambda *where: ref.at[(*where[:-1], pl.ds(where[-1] * half_rows, half_rows))]

        def term(owner, chunk):
            return cut(pbuf)(chunk // 2, owner, chunk % 2)

        def from_mate(block, chunk):
            return cut(rmate)(kit, chunk // 2, block, chunk % 2)

        def from_cross(chunk):
            return cut(rcross)(kit, chunk // 2, chunk % 2)

        def over(chunk):
            return cut(across)(chunk // 2, chunk % 2)

        made = Scatter(at, (term, from_mate, from_cross, over), tsend, trecv, base[0])
        base[0] += 6 * parts
        return made

    steps = 2 * len(orders[0])
    bbase = [0]

    queue, held = [], []
    links = Links()
    quiet = [(start + 0.5, start + 6) for start in (30, 41, 59, 75, 93, 108, 130)]

    def begin(buf, landing, order, out, now):
        made = Reducer(
            at,
            buf,
            landing,
            out,
            orders[order],
            (bsend, brecv),
            bbase[0],
            osem.at[bbase[0] // steps],
        )
        bbase[0] += steps
        held.append(made)
        resume(now)

    def resume(now):
        for made in list(held):
            plan = links.plan(now, *made.next_load())
            over = max(plan.values())
            if any(now < end and over > start for start, end in quiet):
                continue
            links.free.update(plan)
            made.due = over + links.latency
            made.launch()
            held.remove(made)
            queue.append(made)

    def step_on(made, now):
        queue.remove(made)
        if not made.advance():
            held.append(made)
            resume(now)

    def pause(now):
        while queue:
            made = min(queue, key=lambda one: one.due)
            if made.due > now:
                break
            step_on(made, now)
        resume(now)

    big_taken = [0]

    def begin_rows(low, size, order, now):
        room = landing_rows(size, batch_count)
        where = pl.ds(low, size)
        landing = land_big.at[pl.ds(big_taken[0], room)]
        begin(sum_big.at[where], landing, order, big_out.at[where], now)
        big_taken[0] += room

    for low in (0, rows + side):
        acc[:, low : low + side, :] = jnp.zeros((acc.shape[0], side, LANES), F32)

    def norm_back(exchange, load, back, hat, gain, shift, inverse, vec_ref, give, now):
        width = back.shape[1]

        def first(index, carry):
            place = pl.ds(pl.multiple_of(index * vsize, vsize), vsize)
            normed = hat[place, :]
            before = normed * gain + shift
            grown, top = mish_parts(before)
            share = 1.0 / (top + 2.0)
            slope = top * share + before * (4.0 * grown * (1.0 + grown) * share * share)
            value = load(place) * slope
            back[place, :] = value
            return (carry[0] + fold(value), carry[1] + fold(value * normed))

        zero = jnp.zeros((8, width), F32)
        one, two = lax.fori_loop(0, rows // vsize, first, (zero, zero))
        exchange.push(
            two_rows(jnp.sum(one, axis=0, keepdims=True), jnp.sum(two, axis=0, keepdims=True))
        )
        pause(now + 2)
        exchange.take()
        pause(now + 6)
        slots = exchange.slots

        def gather_up(index, total):
            return total + slots[index]

        total = lax.fori_loop(0, batch_count, gather_up, zero)
        vec_ref[...] = total
        scale = gain * inverse
        shift_part, gain_part = total[0:1] / pixels, total[1:2] / pixels

        def second(start):
            place = pl.ds(start, vsize)
            give(start, scale * (back[place, :] - shift_part - hat[place, :] * gain_part))

        tiles(rows, vsize, second)

    across_dims = (((1,), (1,)), ((), ()))
    along_dims = (((0,), (0,)), ((), ()))

    def back_pair(left, weight, pair, chunk, part):
        def body(start):
            begin_at = start + chunk * half_rows
            terms = lax.dot_general(
                left(pl.ds(begin_at, bsize)), weight, across_dims, preferred_element_type=F32
            ).astype(BF16)
            for step in range(2):
                pbuf[part, 2 * pair + step, pl.ds(begin_at, bsize), :] = terms[
                    :, LANES * step : LANES * (step + 1)
                ]

        tiles(half_rows, bsize, body)

    def pair_rows(pair, offset=0):
        return pl.ds(pl.multiple_of(offset + pair * 256, 256), 256)

    def spread_out(go, left, weight_at, parts, now, span):
        chunks = 2 * parts
        for chunk in range(chunks):
            back_pair(left, weight_at(chunk // 2, 1 - at.pair), 1 - at.pair, chunk % 2, chunk // 2)
            go.far_copy(chunk).start()
        pause(now + 0.45 * span)
        for chunk in range(chunks):
            go.relay(chunk, vsize)
        pause(now + 0.5 * span)
        for chunk in range(chunks):
            back_pair(left, weight_at(chunk // 2, at.pair), at.pair, chunk % 2, chunk // 2)
            go.mate_copy(chunk).start()

    def two_of(ref, pair):
        return join([ref[2 * pair + step] for step in range(2)])

    have("grad")
    merge_go = scatter(0, 2)

    def keep_wide(start, value):
        dz_wide[pl.ds(start, vsize), :] = value.astype(BF16)

    norm_back(
        wide_ex[2],
        lambda place: grad[place, :].astype(F32),
        z_wide,
        hat_wide.at[2],
        gain_m[...],
        shift_m[...],
        inv_wide[2, 0:1, :],
        vec_wide.at[2],
        keep_wide,
        6,
    )
    spread_out(
        merge_go,
        lambda place: dz_wide[place, :],
        lambda part, pair: wm[pair_rows(pair, 512 * part), :],
        2,
        12,
        18,
    )
    for part in range(2):
        for pair in range(2):
            sum_merge[pl.ds(512 * part + 256 * pair, 256), :] = lax.dot_general(
                two_of(jbuf.at[part], pair), dz_wide[...], along_dims, preferred_element_type=F32
            ).astype(BF16)
    begin(sum_merge, grad.at[pl.ds(0, landing_rows(1024, batch_count))], 0, merge_out, 24)

    def top_up(chunk):
        def give(start, value):
            z_slim[pl.ds(start + chunk * half_rows, vsize), :] = value

        return give

    for chunk in range(2):
        merge_go.finish(chunk, vsize, top_up(chunk))

    def keep_slim(start, value):
        dz_slim[pl.ds(start, vsize), :] = value.astype(BF16)

    def slim_back(index, load, gain, shift, give, now):
        norm_back(
            slim_ex[index],
            load,
            z_slim,
            hat_slim.at[index],
            gain,
            shift,
            inv_slim[index, 0:1, :],
            vec_slim.at[index],
            give,
            now,
        )

    def settle_with(go, settle, now, span):
        pause(now + 0.7 * span)
        for chunk in range(2):
            go.finish(chunk, vsize, settle(chunk))
            pause(now + (0.85 + 0.15 * chunk) * span)

    def thin_back(stage, index, weight, offset, settle, now, span):
        go = scatter(stage, 1)
        spread_out(
            go,
            lambda place: dz_slim[place, :],
            lambda part, pair: weight[pair_rows(pair), :],
            1,
            now,
            span,
        )
        for pair in range(2):
            sum_big[pl.ds(offset + 256 * pair, 256), :] = lax.dot_general(
                two_of(hbuf.at[index], pair), dz_slim[...], along_dims, preferred_element_type=F32
            ).astype(BF16)
        settle_with(go, settle, now, span)
        return go

    slim_back(4, lambda place: z_slim[place, :], gain_t[...], shift_t[...], keep_slim, 30)

    def branch_new(chunk):
        def give(start, value):
            branch[pl.ds(start + chunk * half_rows, vsize), :] = value

        return give

    def branch_more(chunk):
        def give(start, value):
            branch[pl.ds(start + chunk * half_rows, vsize), :] += value

        return give

    def bypass_up(chunk):
        def give(start, value):
            bypass[pl.ds(start + chunk * half_rows, vsize), :] = value

        return give

    def finish_bypass():
        for chunk in range(2):
            merge_go.finish(2 + chunk, vsize, bypass_up(chunk))
        merge_go.drain()

    finish_bypass()
    thin_back(1, 4, wt, trans_row, branch_new, 30, 11).drain()

    def nine(start, value):
        place = pl.ds(start + side, vsize)
        value = value.astype(BF16).astype(F32)
        acc[1, place, :] = value
        acc[0, place, :] = pltpu.roll(value * flags[place, 4:5], vsize - 1, 0)
        acc[2, place, :] = pltpu.roll(value * flags[place, 5:6], 1, 0)

    def nine_rows(start):
        for row_tap in range(3):
            source = pl.ds(start + side - side * (row_tap - 1), vsize)
            for col_tap in range(3):
                tap = 3 * row_tap + col_tap
                value = acc[col_tap, source, :]
                if row_tap != 1:
                    column = 2 if row_tap == 0 else 3
                    value = value * flags[source, column : column + 1]
                spread[pl.ds(start, vsize), LANES * tap : LANES * (tap + 1)] = value.astype(BF16)

    def tap_back(stage, layer, offset, settle, begin_sums, now, span):
        index = 2 * layer + 1
        go = scatter(stage, 1)
        if stage == 2:
            mixed_copy.wait()
        tiles(rows, vsize, nine_rows)
        spread_out(
            go,
            lambda place: spread[place, :],
            lambda part, pair: w2[layer, pair_rows(pair), :],
            1,
            now,
            span,
        )
        for pair in range(2):
            left = two_of(hbuf.at[index], pair)
            for row_tap in range(3):
                three = lax.dot_general(
                    left,
                    spread[:, 3 * LANES * row_tap : 3 * LANES * (row_tap + 1)],
                    along_dims,
                    preferred_element_type=F32,
                ).astype(BF16)
                for col_tap in range(3):
                    row = offset + 512 * (3 * row_tap + col_tap) + 256 * pair
                    sum_big[pl.ds(row, 256), :] = three[
                        :, LANES * col_tap : LANES * (col_tap + 1)
                    ]
        begin_sums(now + 0.7 * span)
        settle_with(go, settle, now, span)
        go.drain()

    def late_sums(now):
        for low, size, order in late_parts:
            begin_rows(second_row[1] + low, size, order, now)

    def early_sums(now):
        for low, size, order in late_parts:
            begin_rows(low, size, order, now)

    for layer in (1, 0):
        stage = 2 if layer == 1 else 4
        now = 41 if layer == 1 else 75
        slim_back(
            2 * layer + 1,
            lambda place: branch[place, :],
            gain_b[2 * layer + 1 : 2 * layer + 2, :],
            shift_b[2 * layer + 1 : 2 * layer + 2, :],
            nine,
            now,
        )
        tap_back(
            stage,
            layer,
            second_row[layer],
            top_up,
            late_sums if layer == 1 else early_sums,
            now,
            18,
        )
        now += 18
        slim_back(
            2 * layer,
            lambda place: z_slim[place, :],
            gain_b[2 * layer : 2 * layer + 1, :],
            shift_b[2 * layer : 2 * layer + 1, :],
            keep_slim,
            now,
        )
        thin_back(
            stage + 1,
            2 * layer,
            wf.at[layer],
            first_row[layer],
            branch_more,
            now,
            15,
        ).drain()

    norm_back(
        wide_ex[1],
        lambda place: join([branch[place, :], bypass[place, :]]),
        z_wide,
        hat_wide.at[1],
        join([gain_s[0:1, :], gain_s[1:2, :]]),
        join([shift_s[0:1, :], shift_s[1:2, :]]),
        inv_wide[1, 0:1, :],
        vec_wide.at[1],
        keep_wide,
        108,
    )
    split_go = scatter(6, 2)

    def split_terms(owner, chunk):
        def body(start):
            place = pl.ds(start + chunk * half_rows, bsize)
            terms = lax.dot_general(
                dz_wide[place, :],
                ws[pl.ds(pl.multiple_of(owner * 256, 256), 256), :],
                across_dims,
                preferred_element_type=F32,
            ).astype(BF16)
            for part in range(2):
                pbuf[part, owner, place, :] = terms[:, LANES * part : LANES * (part + 1)]

        tiles(half_rows, bsize, body)

    for chunk in range(2):
        split_terms(at.far, chunk)
        for part in range(2):
            split_go.far_copy(2 * part + chunk).start()
    pause(115)
    for chunk in range(2):
        split_terms(at.cross, chunk)
        for part in range(2):
            split_go.relay(2 * part + chunk, vsize)
    pause(118)
    for chunk in range(2):
        split_terms(at.mate, chunk)
        for part in range(2):
            split_go.mate_copy(2 * part + chunk).start()
    for chunk in range(2):
        split_terms(at.chan, chunk)
    for owner in range(4):
        result = lax.dot_general(
            dbuf[rows * owner : rows * (owner + 1), :], dz_wide[...], along_dims, preferred_element_type=F32
        ).astype(BF16)
        for part in range(2):
            sum_big[pl.ds(split_row + 1024 * part + 256 * owner, 256), :] = result[
                :, LANES * part : LANES * (part + 1)
            ]
    for low, size, order in split_parts:
        begin_rows(first_row[0] + low, size, order, 122)
    pause(122)

    def wide_up(part, chunk):
        def give(start, value):
            z_wide[
                pl.ds(start + chunk * half_rows, vsize), LANES * part : LANES * (part + 1)
            ] = value

        return give

    for chunk in range(2):
        for part in range(2):
            split_go.finish(2 * part + chunk, vsize, wide_up(part, chunk))
            pause(124 + 4 * chunk + 2 * part)
    split_go.drain()

    def keep_down(start, value):
        place = pl.ds(start + side, vsize)
        value = value.astype(BF16).astype(F32)
        moved = pltpu.roll(value * flags[place, 1:2], vsize - 1, 0)
        for half in range(2):
            lanes = slice(LANES * half, LANES * (half + 1))
            acc[half, place, :] = value[:, lanes]
            acc[2 + half, place, :] = moved[:, lanes]

    norm_back(
        wide_ex[0],
        lambda place: z_wide[place, :],
        z_wide,
        hat_wide.at[0],
        gain_d[...],
        shift_d[...],
        inv_wide[0, 0:1, :],
        vec_wide.at[0],
        keep_down,
        130,
    )

    def four_rows(start):
        place = pl.ds(start, vsize)
        here, below = pl.ds(start + side, vsize), pl.ds(start + 2 * side, vsize)
        keep = flags[below, 0:1]
        for kind in range(2):
            for half in range(2):
                lane = 256 * kind + LANES * half
                spread[place, lane : lane + LANES] = acc[2 * kind + half, here, :].astype(BF16)
                spread[place, 512 + lane : 512 + lane + LANES] = (
                    acc[2 * kind + half, below, :] * keep
                ).astype(BF16)

    tiles(rows, vsize, four_rows)

    def version(row_tap, col_tap):
        return 256 * (2 * (row_tap == 0) + (col_tap == 0))

    def phase_of(row_tap, col_tap):
        return 2 * (row_tap != 1) + (col_tap != 1)

    now = 137.0
    taken = 0
    for tap in range(9):
        row_tap, col_tap = tap // 3, tap % 3
        lane = version(row_tap, col_tap)
        phase = phase_of(row_tap, col_tap)
        for pair in range(2):
            left = join([fbuf[2 * pair + step, phase] for step in range(2)])
            sum_down[pl.ds(512 * tap + 256 * pair, 256), :] = lax.dot_general(
                left, spread[:, lane : lane + 256], along_dims, preferred_element_type=F32
            ).astype(BF16)
        now += 0.5
        if tap + 1 in tap_ends:
            low = 512 * (([0, *tap_ends])[tap_ends.index(tap + 1)])
            size = 512 * (tap + 1) - low
            piece = pl.ds(low, size)
            room = landing_rows(size, batch_count)
            turn = tap_ends.index(tap + 1) % 3 == 1
            begin(sum_down.at[piece], dbuf.at[pl.ds(taken, room)], int(turn), down_out.at[piece], now)
            taken += room
            pause(now)

    down_go = Scatter(
        at,
        (
            lambda owner, phase: hbuf.at[phase, owner],
            lambda block, phase: jbuf.at[block, phase],
            lambda phase: rcross_d.at[phase],
            lambda phase: feat.at[pl.ds(phase * rows, rows)],
        ),
        tsend,
        trecv,
        base[0],
    )
    order = (3, 2, 1, 0)

    def feature_terms(phase, pair):
        row_taps = (0, 2) if phase // 2 else (1,)
        col_taps = (0, 2) if phase % 2 else (1,)

        def body(start):
            place = pl.ds(start, bsize)
            total = None
            for row_tap in row_taps:
                for col_tap in col_taps:
                    lane = version(row_tap, col_tap)
                    one = lax.dot_general(
                        spread[place, lane : lane + 256],
                        wd[3 * row_tap + col_tap, pair_rows(pair), :],
                        across_dims,
                        preferred_element_type=F32,
                    )
                    total = one if total is None else total + one
            terms = total.astype(BF16)
            for step in range(2):
                hbuf[phase, 2 * pair + step, place, :] = terms[:, LANES * step : LANES * (step + 1)]

        tiles(rows, bsize, body)

    for phase in order:
        feature_terms(phase, 1 - at.pair)
        down_go.far_copy(phase).start()
        now += 1.5
        pause(now)
    for phase in order:
        down_go.relay(phase, vsize)
        feature_terms(phase, at.pair)
        down_go.mate_copy(phase).start()
        now += 1.7
        pause(now)

    def place_back(phase):
        row_par, col_par = phase // 2, phase % 2

        def give(start, value):
            line = start // side
            for step in range(vsize // side):
                feat_grad[2 * (line + step) + row_par, pl.ds(col_par, side, stride=2), :] = value[
                    side * step : side * (step + 1), :
                ]

        return give

    arriving = [(147 + 5.9 * turn + 8.5, phase) for turn, phase in enumerate(order)]
    while queue or held or arriving:
        resume(now)
        made = min(queue, key=lambda one: one.due) if queue else None
        if arriving and (made is None or arriving[0][0] <= made.due):
            due, phase = arriving.pop(0)
            now = max(now, due)
            down_go.finish(phase, vsize, place_back(phase))
        else:
            now = max(now, made.due)
            step_on(made, now)
    down_go.drain()
    for made in (*wide_ex, *slim_ex):
        made.drain()


def section_call(batch_count, side, flags, vectors, feat, grad_in, weights):
    rows = grad_in.shape[0]
    wide = 2 * LANES
    hbm = pl.BlockSpec(memory_space=pl.ANY)
    vmem = pl.BlockSpec(memory_space=pltpu.VMEM)
    dma = pltpu.SemaphoreType.DMA
    shape = jax.ShapeDtypeStruct
    bits = batch_count.bit_length() - 1
    near = list(range(bits))
    turned = [1, 0, *near[2:]] if bits > 1 else near
    sums = [
        shape((1024, wide), BF16),
        shape((big_rows, LANES), BF16),
        shape((4608, wide), BF16),
    ]
    slots = [
        pltpu.VMEM((3, batch_count, 8, wide), F32),
        pltpu.VMEM((5, batch_count, 8, LANES), F32),
    ]
    turns = [dma((3, batch_count)), dma((5, batch_count))]
    scratch = [
        pltpu.VMEM(feat.shape, BF16),
        pltpu.VMEM((rows, wide), BF16),
        pltpu.VMEM((9, 512, wide), BF16),
        pltpu.VMEM((1024, wide), BF16),
        pltpu.VMEM((2, 512, LANES), BF16),
        pltpu.VMEM((2, 512, 9 * LANES), BF16),
        pltpu.VMEM((512, LANES), BF16),
        pltpu.VMEM((1024, wide), BF16),
        pltpu.VMEM((4, 4, rows, LANES), BF16),
        pltpu.VMEM((4 * rows, wide), BF16),
        pltpu.VMEM((5, 4, rows, LANES), BF16),
        pltpu.VMEM((2, 4, rows, LANES), BF16),
        pltpu.VMEM((3, rows, wide), F32),
        pltpu.VMEM((5, rows, LANES), F32),
        pltpu.VMEM((3, 8, wide), F32),
        pltpu.VMEM((5, 8, LANES), F32),
        pltpu.VMEM((4, rows + 2 * side, LANES), F32),
        pltpu.VMEM((rows, wide), F32),
        pltpu.VMEM((rows, LANES), F32),
        pltpu.VMEM((rows, LANES), F32),
        pltpu.VMEM((rows, LANES), F32),
        pltpu.VMEM((rows, 9 * LANES), BF16),
        pltpu.VMEM((rows, wide), BF16),
        pltpu.VMEM((rows, LANES), BF16),
        pltpu.VMEM((2, 4, rows, LANES), BF16),
        pltpu.VMEM((2, 2, 2, rows, LANES), BF16),
        pltpu.VMEM((2, 2, rows, LANES), BF16),
        pltpu.VMEM((2, rows, LANES), BF16),
        pltpu.VMEM((4, rows, LANES), BF16),
        *[pltpu.VMEM(one.shape, one.dtype) for one in sums],
        pltpu.VMEM((landing_rows(big_rows, batch_count), LANES), BF16),
        *slots,
        *turns,
        *turns,
        dma((110,)),
        dma((110,)),
        dma((72,)),
        dma((72,)),
        dma((15 * 2 * bits,)),
        dma((15 * 2 * bits,)),
        dma((40,)),
        dma((16,)),
    ]
    return pl.pallas_call(
        functools.partial(section_kernel, batch_count, side, (near, turned)),
        out_shape=[
            shape((rows, wide), BF16),
            shape((2 * rows // side, 2 * side, LANES), F32),
            shape((3, 8, wide), F32),
            shape((5, 8, LANES), F32),
            *sums,
        ],
        in_specs=[vmem] * 11 + [hbm] * 8,
        out_specs=[hbm] + [vmem] * 3 + [hbm] * 3,
        scratch_shapes=scratch,
        compiler_params=pltpu.CompilerParams(
            collective_id=0, has_side_effects=True, vmem_limit_bytes=VMEM_LIMIT
        ),
    )(flags, *vectors, feat, grad_in, *weights)


def local(
    features,
    tile_split,
    out_grad,
    w_down,
    gain_down,
    shift_down,
    w_split,
    gain_split,
    shift_split,
    w_first,
    w_second,
    gain_block,
    shift_block,
    w_trans,
    gain_trans,
    shift_trans,
    w_merge,
    gain_merge,
    shift_merge,
):
    side = out_grad.shape[1]
    count = lax.axis_size("batch")
    flags = mask_columns(tile_split, side)

    def row(vec):
        return vec.reshape(1, -1)

    weights = (
        w_down.reshape(9, w_down.shape[2], w_down.shape[3]),
        w_split,
        w_first,
        w_second.reshape(2, 9, w_second.shape[3], w_second.shape[4]),
        w_trans,
        w_merge,
    )
    vectors = (
        row(gain_down),
        row(shift_down),
        gain_split,
        shift_split,
        gain_block.reshape(4, -1),
        shift_block.reshape(4, -1),
        row(gain_trans),
        row(shift_trans),
        row(gain_merge),
        row(shift_merge),
    )
    mixed, feat_grad, vec_wide, vec_slim, merge, big, down = section_call(
        count,
        side,
        flags,
        vectors,
        features.reshape(-1, features.shape[3]),
        out_grad.reshape(-1, out_grad.shape[3]),
        weights,
    )
    rows = w_trans.shape[0]
    two = second_row[0]
    second_grad = big[two : two + 18 * rows].reshape(w_second.shape)
    first_grad = jnp.stack([big[low : low + rows] for low in first_row])
    return (
        mixed.reshape(out_grad.shape),
        feat_grad.reshape(features.shape),
        down.reshape(w_down.shape).astype(F32),
        vec_wide[0, 1],
        vec_wide[0, 0],
        big[split_row:].reshape(w_split.shape).astype(F32),
        vec_wide[1, 1].reshape(gain_split.shape),
        vec_wide[1, 0].reshape(shift_split.shape),
        first_grad.astype(F32),
        second_grad.astype(F32),
        vec_slim[:4, 1].reshape(gain_block.shape),
        vec_slim[:4, 0].reshape(shift_block.shape),
        big[trans_row : trans_row + rows].astype(F32),
        vec_slim[4, 1],
        vec_slim[4, 0],
        merge.astype(F32),
        vec_wide[2, 1],
        vec_wide[2, 0],
    )


def solution(mesh):
    placed = (
        P("batch", None, None, "chan"),
        P("batch", None),
        P("batch", None, None, "chan"),
        P(None, None, None, "chan"),
        P("chan"),
        P("chan"),
        P(None, None, "chan"),
        P(None, "chan"),
        P(None, "chan"),
        P(None, None, "chan"),
        P(None, None, None, None, "chan"),
        P(None, None, "chan"),
        P(None, None, "chan"),
        P(None, "chan"),
        P("chan"),
        P("chan"),
        P(None, "chan"),
        P("chan"),
        P("chan"),
    )
    return jax.shard_map(
        local,
        mesh=mesh,
        in_specs=placed,
        out_specs=(
            P("batch", None, None, "chan"),
            P("batch", None, None, "chan"),
            P(None, None, None, "chan"),
            P("chan"),
            P("chan"),
            P(None, None, "chan"),
            P(None, "chan"),
            P(None, "chan"),
            P(None, None, "chan"),
            P(None, None, None, None, "chan"),
            P(None, None, "chan"),
            P(None, None, "chan"),
            P(None, "chan"),
            P("chan"),
            P("chan"),
            P(None, "chan"),
            P("chan"),
            P("chan"),
        ),
        check_vma=False,
    )
```

```python
import functools

import jax
import jax.numpy as jnp
from jax import lax
from jax.experimental import pallas as pl
from jax.experimental.pallas import tpu as pltpu
from jax.sharding import PartitionSpec as P

epsilon = 1e-05
F32 = jnp.float32
BF16 = jnp.bfloat16
MESH = pl.DeviceIdType.MESH
LANES = 128
VMEM_LIMIT = 60 * 1024 * 1024


def tap_masks(splits, side_len, stride):
    places = jnp.arange(side_len, dtype=jnp.int32)
    offset = jnp.arange(3, dtype=jnp.int32) - 1
    source = stride * places[:, None] + offset[None, :]
    inside = (source >= 0) & (source < stride * side_len)

    def along_axis(cut_at):
        cut_at = cut_at[:, None, None]
        same_tile = (source[None] < stride * cut_at) == (places[None, :, None] < cut_at)
        return (inside[None] & same_tile).astype(jnp.float32)

    return (along_axis(splits[:, 0]), along_axis(splits[:, 1]))


def mask_columns(tile_split, side_len):
    number = tile_split.shape[0]
    rows_two, cols_two = tap_masks(tile_split, side_len, 2)
    rows_one, cols_one = tap_masks(tile_split, side_len, 1)

    def by_row(flags):
        return jnp.broadcast_to(flags[:, :, None], (number, side_len, side_len)).reshape(-1)

    def by_col(flags):
        return jnp.broadcast_to(flags[:, None, :], (number, side_len, side_len)).reshape(-1)

    stacked = jnp.stack(
        [
            by_row(rows_two[:, :, 0]),
            by_col(cols_two[:, :, 0]),
            by_row(rows_one[:, :, 0]),
            by_row(rows_one[:, :, 2]),
            by_col(cols_one[:, :, 0]),
            by_col(cols_one[:, :, 2]),
        ],
        axis=1,
    )
    return jnp.pad(stacked, ((side_len, side_len), (0, 2)))


class Places:
    def __init__(self, batch_count):
        self.count = batch_count
        self.chan = lax.axis_index("chan")
        self.batch = lax.axis_index("batch")
        self.mate = self.chan + 1 - 2 * lax.rem(self.chan, 2)
        self.cross = lax.rem(self.chan + 2, 4)
        self.far = lax.rem(self.mate + 2, 4)
        self.pair = self.chan // 2

    def greet(self):
        barrier = pltpu.get_barrier_semaphore()
        for partner in (self.mate, self.cross):
            pl.semaphore_signal(
                barrier, inc=1, device_id={"chan": partner}, device_id_type=MESH
            )

        def hail(step, carry):
            peer = lax.rem(self.batch + step, self.count)
            pl.semaphore_signal(barrier, inc=1, device_id={"batch": peer}, device_id_type=MESH)
            return carry

        lax.fori_loop(1, self.count, hail, 0)
        pl.semaphore_wait(barrier, 2 + self.count - 1)


class Gather:
    def __init__(self, places, view, chunks, send, recv, base):
        self.at, self.view, self.chunks = places, view, chunks
        self.send, self.recv, self.base = send, recv, base

    def copy(self, owner, chunk, kind, partner):
        ref = self.view(owner, chunk)
        slot = self.base + 3 * chunk + kind
        return pltpu.make_async_remote_copy(
            src_ref=ref,
            dst_ref=ref,
            send_sem=self.send.at[slot],
            recv_sem=self.recv.at[slot],
            device_id={"chan": partner},
            device_id_type=MESH,
        )

    def start(self, chunk):
        self.copy(self.at.chan, chunk, 1, self.at.cross).start()
        self.copy(self.at.chan, chunk, 0, self.at.mate).start()

    def wait_mate(self, chunk):
        self.copy(self.at.mate, chunk, 0, self.at.mate).wait_recv()

    def forward(self, chunk):
        self.copy(self.at.cross, chunk, 1, self.at.cross).wait_recv()
        self.copy(self.at.cross, chunk, 2, self.at.mate).start()

    def wait_far(self, chunk):
        self.copy(self.at.far, chunk, 2, self.at.mate).wait_recv()

    def drain(self):
        for chunk in range(self.chunks):
            self.copy(self.at.chan, chunk, 0, self.at.mate).wait_send()
            self.copy(self.at.chan, chunk, 1, self.at.cross).wait_send()
            self.copy(self.at.cross, chunk, 2, self.at.mate).wait_send()


class Exchange:
    def __init__(self, places, slots, send, recv):
        self.at, self.slots, self.send, self.recv = places, slots, send, recv

    def copy(self, step, owner, peer):
        ref = self.slots.at[owner]
        return pltpu.make_async_remote_copy(
            src_ref=ref,
            dst_ref=ref,
            send_sem=self.send.at[step],
            recv_sem=self.recv.at[step],
            device_id={"batch": peer},
            device_id_type=MESH,
        )

    def push(self, block):
        at = self.at
        self.slots[at.batch] = block

        def start(step, carry):
            self.copy(step, at.batch, lax.rem(at.batch + step, at.count)).start()
            return carry

        lax.fori_loop(1, at.count, start, 0)

    def take(self):
        at = self.at

        def arrive(step, carry):
            owner = lax.rem(at.batch + at.count - step, at.count)
            self.copy(step, owner, owner).wait_recv()
            return carry

        lax.fori_loop(1, at.count, arrive, 0)

    def drain(self):
        at = self.at

        def sent(step, carry):
            self.copy(step, at.batch, lax.rem(at.batch + step, at.count)).wait_send()
            return carry

        lax.fori_loop(1, at.count, sent, 0)


def two_rows(first, second):
    return jnp.where(
        lax.broadcasted_iota(jnp.int32, (8, first.shape[1]), 0) == 0, first, second
    )


def fold(values):
    return jnp.sum(values.reshape(values.shape[0] // 8, 8, values.shape[1]), axis=0)


def tiles(total, size, body):
    def step(index, carry):
        body(pl.multiple_of(index * size, size))
        return carry

    lax.fori_loop(0, total // size, step, 0)


def mish_parts(before):
    grown = jnp.exp(jnp.minimum(before, 20.0))
    top = grown * (grown + 2.0)
    return grown, top


def join(halves):
    return jnp.concatenate(halves, axis=1)


CHUNKS = 4


class Norms:
    def __init__(self, exchange, rows, pixels):
        self.exchange, self.rows, self.pixels = exchange, rows, pixels

    def statistics(self, z_ref):
        rows, width = self.rows, z_ref.shape[1]
        size = 96

        def add_up(index, total):
            return total + fold(z_ref[pl.ds(pl.multiple_of(index * size, size), size), :])

        zero = jnp.zeros((8, width), F32)
        total = lax.fori_loop(0, rows // size, add_up, zero)
        mean = jnp.sum(total, axis=0, keepdims=True) / rows

        def spread(index, total):
            away = z_ref[pl.ds(pl.multiple_of(index * size, size), size), :] - mean
            return total + fold(away * away)

        total = lax.fori_loop(0, rows // size, spread, zero)
        square = jnp.sum(total, axis=0, keepdims=True)
        self.exchange.push(two_rows(mean, square))
        self.exchange.take()
        slots, count = self.exchange.slots, self.exchange.at.count

        def means(index, total):
            return total + slots[index]

        whole = lax.fori_loop(0, count, means, zero)[0:1] / count

        def squares(index, total):
            block = slots[index]
            away = block[0:1] - whole
            return total + block[1:2] + rows * (away * away)

        variance = lax.fori_loop(0, count, squares, jnp.zeros((1, width), F32)) / self.pixels
        return whole, lax.rsqrt(variance + epsilon)


class Scatter:
    def __init__(self, places, views, send, recv, base):
        self.at = places
        self.term, self.from_mate, self.from_cross, self.across = views
        self.send, self.recv, self.base = send, recv, base
        self.used = []

    def copy(self, source, target, chunk, kind, partner):
        slot = self.base + 3 * chunk + kind
        return pltpu.make_async_remote_copy(
            src_ref=source,
            dst_ref=target,
            send_sem=self.send.at[slot],
            recv_sem=self.recv.at[slot],
            device_id={"chan": partner},
            device_id_type=MESH,
        )

    def far_copy(self, chunk):
        return self.copy(
            self.term(self.at.far, chunk), self.from_mate(0, chunk), chunk, 0, self.at.mate
        )

    def mate_copy(self, chunk):
        return self.copy(
            self.term(self.at.mate, chunk), self.from_mate(1, chunk), chunk, 1, self.at.mate
        )

    def cross_copy(self, chunk):
        return self.copy(self.across(chunk), self.from_cross(chunk), chunk, 2, self.at.cross)

    def relay(self, chunk, size):
        self.far_copy(chunk).wait_recv()
        mine, theirs, both = (
            self.term(self.at.cross, chunk),
            self.from_mate(0, chunk),
            self.across(chunk),
        )

        def add(start):
            place = pl.ds(start, size)
            both[place, :] = (mine[place, :].astype(F32) + theirs[place, :].astype(F32)).astype(
                BF16
            )

        tiles(mine.shape[0], size, add)
        self.cross_copy(chunk).start()

    def finish(self, chunk, size, give):
        self.mate_copy(chunk).wait_recv()
        self.cross_copy(chunk).wait_recv()
        parts = (self.term(self.at.chan, chunk), self.from_mate(1, chunk), self.from_cross(chunk))

        def add(start):
            place = pl.ds(start, size)
            first, second, third = [part[place, :].astype(F32) for part in parts]
            give(start, first + second + third)

        tiles(parts[0].shape[0], size, add)
        self.used.append(chunk)

    def drain(self):
        for chunk in self.used:
            self.far_copy(chunk).wait_send()
            self.mate_copy(chunk).wait_send()
            self.cross_copy(chunk).wait_send()


def tile_of(rows):
    return max(size for size in range(8, 321, 8) if rows % size == 0)


class Links:
    rate, latency = 50000.0, 2.5

    def __init__(self):
        self.free = {}

    def plan(self, now, bit, size):
        span = size / self.rate
        loads = {2: ((1, span), (2, 2 * span))}.get(bit, ((bit, span),))
        return {link: max(now, self.free.get(link, 0.0)) + load for link, load in loads}


class Reducer:
    def __init__(self, places, buf, landing, out, order, sems, base, own_sem):
        self.at, self.buf, self.landing, self.out = places, buf, landing, out
        self.order, (self.send, self.recv), self.base = order, sems, base
        self.own_sem = own_sem
        self.low, self.size, self.taken, self.step = 0, buf.shape[0], 0, 0
        self.due = 0.0

    def next_load(self):
        steps = len(self.order)
        if self.step < steps:
            bit, size = self.order[self.step], self.size // 2
        else:
            bit, size = self.order[2 * steps - 1 - self.step], self.size
        return bit, 2 * size * self.buf.shape[1]

    def partner(self, bit):
        side = lax.rem(self.at.batch // (1 << bit), 2)
        return side, self.at.batch + (1 - 2 * side) * (1 << bit)

    def copy(self, source, target, partner):
        return pltpu.make_async_remote_copy(
            src_ref=source,
            dst_ref=target,
            send_sem=self.send.at[self.base + self.step],
            recv_sem=self.recv.at[self.base + self.step],
            device_id={"batch": partner},
            device_id_type=MESH,
        )

    def rows(self, low, size):
        return pl.ds(pl.multiple_of(low, 8), size)

    def launch(self):
        steps = len(self.order)
        if self.step < steps:
            side, partner = self.partner(self.order[self.step])
            half = self.size // 2
            gone = self.low + (1 - side) * half
            self.flying = self.copy(
                self.buf.at[self.rows(gone, half)],
                self.landing.at[pl.ds(self.taken, half)],
                partner,
            )
            self.kept = self.low + side * half
            self.flying.start()
            return
        side, partner = self.partner(self.order[2 * steps - 1 - self.step])
        target = self.out.at[self.rows(self.low, self.size)]
        source = target
        if self.step == steps:
            source = self.buf.at[self.rows(self.low, self.size)]
            self.own = pltpu.make_async_copy(source, target, self.own_sem)
            self.own.start()
        self.flying = self.copy(source, target, partner)
        self.flying.start()
        other = self.out.at[self.rows(self.low + (1 - 2 * side) * self.size, self.size)]
        self.coming = self.copy(other, other, partner)
        self.next_low = self.low - side * self.size

    def advance(self):
        steps = len(self.order)
        if self.step < steps:
            self.flying.wait()
            half = self.size // 2
            size = tile_of(half)
            taken, kept = self.taken, self.kept

            def add(start):
                place = self.rows(kept + start, size)
                self.buf[place, :] = (
                    self.buf[place, :].astype(F32)
                    + self.landing[pl.ds(taken + start, size), :].astype(F32)
                ).astype(BF16)

            tiles(half, size, add)
            self.low, self.size, self.taken = kept, half, taken + half
        else:
            self.coming.wait_recv()
            self.flying.wait_send()
            if self.step == steps:
                self.own.wait()
            self.low, self.size = self.next_low, 2 * self.size
        self.step += 1
        return self.step == 2 * steps


first_row = (10240, 0)
second_row = (512, 5120)
trans_row = 9728
split_row = 10752
tap_ends = (2, 4, 6, 8, 9)
late_parts = ((0, 1536, 0), (1536, 1536, 1), (3072, 2048, 0))
split_parts = ((0, 1536, 0), (1536, 1024, 1))
big_rows = 12800


def landing_rows(rows, batch_count):
    return rows - rows // batch_count


def section_kernel(
    batch_count,
    side,
    orders,
    flags,
    gain_d,
    shift_d,
    gain_s,
    shift_s,
    gain_b,
    shift_b,
    gain_t,
    shift_t,
    gain_m,
    shift_m,
    feat_in,
    grad_in,
    wd_in,
    ws_in,
    wf_in,
    w2_in,
    wt_in,
    wm_in,
    mixed,
    feat_grad,
    vec_wide,
    vec_slim,
    merge_out,
    big_out,
    down_out,
    feat,
    grad,
    wd,
    ws,
    wf,
    w2,
    wt,
    wm,
    fbuf,
    dbuf,
    hbuf,
    jbuf,
    hat_wide,
    hat_slim,
    inv_wide,
    inv_slim,
    acc,
    z_wide,
    z_slim,
    branch,
    bypass,
    spread,
    dz_wide,
    dz_slim,
    pbuf,
    rmate,
    rcross,
    across,
    rcross_d,
    sum_merge,
    sum_big,
    sum_down,
    land_big,
    slots_wide,
    slots_slim,
    wide_sem,
    slim_sem,
    wide_rsem,
    slim_rsem,
    send,
    recv,
    tsend,
    trecv,
    bsend,
    brecv,
    wsem,
    osem,
):
    raw = feat_grad
    at = Places(batch_count)
    me = at.chan
    rows = z_wide.shape[0]
    half_rows = rows // 2
    parts = CHUNKS
    part_rows = rows // parts
    pixels = rows * batch_count
    area = side * side

    weight_copies = {}

    def bring(name, pairs):
        copies = []
        for source, target in pairs:
            slot = sum(len(done) for done in weight_copies.values()) + len(copies)
            copies.append(pltpu.make_async_copy(source, target, wsem.at[slot]))
        weight_copies[name] = copies
        for copy in copies:
            copy.start()

    def have(name):
        for copy in weight_copies[name]:
            copy.wait()

    bring("features", [(feat_in, feat)])
    bring("down", [(wd_in.at[tap], wd.at[tap]) for tap in range(9)])
    bring("split", [(ws_in.at[part], ws.at[:, pl.ds(LANES * part, LANES)]) for part in range(2)])
    for layer in range(2):
        bring(f"first{layer}", [(wf_in.at[layer], wf.at[layer])])
        bring(
            f"second{layer}",
            [
                (w2_in.at[layer, tap], w2.at[layer, :, pl.ds(LANES * tap, LANES)])
                for tap in range(9)
            ],
        )
    bring("trans", [(wt_in, wt)])
    bring("merge", [(wm_in, wm)])
    bring("grad", [(grad_in, grad)])

    base = [0]

    def gather(view, chunks):
        made = Gather(at, view, chunks, send, recv, base[0])
        base[0] += 3 * chunks
        return made

    def by_half(ref):
        return lambda owner, chunk: ref.at[owner, pl.ds(chunk * part_rows, part_rows)]

    feat_go = gather(lambda owner, phase: fbuf.at[owner, phase], 4)
    def down_rows(owner, start, size):
        return pl.ds(pl.multiple_of(owner * rows + start, 16), size)

    down_go = gather(
        lambda owner, chunk: dbuf.at[down_rows(owner, chunk * part_rows, part_rows)], parts
    )
    half_go = [gather(by_half(hbuf.at[index]), parts) for index in range(5)]
    side_go = gather(by_half(jbuf.at[1]), parts)
    top_go = gather(by_half(jbuf.at[0]), parts)
    wide_ex = [
        Exchange(at, slots_wide.at[index], wide_sem.at[index], wide_rsem.at[index])
        for index in range(3)
    ]
    slim_ex = [
        Exchange(at, slots_slim.at[index], slim_sem.at[index], slim_rsem.at[index])
        for index in range(5)
    ]

    at.greet()

    have("features")

    for phase in range(4):
        row_par, col_par = phase // 2, phase % 2

        if col_par == 0:

            def widen(index, carry):
                line = pl.multiple_of((2 * index + row_par) * 2 * side, 16)
                raw[index] = feat[pl.ds(line, 2 * side), :].astype(F32)
                return carry

            lax.fori_loop(0, raw.shape[0] // 2, widen, 0)

        def pick(start):
            both = [
                raw[2 * (start // (2 * side)) + step, pl.ds(col_par, side, stride=2), :]
                for step in range(2)
            ]
            fbuf[me, phase, pl.ds(start, 2 * side), :] = jnp.concatenate(both, axis=0).astype(BF16)

        tiles(rows, 2 * side, pick)
        feat_go.start(phase)

    acc[...] = jnp.zeros_like(acc)
    have("down")

    def down_pair(phase, pair):
        row_par, col_par = phase // 2, phase % 2
        row_taps = (0, 2) if row_par else (1,)
        col_taps = (0, 2) if col_par else (1,)
        size = 192

        def body(start):
            block = join(
                [fbuf[2 * pair + step, phase, pl.ds(start, size), :] for step in range(2)]
            )
            for row_tap in row_taps:
                for col_tap in col_taps:
                    part = jnp.dot(
                        block,
                        wd[3 * row_tap + col_tap, pl.ds(pl.multiple_of(pair * 256, 256), 256), :],
                        preferred_element_type=F32,
                    )
                    place = pl.ds(start + (2 * side if row_tap == 0 else side), size)
                    if row_tap == 0:
                        part = part * flags[place, 0:1]
                    kind = 1 if col_tap == 0 else 0
                    for half in range(2):
                        acc[2 * kind + half, place, :] += part[:, LANES * half : LANES * (half + 1)]

        tiles(rows, size, body)

    for phase in range(4):
        feat_go.wait_mate(phase)
        down_pair(phase, at.pair)
        feat_go.forward(phase)
    for phase in range(4):
        feat_go.wait_far(phase)
        down_pair(phase, 1 - at.pair)

    vsize = 4 * side

    def settle_down(start):
        place = pl.ds(start + side, vsize)
        for half in range(2):
            z_wide[pl.ds(start, vsize), LANES * half : LANES * (half + 1)] = acc[
                half, place, :
            ] + flags[place, 1:2] * pltpu.roll(acc[2 + half, place, :], 1, 0)

    tiles(rows, vsize, settle_down)

    def activate(exchange, z_ref, hat_ref, gain, shift, inv_ref, give, begin):
        mean, inverse = Norms(exchange, rows, pixels).statistics(z_ref)
        inv_ref[...] = jnp.broadcast_to(inverse, inv_ref.shape)

        def body(start):
            place = pl.ds(start, vsize)
            normed = (z_ref[place, :] - mean) * inverse
            hat_ref[place, :] = normed
            before = normed * gain + shift
            _, top = mish_parts(before)
            give(start, before * (top / (top + 2.0)))

        for chunk in range(parts):

            def inner(start):
                body(start + chunk * part_rows)

            tiles(part_rows, vsize, inner)
            begin(chunk)

    def keep_down(start, value):
        dbuf[down_rows(me, start, vsize), :] = value.astype(BF16)

    activate(
        wide_ex[0], z_wide, hat_wide.at[0], gain_d[...], shift_d[...], inv_wide.at[0], keep_down,
        down_go.start,
    )
    have("split")

    msize = max(size for size in (288, 192) if part_rows % size == 0)

    def split_block(owner, chunk, first):
        def body(start):
            place = pl.ds(start + chunk * part_rows, msize)
            part = jnp.dot(
                dbuf[down_rows(owner, start + chunk * part_rows, msize), :],
                ws[pl.ds(pl.multiple_of(owner * 256, 256), 256), :],
                preferred_element_type=F32,
            )
            if first:
                z_wide[place, :] = part
            else:
                z_wide[place, :] += part

        tiles(part_rows, msize, body)

    for chunk in range(parts):
        split_block(me, chunk, True)
    for chunk in range(parts):
        down_go.wait_mate(chunk)
        split_block(at.mate, chunk, False)
    for chunk in range(parts):
        down_go.forward(chunk)
        split_block(at.cross, chunk, False)
    for chunk in range(parts):
        down_go.wait_far(chunk)
        split_block(at.far, chunk, False)

    def keep_split(start, value):
        place = pl.ds(start, vsize)
        branch[place, :] = value[:, :LANES]
        hbuf[0, me, place, :] = value[:, :LANES].astype(BF16)
        jbuf[1, me, place, :] = value[:, LANES:].astype(BF16)

    activate(
        wide_ex[1],
        z_wide,
        hat_wide.at[1],
        join([gain_s[0:1, :], gain_s[1:2, :]]),
        join([shift_s[0:1, :], shift_s[1:2, :]]),
        inv_wide.at[1],
        keep_split,
        half_go[0].start,
    )
    for chunk in range(parts):
        side_go.start(chunk)

    def two_of(ref, pair, place):
        return join([ref[2 * pair + step, place, :] for step in range(2)])

    def thin_pair(source, weight, pair, chunk, first):
        def body(start):
            place = pl.ds(start + chunk * part_rows, msize)
            part = jnp.dot(
                two_of(source, pair, place),
                weight[pl.ds(pl.multiple_of(pair * 256, 256), 256), :],
                preferred_element_type=F32,
            )
            if first:
                z_slim[place, :] = part
            else:
                z_slim[place, :] += part

        tiles(part_rows, msize, body)

    def thin_conv(index, weight):
        source, go = hbuf.at[index], half_go[index]
        for chunk in range(parts):
            go.wait_mate(chunk)
            thin_pair(source, weight, at.pair, chunk, True)
        for chunk in range(parts):
            go.forward(chunk)
        for chunk in range(parts):
            go.wait_far(chunk)
            thin_pair(source, weight, 1 - at.pair, chunk, False)

    def tap_pair(source, weight, pair, chunk):
        def body(start):
            begin = start + chunk * part_rows
            part = jnp.dot(
                two_of(source, pair, pl.ds(begin, msize)),
                weight[pl.ds(pl.multiple_of(pair * 256, 256), 256), :],
                preferred_element_type=F32,
            )
            for col_tap in range(3):
                for row_tap in range(3):
                    tap = 3 * row_tap + col_tap
                    piece = part[:, LANES * tap : LANES * (tap + 1)]
                    place = pl.ds(begin + side - side * (row_tap - 1), msize)
                    if row_tap != 1:
                        column = 2 if row_tap == 0 else 3
                        piece = piece * flags[place, column : column + 1]
                    acc[col_tap, place, :] += piece

        tiles(part_rows, msize, body)

    def tap_conv(index, weight):
        source, go = hbuf.at[index], half_go[index]
        acc[0:3] = jnp.zeros((3, *acc.shape[1:]), F32)
        for chunk in range(parts):
            go.wait_mate(chunk)
            tap_pair(source, weight, at.pair, chunk)
        for chunk in range(parts):
            go.forward(chunk)
        for chunk in range(parts):
            go.wait_far(chunk)
            tap_pair(source, weight, 1 - at.pair, chunk)

        def settle(start):
            place = pl.ds(start + side, vsize)
            z_slim[pl.ds(start, vsize), :] = (
                acc[1, place, :]
                + flags[place, 4:5] * pltpu.roll(acc[0, place, :], 1, 0)
                + flags[place, 5:6] * pltpu.roll(acc[2, place, :], vsize - 1, 0)
            )

        tiles(rows, vsize, settle)

    def slim_act(index, gain, shift, give, begin):
        activate(
            slim_ex[index], z_slim, hat_slim.at[index], gain, shift, inv_slim.at[index], give, begin
        )

    for layer in range(2):
        have(f"first{layer}")
        thin_conv(2 * layer, wf.at[layer])

        def keep_inner(start, value):
            place = pl.ds(start, vsize)
            hbuf[2 * layer + 1, me, place, :] = value.astype(BF16)

        slim_act(
            2 * layer,
            gain_b[2 * layer : 2 * layer + 1, :],
            shift_b[2 * layer : 2 * layer + 1, :],
            keep_inner,
            half_go[2 * layer + 1].start,
        )
        have(f"second{layer}")
        tap_conv(2 * layer + 1, w2.at[layer])

        def keep_branch(start, value):
            place = pl.ds(start, vsize)
            total = branch[place, :] + value
            branch[place, :] = total
            hbuf[2 * layer + 2, me, place, :] = total.astype(BF16)

        slim_act(
            2 * layer + 1,
            gain_b[2 * layer + 1 : 2 * layer + 2, :],
            shift_b[2 * layer + 1 : 2 * layer + 2, :],
            keep_branch,
            half_go[2 * layer + 2].start,
        )
        if layer == 0:
            for chunk in range(parts):
                side_go.forward(chunk)
    have("trans")
    thin_conv(4, wt)

    def keep_top(start, value):
        place = pl.ds(start, vsize)
        jbuf[0, me, place, :] = value.astype(BF16)

    slim_act(4, gain_t[...], shift_t[...], keep_top, top_go.start)
    have("merge")

    def merge_pair(part_index, pair, chunk, first):
        def body(start):
            place = pl.ds(start + chunk * part_rows, msize)
            part = jnp.dot(
                two_of(jbuf.at[part_index], pair, place),
                wm[pl.ds(pl.multiple_of(part_index * 512 + pair * 256, 256), 256), :],
                preferred_element_type=F32,
            )
            if first:
                z_wide[place, :] = part
            else:
                z_wide[place, :] += part

        tiles(part_rows, msize, body)

    for chunk in range(parts):
        side_go.wait_mate(chunk)
        merge_pair(1, at.pair, chunk, True)
    for chunk in range(parts):
        side_go.wait_far(chunk)
        merge_pair(1, 1 - at.pair, chunk, False)
    for chunk in range(parts):
        top_go.wait_mate(chunk)
        merge_pair(0, at.pair, chunk, False)
    for chunk in range(parts):
        top_go.forward(chunk)
    for chunk in range(parts):
        top_go.wait_far(chunk)
        merge_pair(0, 1 - at.pair, chunk, False)

    def keep_mixed(start, value):
        place = pl.ds(start, vsize)
        spread[place, 0:256] = value.astype(BF16)

    activate(
        wide_ex[2], z_wide, hat_wide.at[2], gain_m[...], shift_m[...], inv_wide.at[2], keep_mixed,
        lambda chunk: None,
    )

    for made in (feat_go, down_go, *half_go, side_go, top_go):
        made.drain()
    for made in (*wide_ex, *slim_ex):
        made.drain()
    mixed_copy = pltpu.make_async_copy(spread.at[:, pl.ds(0, 256)], mixed, osem.at[15])
    mixed_copy.start()

    wide_ex = [wide_ex[index] for index in (2, 1, 0)]

    base = [0]

    def scatter(stage, count):
        kit = stage % 2

        def cut(ref):
            return lambda *where: ref.at[(*where[:-1], pl.ds(where[-1] * part_rows, part_rows))]

        def term(owner, chunk):
            return cut(pbuf)(chunk // parts, owner, chunk % parts)

        def from_mate(block, chunk):
            return cut(rmate)(kit, chunk // parts, block, chunk % parts)

        def from_cross(chunk):
            return cut(rcross)(kit, chunk // parts, chunk % parts)

        def over(chunk):
            return cut(across)(chunk // parts, chunk % parts)

        made = Scatter(at, (term, from_mate, from_cross, over), tsend, trecv, base[0])
        base[0] += 3 * parts * count
        return made

    steps = 2 * len(orders[0])
    bbase = [0]

    queue, held = [], []
    links = Links()
    quiet = [(start + 0.5, start + 6) for start in (30, 41, 59, 75, 93, 108, 130)]

    def begin(buf, landing, order, out, now):
        made = Reducer(
            at,
            buf,
            landing,
            out,
            orders[order],
            (bsend, brecv),
            bbase[0],
            osem.at[bbase[0] // steps],
        )
        bbase[0] += steps
        held.append(made)
        resume(now)

    def resume(now):
        for made in list(held):
            plan = links.plan(now, *made.next_load())
            over = max(plan.values())
            if any(now < end and over > start for start, end in quiet):
                continue
            links.free.update(plan)
            made.due = over + links.latency
            made.launch()
            held.remove(made)
            queue.append(made)

    def step_on(made, now):
        queue.remove(made)
        if not made.advance():
            held.append(made)
            resume(now)

    def pause(now):
        while queue:
            made = min(queue, key=lambda one: one.due)
            if made.due > now:
                break
            step_on(made, now)
        resume(now)

    big_taken = [0]

    def begin_rows(low, size, order, now):
        room = landing_rows(size, batch_count)
        where = pl.ds(low, size)
        landing = land_big.at[pl.ds(big_taken[0], room)]
        begin(sum_big.at[where], landing, order, big_out.at[where], now)
        big_taken[0] += room

    for low in (0, rows + side):
        acc[:, low : low + side, :] = jnp.zeros((acc.shape[0], side, LANES), F32)

    def norm_back(exchange, load, back, hat, gain, shift, inverse, vec_ref, give, now):
        width = back.shape[1]

        def first(index, carry):
            place = pl.ds(pl.multiple_of(index * vsize, vsize), vsize)
            normed = hat[place, :]
            before = normed * gain + shift
            grown, top = mish_parts(before)
            share = 1.0 / (top + 2.0)
            slope = top * share + before * (4.0 * grown * (1.0 + grown) * share * share)
            value = load(place) * slope
            back[place, :] = value
            return (carry[0] + fold(value), carry[1] + fold(value * normed))

        zero = jnp.zeros((8, width), F32)
        one, two = lax.fori_loop(0, rows // vsize, first, (zero, zero))
        exchange.push(
            two_rows(jnp.sum(one, axis=0, keepdims=True), jnp.sum(two, axis=0, keepdims=True))
        )
        pause(now + 2)
        exchange.take()
        pause(now + 6)
        slots = exchange.slots

        def gather_up(index, total):
            return total + slots[index]

        total = lax.fori_loop(0, batch_count, gather_up, zero)
        vec_ref[...] = total
        scale = gain * inverse
        shift_part, gain_part = total[0:1] / pixels, total[1:2] / pixels

        def second(start):
            place = pl.ds(start, vsize)
            give(start, scale * (back[place, :] - shift_part - hat[place, :] * gain_part))

        tiles(rows, vsize, second)

    across_dims = (((1,), (1,)), ((), ()))
    along_dims = (((0,), (0,)), ((), ()))

    def back_pair(left, weight, pair, chunk, part):
        def body(start):
            begin_at = start + chunk * part_rows
            terms = lax.dot_general(
                left(pl.ds(begin_at, msize)), weight, across_dims, preferred_element_type=F32
            ).astype(BF16)
            for step in range(2):
                pbuf[part, 2 * pair + step, pl.ds(begin_at, msize), :] = terms[
                    :, LANES * step : LANES * (step + 1)
                ]

        tiles(part_rows, msize, body)

    def pair_rows(pair, offset=0):
        return pl.ds(pl.multiple_of(offset + pair * 256, 256), 256)

    def spread_out(go, left, weight_at, count, now, span):
        chunks = parts * count
        for chunk in range(chunks):
            back_pair(left, weight_at(chunk // parts, 1 - at.pair), 1 - at.pair, chunk % parts, chunk // parts)
            go.far_copy(chunk).start()
        pause(now + 0.45 * span)
        for chunk in range(chunks):
            go.relay(chunk, vsize)
        pause(now + 0.5 * span)
        for chunk in range(chunks):
            back_pair(left, weight_at(chunk // parts, at.pair), at.pair, chunk % parts, chunk // parts)
            go.mate_copy(chunk).start()

    def two_of(ref, pair):
        return join([ref[2 * pair + step] for step in range(2)])

    have("grad")
    merge_go = scatter(0, 2)

    def keep_wide(start, value):
        dz_wide[pl.ds(start, vsize), :] = value.astype(BF16)

    norm_back(
        wide_ex[2],
        lambda place: grad[place, :].astype(F32),
        z_wide,
        hat_wide.at[2],
        gain_m[...],
        shift_m[...],
        inv_wide[2, 0:1, :],
        vec_wide.at[2],
        keep_wide,
        6,
    )
    spread_out(
        merge_go,
        lambda place: dz_wide[place, :],
        lambda part, pair: wm[pair_rows(pair, 512 * part), :],
        2,
        12,
        18,
    )
    for part in range(2):
        for pair in range(2):
            sum_merge[pl.ds(512 * part + 256 * pair, 256), :] = lax.dot_general(
                two_of(jbuf.at[part], pair), dz_wide[...], along_dims, preferred_element_type=F32
            ).astype(BF16)
    begin(sum_merge, grad.at[pl.ds(0, landing_rows(1024, batch_count))], 0, merge_out, 24)

    def top_up(chunk):
        def give(start, value):
            z_slim[pl.ds(start + chunk * part_rows, vsize), :] = value

        return give

    for chunk in range(parts):
        merge_go.finish(chunk, vsize, top_up(chunk))

    def keep_slim(start, value):
        dz_slim[pl.ds(start, vsize), :] = value.astype(BF16)

    def slim_back(index, load, gain, shift, give, now):
        norm_back(
            slim_ex[index],
            load,
            z_slim,
            hat_slim.at[index],
            gain,
            shift,
            inv_slim[index, 0:1, :],
            vec_slim.at[index],
            give,
            now,
        )

    def settle_with(go, settle, now, span):
        pause(now + 0.7 * span)
        for chunk in range(parts):
            go.finish(chunk, vsize, settle(chunk))
            pause(now + (0.8 + 0.2 * chunk / (parts - 1)) * span)

    def thin_back(stage, index, weight, offset, settle, now, span):
        go = scatter(stage, 1)
        spread_out(
            go,
            lambda place: dz_slim[place, :],
            lambda part, pair: weight[pair_rows(pair), :],
            1,
            now,
            span,
        )
        for pair in range(2):
            sum_big[pl.ds(offset + 256 * pair, 256), :] = lax.dot_general(
                two_of(hbuf.at[index], pair), dz_slim[...], along_dims, preferred_element_type=F32
            ).astype(BF16)
        settle_with(go, settle, now, span)
        return go

    slim_back(4, lambda place: z_slim[place, :], gain_t[...], shift_t[...], keep_slim, 30)

    def branch_new(chunk):
        def give(start, value):
            branch[pl.ds(start + chunk * part_rows, vsize), :] = value

        return give

    def branch_more(chunk):
        def give(start, value):
            branch[pl.ds(start + chunk * part_rows, vsize), :] += value

        return give

    def bypass_up(chunk):
        def give(start, value):
            bypass[pl.ds(start + chunk * part_rows, vsize), :] = value

        return give

    def finish_bypass():
        for chunk in range(parts):
            merge_go.finish(parts + chunk, vsize, bypass_up(chunk))
        merge_go.drain()

    finish_bypass()
    thin_back(1, 4, wt, trans_row, branch_new, 30, 11).drain()

    def nine(start, value):
        place = pl.ds(start + side, vsize)
        value = value.astype(BF16).astype(F32)
        acc[1, place, :] = value
        acc[0, place, :] = pltpu.roll(value * flags[place, 4:5], vsize - 1, 0)
        acc[2, place, :] = pltpu.roll(value * flags[place, 5:6], 1, 0)

    def nine_rows(start):
        for row_tap in range(3):
            source = pl.ds(start + side - side * (row_tap - 1), vsize)
            for col_tap in range(3):
                tap = 3 * row_tap + col_tap
                value = acc[col_tap, source, :]
                if row_tap != 1:
                    column = 2 if row_tap == 0 else 3
                    value = value * flags[source, column : column + 1]
                spread[pl.ds(start, vsize), LANES * tap : LANES * (tap + 1)] = value.astype(BF16)

    def tap_back(stage, layer, offset, settle, begin_sums, now, span):
        index = 2 * layer + 1
        go = scatter(stage, 1)
        if stage == 2:
            mixed_copy.wait()
        tiles(rows, vsize, nine_rows)
        spread_out(
            go,
            lambda place: spread[place, :],
            lambda part, pair: w2[layer, pair_rows(pair), :],
            1,
            now,
            span,
        )
        for pair in range(2):
            left = two_of(hbuf.at[index], pair)
            for row_tap in range(3):
                three = lax.dot_general(
                    left,
                    spread[:, 3 * LANES * row_tap : 3 * LANES * (row_tap + 1)],
                    along_dims,
                    preferred_element_type=F32,
                ).astype(BF16)
                for col_tap in range(3):
                    row = offset + 512 * (3 * row_tap + col_tap) + 256 * pair
                    sum_big[pl.ds(row, 256), :] = three[
                        :, LANES * col_tap : LANES * (col_tap + 1)
                    ]
        begin_sums(now + 0.7 * span)
        settle_with(go, settle, now, span)
        go.drain()

    def late_sums(now):
        for low, size, order in late_parts:
            begin_rows(second_row[1] + low, size, order, now)

    def early_sums(now):
        for low, size, order in late_parts:
            begin_rows(low, size, order, now)

    for layer in (1, 0):
        stage = 2 if layer == 1 else 4
        now = 41 if layer == 1 else 75
        slim_back(
            2 * layer + 1,
            lambda place: branch[place, :],
            gain_b[2 * layer + 1 : 2 * layer + 2, :],
            shift_b[2 * layer + 1 : 2 * layer + 2, :],
            nine,
            now,
        )
        tap_back(
            stage,
            layer,
            second_row[layer],
            top_up,
            late_sums if layer == 1 else early_sums,
            now,
            18,
        )
        now += 18
        slim_back(
            2 * layer,
            lambda place: z_slim[place, :],
            gain_b[2 * layer : 2 * layer + 1, :],
            shift_b[2 * layer : 2 * layer + 1, :],
            keep_slim,
            now,
        )
        thin_back(
            stage + 1,
            2 * layer,
            wf.at[layer],
            first_row[layer],
            branch_more,
            now,
            15,
        ).drain()

    norm_back(
        wide_ex[1],
        lambda place: join([branch[place, :], bypass[place, :]]),
        z_wide,
        hat_wide.at[1],
        join([gain_s[0:1, :], gain_s[1:2, :]]),
        join([shift_s[0:1, :], shift_s[1:2, :]]),
        inv_wide[1, 0:1, :],
        vec_wide.at[1],
        keep_wide,
        108,
    )
    split_go = scatter(6, 2)

    def split_terms(owner, chunk):
        def body(start):
            place = pl.ds(start + chunk * part_rows, msize)
            terms = lax.dot_general(
                dz_wide[place, :],
                ws[pl.ds(pl.multiple_of(owner * 256, 256), 256), :],
                across_dims,
                preferred_element_type=F32,
            ).astype(BF16)
            for part in range(2):
                pbuf[part, owner, place, :] = terms[:, LANES * part : LANES * (part + 1)]

        tiles(part_rows, msize, body)

    for chunk in range(parts):
        split_terms(at.far, chunk)
        for part in range(2):
            split_go.far_copy(parts * part + chunk).start()
    pause(115)
    for chunk in range(parts):
        split_terms(at.cross, chunk)
        for part in range(2):
            split_go.relay(parts * part + chunk, vsize)
    pause(118)
    for chunk in range(parts):
        split_terms(at.mate, chunk)
        for part in range(2):
            split_go.mate_copy(parts * part + chunk).start()
    for chunk in range(parts):
        split_terms(at.chan, chunk)
    for owner in range(4):
        result = lax.dot_general(
            dbuf[rows * owner : rows * (owner + 1), :], dz_wide[...], along_dims, preferred_element_type=F32
        ).astype(BF16)
        for part in range(2):
            sum_big[pl.ds(split_row + 1024 * part + 256 * owner, 256), :] = result[
                :, LANES * part : LANES * (part + 1)
            ]
    for low, size, order in split_parts:
        begin_rows(first_row[0] + low, size, order, 122)
    pause(122)

    def wide_up(part, chunk):
        def give(start, value):
            z_wide[
                pl.ds(start + chunk * part_rows, vsize), LANES * part : LANES * (part + 1)
            ] = value

        return give

    for chunk in range(parts):
        for part in range(2):
            split_go.finish(parts * part + chunk, vsize, wide_up(part, chunk))
            pause(124 + 6 * (2 * chunk + part) / (2 * parts - 1))
    split_go.drain()

    def keep_down(start, value):
        place = pl.ds(start + side, vsize)
        value = value.astype(BF16).astype(F32)
        moved = pltpu.roll(value * flags[place, 1:2], vsize - 1, 0)
        for half in range(2):
            lanes = slice(LANES * half, LANES * (half + 1))
            acc[half, place, :] = value[:, lanes]
            acc[2 + half, place, :] = moved[:, lanes]

    norm_back(
        wide_ex[0],
        lambda place: z_wide[place, :],
        z_wide,
        hat_wide.at[0],
        gain_d[...],
        shift_d[...],
        inv_wide[0, 0:1, :],
        vec_wide.at[0],
        keep_down,
        130,
    )

    def four_rows(start):
        place = pl.ds(start, vsize)
        here, below = pl.ds(start + side, vsize), pl.ds(start + 2 * side, vsize)
        keep = flags[below, 0:1]
        for kind in range(2):
            for half in range(2):
                lane = 256 * kind + LANES * half
                spread[place, lane : lane + LANES] = acc[2 * kind + half, here, :].astype(BF16)
                spread[place, 512 + lane : 512 + lane + LANES] = (
                    acc[2 * kind + half, below, :] * keep
                ).astype(BF16)

    tiles(rows, vsize, four_rows)

    def version(row_tap, col_tap):
        return 256 * (2 * (row_tap == 0) + (col_tap == 0))

    def phase_of(row_tap, col_tap):
        return 2 * (row_tap != 1) + (col_tap != 1)

    now = 137.0
    taken = 0
    for tap in range(9):
        row_tap, col_tap = tap // 3, tap % 3
        lane = version(row_tap, col_tap)
        phase = phase_of(row_tap, col_tap)
        for pair in range(2):
            left = join([fbuf[2 * pair + step, phase] for step in range(2)])
            sum_down[pl.ds(512 * tap + 256 * pair, 256), :] = lax.dot_general(
                left, spread[:, lane : lane + 256], along_dims, preferred_element_type=F32
            ).astype(BF16)
        now += 0.5
        if tap + 1 in tap_ends:
            low = 512 * (([0, *tap_ends])[tap_ends.index(tap + 1)])
            size = 512 * (tap + 1) - low
            piece = pl.ds(low, size)
            room = landing_rows(size, batch_count)
            turn = tap_ends.index(tap + 1) % 3 == 1
            begin(sum_down.at[piece], dbuf.at[pl.ds(taken, room)], int(turn), down_out.at[piece], now)
            taken += room
            pause(now)

    down_go = Scatter(
        at,
        (
            lambda owner, phase: hbuf.at[phase, owner],
            lambda block, phase: jbuf.at[block, phase],
            lambda phase: rcross_d.at[phase],
            lambda phase: feat.at[pl.ds(phase * rows, rows)],
        ),
        tsend,
        trecv,
        base[0],
    )
    order = (3, 2, 1, 0)

    def feature_terms(phase, pair):
        row_taps = (0, 2) if phase // 2 else (1,)
        col_taps = (0, 2) if phase % 2 else (1,)

        def body(start):
            place = pl.ds(start, msize)
            total = None
            for row_tap in row_taps:
                for col_tap in col_taps:
                    lane = version(row_tap, col_tap)
                    one = lax.dot_general(
                        spread[place, lane : lane + 256],
                        wd[3 * row_tap + col_tap, pair_rows(pair), :],
                        across_dims,
                        preferred_element_type=F32,
                    )
                    total = one if total is None else total + one
            terms = total.astype(BF16)
            for step in range(2):
                hbuf[phase, 2 * pair + step, place, :] = terms[:, LANES * step : LANES * (step + 1)]

        tiles(rows, msize, body)

    for phase in order:
        feature_terms(phase, 1 - at.pair)
        down_go.far_copy(phase).start()
        now += 1.5
        pause(now)
    for phase in order:
        down_go.relay(phase, vsize)
        feature_terms(phase, at.pair)
        down_go.mate_copy(phase).start()
        now += 1.7
        pause(now)

    def place_back(phase):
        row_par, col_par = phase // 2, phase % 2

        def give(start, value):
            line = start // side
            for step in range(vsize // side):
                feat_grad[2 * (line + step) + row_par, pl.ds(col_par, side, stride=2), :] = value[
                    side * step : side * (step + 1), :
                ]

        return give

    arriving = [(147 + 5.9 * turn + 8.5, phase) for turn, phase in enumerate(order)]
    while queue or held or arriving:
        resume(now)
        made = min(queue, key=lambda one: one.due) if queue else None
        if arriving and (made is None or arriving[0][0] <= made.due):
            due, phase = arriving.pop(0)
            now = max(now, due)
            down_go.finish(phase, vsize, place_back(phase))
        else:
            now = max(now, made.due)
            step_on(made, now)
    down_go.drain()
    for made in (*wide_ex, *slim_ex):
        made.drain()


def section_call(batch_count, side, flags, vectors, feat, grad_in, weights):
    rows = grad_in.shape[0]
    wide = 2 * LANES
    hbm = pl.BlockSpec(memory_space=pl.ANY)
    vmem = pl.BlockSpec(memory_space=pltpu.VMEM)
    dma = pltpu.SemaphoreType.DMA
    shape = jax.ShapeDtypeStruct
    bits = batch_count.bit_length() - 1
    near = list(range(bits))
    turned = [1, 0, *near[2:]] if bits > 1 else near
    sums = [
        shape((1024, wide), BF16),
        shape((big_rows, LANES), BF16),
        shape((4608, wide), BF16),
    ]
    slots = [
        pltpu.VMEM((3, batch_count, 8, wide), F32),
        pltpu.VMEM((5, batch_count, 8, LANES), F32),
    ]
    turns = [dma((3, batch_count)), dma((5, batch_count))]
    scratch = [
        pltpu.VMEM(feat.shape, BF16),
        pltpu.VMEM((rows, wide), BF16),
        pltpu.VMEM((9, 512, wide), BF16),
        pltpu.VMEM((1024, wide), BF16),
        pltpu.VMEM((2, 512, LANES), BF16),
        pltpu.VMEM((2, 512, 9 * LANES), BF16),
        pltpu.VMEM((512, LANES), BF16),
        pltpu.VMEM((1024, wide), BF16),
        pltpu.VMEM((4, 4, rows, LANES), BF16),
        pltpu.VMEM((4 * rows, wide), BF16),
        pltpu.VMEM((5, 4, rows, LANES), BF16),
        pltpu.VMEM((2, 4, rows, LANES), BF16),
        pltpu.VMEM((3, rows, wide), F32),
        pltpu.VMEM((5, rows, LANES), F32),
        pltpu.VMEM((3, 8, wide), F32),
        pltpu.VMEM((5, 8, LANES), F32),
        pltpu.VMEM((4, rows + 2 * side, LANES), F32),
        pltpu.VMEM((rows, wide), F32),
        pltpu.VMEM((rows, LANES), F32),
        pltpu.VMEM((rows, LANES), F32),
        pltpu.VMEM((rows, LANES), F32),
        pltpu.VMEM((rows, 9 * LANES), BF16),
        pltpu.VMEM((rows, wide), BF16),
        pltpu.VMEM((rows, LANES), BF16),
        pltpu.VMEM((2, 4, rows, LANES), BF16),
        pltpu.VMEM((2, 2, 2, rows, LANES), BF16),
        pltpu.VMEM((2, 2, rows, LANES), BF16),
        pltpu.VMEM((2, rows, LANES), BF16),
        pltpu.VMEM((4, rows, LANES), BF16),
        *[pltpu.VMEM(one.shape, one.dtype) for one in sums],
        pltpu.VMEM((landing_rows(big_rows, batch_count), LANES), BF16),
        *slots,
        *turns,
        *turns,
        dma((110,)),
        dma((110,)),
        dma((130,)),
        dma((130,)),
        dma((15 * 2 * bits,)),
        dma((15 * 2 * bits,)),
        dma((40,)),
        dma((16,)),
    ]
    return pl.pallas_call(
        functools.partial(section_kernel, batch_count, side, (near, turned)),
        out_shape=[
            shape((rows, wide), BF16),
            shape((2 * rows // side, 2 * side, LANES), F32),
            shape((3, 8, wide), F32),
            shape((5, 8, LANES), F32),
            *sums,
        ],
        in_specs=[vmem] * 11 + [hbm] * 8,
        out_specs=[hbm] + [vmem] * 3 + [hbm] * 3,
        scratch_shapes=scratch,
        compiler_params=pltpu.CompilerParams(
            collective_id=0, has_side_effects=True, vmem_limit_bytes=VMEM_LIMIT
        ),
    )(flags, *vectors, feat, grad_in, *weights)


def local(
    features,
    tile_split,
    out_grad,
    w_down,
    gain_down,
    shift_down,
    w_split,
    gain_split,
    shift_split,
    w_first,
    w_second,
    gain_block,
    shift_block,
    w_trans,
    gain_trans,
    shift_trans,
    w_merge,
    gain_merge,
    shift_merge,
):
    side = out_grad.shape[1]
    count = lax.axis_size("batch")
    flags = mask_columns(tile_split, side)

    def row(vec):
        return vec.reshape(1, -1)

    weights = (
        w_down.reshape(9, w_down.shape[2], w_down.shape[3]),
        w_split,
        w_first,
        w_second.reshape(2, 9, w_second.shape[3], w_second.shape[4]),
        w_trans,
        w_merge,
    )
    vectors = (
        row(gain_down),
        row(shift_down),
        gain_split,
        shift_split,
        gain_block.reshape(4, -1),
        shift_block.reshape(4, -1),
        row(gain_trans),
        row(shift_trans),
        row(gain_merge),
        row(shift_merge),
    )
    mixed, feat_grad, vec_wide, vec_slim, merge, big, down = section_call(
        count,
        side,
        flags,
        vectors,
        features.reshape(-1, features.shape[3]),
        out_grad.reshape(-1, out_grad.shape[3]),
        weights,
    )
    rows = w_trans.shape[0]
    two = second_row[0]
    second_grad = big[two : two + 18 * rows].reshape(w_second.shape)
    first_grad = jnp.stack([big[low : low + rows] for low in first_row])
    return (
        mixed.reshape(out_grad.shape),
        feat_grad.reshape(features.shape),
        down.reshape(w_down.shape).astype(F32),
        vec_wide[0, 1],
        vec_wide[0, 0],
        big[split_row:].reshape(w_split.shape).astype(F32),
        vec_wide[1, 1].reshape(gain_split.shape),
        vec_wide[1, 0].reshape(shift_split.shape),
        first_grad.astype(F32),
        second_grad.astype(F32),
        vec_slim[:4, 1].reshape(gain_block.shape),
        vec_slim[:4, 0].reshape(shift_block.shape),
        big[trans_row : trans_row + rows].astype(F32),
        vec_slim[4, 1],
        vec_slim[4, 0],
        merge.astype(F32),
        vec_wide[2, 1],
        vec_wide[2, 0],
    )


def solution(mesh):
    placed = (
        P("batch", None, None, "chan"),
        P("batch", None),
        P("batch", None, None, "chan"),
        P(None, None, None, "chan"),
        P("chan"),
        P("chan"),
        P(None, None, "chan"),
        P(None, "chan"),
        P(None, "chan"),
        P(None, None, "chan"),
        P(None, None, None, None, "chan"),
        P(None, None, "chan"),
        P(None, None, "chan"),
        P(None, "chan"),
        P("chan"),
        P("chan"),
        P(None, "chan"),
        P("chan"),
        P("chan"),
    )
    return jax.shard_map(
        local,
        mesh=mesh,
        in_specs=placed,
        out_specs=(
            P("batch", None, None, "chan"),
            P("batch", None, None, "chan"),
            P(None, None, None, "chan"),
            P("chan"),
            P("chan"),
            P(None, None, "chan"),
            P(None, "chan"),
            P(None, "chan"),
            P(None, None, "chan"),
            P(None, None, None, None, "chan"),
            P(None, None, "chan"),
            P(None, None, "chan"),
            P(None, "chan"),
            P("chan"),
            P("chan"),
            P(None, "chan"),
            P("chan"),
            P("chan"),
        ),
        check_vma=False,
    )
```
